32 devices in a mesh: dp: 8 (over y, x, core), mp: 4 (over z).
Axes of the slice: x: 2, y: 2, z: 4, core: 2. Of those that a mesh axis runs over, the one named last changes fastest.
Arguments:
- tokens: bfloat16 [24576, 768], P(('dp', 'mp')), may hold values from -6 to 6
- grad_out: bfloat16 [24576, 768], P(('dp', 'mp')), may hold values from -6 to 6
- pass_len: int32 [24, 4], P('dp'), may hold values from 100 to 200, as said below
- labels: int32 [96], P('dp'), may hold values from 0 to 95, each once
- w_query: bfloat16 [768, 768], P(None, 'mp'), may hold values from -0.21875 to 0.21875
- w_key: bfloat16 [768, 768], P(None, 'mp'), may hold values from -0.21875 to 0.21875
- w_value: bfloat16 [768, 768], P(None, 'mp'), may hold values from -0.21875 to 0.21875
- b_query: float32 [768], P('mp'), may hold values from -1 to 1
- b_value: float32 [768], P('mp'), may hold values from -1 to 1
- w_out: bfloat16 [768, 768], P('mp'), may hold values from -1.5 to 1.5
- b_out: float32 [768], replicated, may hold values from -1 to 1
- ln1_gain: float32 [768], replicated, may hold values from 0.5 to 1.5
- ln1_shift: float32 [768], replicated, may hold values from -1 to 1
- w_in: bfloat16 [768, 3072], P(None, 'mp'), may hold values from -0.21875 to 0.21875
- b_in: float32 [3072], P('mp'), may hold values from -1 to 1
- w_back: bfloat16 [3072, 768], P('mp'), may hold values from -0.15625 to 0.15625
- b_back: float32 [768], replicated, may hold values from -1 to 1
- ln2_gain: float32 [768], replicated, may hold values from 0.5 to 1.5
- ln2_shift: float32 [768], replicated, may hold values from -1 to 1
Outputs:
- mixed: bfloat16 [24576, 768], P(('dp', 'mp'))
- query_losses: float32 [96], P('dp')
- d_tokens: float32 [24576, 768], P(('dp', 'mp'))
- d_w_query: float32 [768, 768], P(None, 'mp')
- d_w_key: float32 [768, 768], P(None, 'mp')
- d_w_value: float32 [768, 768], P(None, 'mp')
- d_b_query: float32 [768], P('mp')
- d_b_value: float32 [768], P('mp')
- d_w_out: float32 [768, 768], P('mp')
- d_b_out: float32 [768], P('mp')
- d_ln1_gain: float32 [768], P('mp')
- d_ln1_shift: float32 [768], P('mp')
- d_w_in: float32 [768, 3072], P(None, 'mp')
- d_b_in: float32 [3072], P('mp')
- d_w_back: float32 [3072, 768], P('mp')
- d_b_back: float32 [768], P('mp')
- d_ln2_gain: float32 [768], P('mp')
- d_ln2_shift: float32 [768], P('mp')
The draws below stay inside these ranges and needn't reach their ends.
Inputs may be any that keep to these rules, and one draw needn't show every extreme that they name: `pass_len`: each passage length lies in the stated range; the passages of a row follow its 4 queries of 32 tokens and the rest of the row is padding; row 0 holds a passage of exactly 200 tokens.
All inputs are finite; a program needn't handle non-finite values.
Results may differ from the reference program's by a relative error of at most 0.015.
The reference program's roundings to bfloat16 on the way count: a program that leaves them out, or rounds other values in their place, can miss the bound.
Values may be sent and summed in bfloat16 or wider, within the bound.
No kernel may reach another device: no remote copies, remote signals or barrier semaphores. Data moves between devices by JAX's collectives and lax.ppermute only.
A program may use at most 128 MiB of HBM per device.

```python
import math
import jax
import jax.numpy as jnp
from jax import lax

D = 768
HEADS = 12
HEAD = 64
FF = 3072
ROW_LEN = 1024
PAIRS = 4
QLEN = 32
PMAX = 200
ROWS_TOTAL = 24
TOKENS = 24576
PAIRS_ALL = 96


def draw_pass_len(key, part):
    key = jax.random.fold_in(key, 7)
    first_key, second_key = jax.random.split(key)
    lengths = jax.random.randint(first_key, (ROWS_TOTAL, PAIRS), PMAX // 2, PMAX + 1)
    longest = jax.random.randint(second_key, (), 0, PAIRS)
    return lengths.at[0, longest].set(PMAX).astype(jnp.int32)


def block_levels(stream_key, dims, cuts, low, top_value):
    level, own = 1.0, jax.random.fold_in(stream_key, 6)
    for dim, blocks in cuts:
        draws = jnp.exp(jax.random.uniform(jax.random.fold_in(own, dim), (blocks,), jnp.float32, low / len(cuts), top_value / len(cuts)))
        level = level * jnp.repeat(draws, dims[dim] // blocks).reshape([-1 if axis == dim else 1 for axis in range(len(dims))])
    return level


def scatter_about(rng, shape, width, most, pieces=(), kind=jnp.bfloat16):
    drawn = width * jax.random.normal(rng, shape, jnp.float32)
    if pieces:
        drawn = drawn * block_levels(rng, shape, pieces, -0.22, 0.18)
    return jnp.clip(drawn, -most, most).astype(kind)


def setup_inputs(seed: int = 0) -> dict:
    splits = jax.random.split(jax.random.key(seed), 20)
    tokens = scatter_about(splits[0], (TOKENS, D), 1.0, 6.0, ((0, 32),))
    grad_out = scatter_about(splits[1], (TOKENS, D), 1.0, 6.0, ((0, 32),))
    pass_len = draw_pass_len(jax.random.fold_in(splits[19], 71), 0)
    labels = jax.random.permutation(splits[3], PAIRS_ALL).astype(jnp.int32)
    w_query = scatter_about(splits[4], (D, D), D ** -0.5, 0.21875, ((1, 4),))
    w_key = scatter_about(splits[5], (D, D), D ** -0.5, 0.21875, ((1, 4),))
    w_value = scatter_about(splits[6], (D, D), D ** -0.5, 0.21875, ((1, 4),))
    b_query = scatter_about(splits[7], (D,), 0.2, 1.0, ((0, 4),), jnp.float32)
    b_value = scatter_about(splits[8], (D,), 0.2, 1.0, ((0, 4),), jnp.float32)
    w_out = scatter_about(splits[9], (D, D), (max(D // 48, 8)) ** -0.5, 1.5, ((0, 4),))
    b_out = scatter_about(splits[10], (D,), 0.2, 1.0, (), jnp.float32)
    ln1_gain = jnp.clip(1.0 + 0.1 * jax.random.normal(splits[11], (D,), jnp.float32), 0.5, 1.5)
    ln1_shift = scatter_about(splits[12], (D,), 0.2, 1.0, (), jnp.float32)
    w_in = scatter_about(splits[13], (D, FF), D ** -0.5, 0.21875, ((1, 4),))
    b_in = scatter_about(splits[14], (FF,), 0.2, 1.0, ((0, 4),), jnp.float32)
    w_back = scatter_about(splits[15], (FF, D), (FF // 2) ** -0.5, 0.15625, ((0, 4),))
    b_back = scatter_about(splits[16], (D,), 0.2, 1.0, (), jnp.float32)
    ln2_gain = jnp.clip(1.0 + 0.1 * jax.random.normal(splits[17], (D,), jnp.float32), 0.5, 1.5)
    ln2_shift = scatter_about(splits[18], (D,), 0.2, 1.0, (), jnp.float32)
    return dict(tokens=tokens, grad_out=grad_out, pass_len=pass_len, labels=labels, w_query=w_query, w_key=w_key, w_value=w_value, b_query=b_query, b_value=b_value, w_out=w_out, b_out=b_out, ln1_gain=ln1_gain, ln1_shift=ln1_shift, w_in=w_in, b_in=b_in, w_back=w_back, b_back=b_back, ln2_gain=ln2_gain, ln2_shift=ln2_shift)


epsilon = 1e-12
masked_score = -1e+30
highest = lax.Precision.HIGHEST

@jax.custom_vjp
def low(v):
    return lax.optimization_barrier(v.astype(jnp.bfloat16)).astype(jnp.float32)

@jax.custom_vjp
def low_back(v):
    return v

def low_keep(v):
    return (low(v), None)

def low_pass(kept, grad):
    return (grad,)

def back_keep(v):
    return (v, None)

def back_low(kept, grad):
    return (low(grad),)
low.defvjp(low_keep, low_pass)
low_back.defvjp(back_keep, back_low)

def layer_norm(values, gain, shift):
    center = values - lax.optimization_barrier(jnp.mean(values, axis=-1, keepdims=True))
    spread = lax.optimization_barrier(jnp.mean(center * center, axis=-1, keepdims=True))
    return center * lax.rsqrt(spread + epsilon) * gain + shift

def row_segments(pass_len):
    query_span = PAIRS * QLEN
    passage_ends = (query_span + jnp.cumsum(pass_len, axis=1)).astype(jnp.int32)
    places = jnp.arange(ROW_LEN, dtype=jnp.int32)
    passed = lax.optimization_barrier(jnp.sum((places[None, :, None] >= passage_ends[:, None, :]).astype(jnp.int32), axis=2)).astype(jnp.int32)
    return jnp.where(places[None, :] < query_span, places[None, :] // QLEN, PAIRS + passed).astype(jnp.int32)

def cls_places(pass_len):
    passage_ends = (PAIRS * QLEN + jnp.cumsum(pass_len, axis=1)).astype(jnp.int32)
    query_starts = jnp.arange(PAIRS, dtype=jnp.int32) * QLEN
    query_starts = jnp.broadcast_to(query_starts[None, :], pass_len.shape)
    return jnp.concatenate([query_starts, passage_ends - pass_len], axis=1).astype(jnp.int32)

def attend(parts):
    query_row, key_row, value_row, segment_row = parts
    scores = low_back(jnp.einsum('qhd,khd->hqk', query_row, key_row, precision=highest))
    same = segment_row[:, None] == segment_row[None, :]
    scores = jnp.where(same[None, :, :], scores, masked_score)
    top = lax.optimization_barrier(jnp.max(scores, axis=-1, keepdims=True))
    raised = jnp.exp(scores - top)
    weights = raised / lax.optimization_barrier(jnp.sum(raised, axis=-1, keepdims=True))
    return jnp.einsum('hqk,khd->qhd', low(weights), value_row, precision=highest)

def reference(tokens, grad_out, pass_len, labels, w_query, w_key, w_value, b_query, b_value, w_out, b_out, ln1_gain, ln1_shift, w_in, b_in, w_back, b_back, ln2_gain, ln2_shift):
    segment = row_segments(pass_len)
    places = cls_places(pass_len) + (jnp.arange(ROWS_TOTAL, dtype=jnp.int32) * ROW_LEN)[:, None]
    places = places.reshape(-1).astype(jnp.int32)
    scale = 1.0 / math.sqrt(HEAD)
    temper = 2.0 / math.sqrt(D)
    targets = labels[:, None] == jnp.arange(PAIRS_ALL, dtype=jnp.int32)[None, :]
    shape_four = (ROWS_TOTAL, ROW_LEN, HEADS, HEAD)

    def forward(inputs, params):
        wq_full, wk_full, wv_full, bq_full, bv_full, wo_full, bo_full, gain_one, shift_one, wi_full, bi_full, wb_full, bb_full, gain_two, shift_two = params
        queries = low(low_back((jnp.dot(inputs, wq_full, precision=highest) + bq_full) * scale))
        keys = low(low_back(jnp.dot(inputs, wk_full, precision=highest)))
        values = low(low_back(jnp.dot(inputs, wv_full, precision=highest) + bv_full))
        context = lax.map(jax.checkpoint(attend), (queries.reshape(shape_four), keys.reshape(shape_four), values.reshape(shape_four), segment))
        context = low(low_back(context.reshape(TOKENS, D)))
        first_sum = inputs + low_back(jnp.dot(context, wo_full, precision=highest)) + bo_full
        hidden = layer_norm(first_sum, gain_one, shift_one)
        before = low_back(jnp.dot(low(hidden), wi_full, precision=highest) + bi_full)
        active = low(jax.nn.gelu(before, approximate=False))
        second_sum = hidden + low_back(jnp.dot(active, wb_full, precision=highest)) + bb_full
        mixed = layer_norm(second_sum, gain_two, shift_two)
        vectors = low(mixed[places]).reshape(ROWS_TOTAL, 2 * PAIRS, D)
        query_cls = vectors[:, :PAIRS].reshape(PAIRS_ALL, D)
        passage_cls = vectors[:, PAIRS:].reshape(PAIRS_ALL, D)
        logits = jnp.dot(query_cls, passage_cls.T, precision=highest) * temper
        top = lax.optimization_barrier(jnp.max(logits, axis=1, keepdims=True))
        log_total = top[:, 0] + jnp.log(lax.optimization_barrier(jnp.sum(jnp.exp(logits - top), axis=1)))
        chosen = lax.optimization_barrier(jnp.sum(jnp.where(targets, logits, 0.0), axis=1))
        return (mixed, log_total - chosen)
    params = (w_query.astype(jnp.float32), w_key.astype(jnp.float32), w_value.astype(jnp.float32), b_query, b_value, w_out.astype(jnp.float32), b_out, ln1_gain, ln1_shift, w_in.astype(jnp.float32), b_in, w_back.astype(jnp.float32), b_back, ln2_gain, ln2_shift)
    (mixed, losses), pull = jax.vjp(forward, tokens.astype(jnp.float32), params)
    d_tokens, grads = pull((grad_out.astype(jnp.float32), jnp.ones_like(losses)))
    return (mixed.astype(jnp.bfloat16), losses, d_tokens, grads[0], grads[1], grads[2], grads[3], grads[4], grads[5], grads[6], grads[7], grads[8], grads[9], grads[10], grads[11], grads[12], grads[13], grads[14])
```

```python
import functools
import math

import jax
import jax.numpy as jnp
from jax import lax
from jax.experimental import pallas as pl
from jax.experimental.pallas import tpu as pltpu
from jax.sharding import PartitionSpec as P

HEAD = 64
ROW_LEN = 1024
PAIRS = 4
QLEN = 32
TILE = 128
ALIGN = 32
BLOCKS = (2, 3, 4, 5, 7, 10)

epsilon = 1e-12
masked_score = -1e30
highest = lax.Precision.HIGHEST
f32 = jnp.float32
bf16 = jnp.bfloat16
NT = (((1,), (1,)), ((), ()))
TN = (((0,), (0,)), ((), ()))
NN = (((1,), (0,)), ((), ()))


def mm(a, b, dims=NN):
    return lax.dot_general(a, b, dims, preferred_element_type=f32)


def segment_bounds(pass_len, start, count):
    rows = pass_len.shape[0]
    lens = [pass_len[:, j] for j in range(PAIRS)]
    cuts = [jnp.full((rows,), j * QLEN, jnp.int32) for j in range(PAIRS + 1)]
    for j in range(PAIRS):
        cuts.append(cuts[-1] + lens[j])
    cuts = jnp.stack(cuts, axis=1) + (jnp.arange(rows, dtype=jnp.int32) * ROW_LEN)[:, None]
    cuts = cuts.reshape(-1)
    place = start + jnp.arange(count, dtype=jnp.int32)
    below = cuts[None, :] <= place[:, None]
    low = jnp.max(jnp.where(below, cuts[None, :], start), axis=1)
    high = jnp.min(jnp.where(below, rows * ROW_LEN, cuts[None, :]), axis=1)
    outside = place >= rows * ROW_LEN
    low = jnp.where(outside, rows * ROW_LEN, low)
    high = jnp.where(outside, start + count, high)
    return jnp.clip(low - start, 0, count), jnp.clip(high - start, 0, count)


def cls_places(pass_len):
    lens = [pass_len[:, j] for j in range(PAIRS)]
    starts = [jnp.full_like(lens[0], j * QLEN) for j in range(PAIRS)]
    at = jnp.full_like(lens[0], PAIRS * QLEN)
    for j in range(PAIRS):
        starts.append(at)
        at = at + lens[j]
    return jnp.stack(starts, axis=1)


def by_span(blocks, count, act):
    least = 0
    for size in BLOCKS:
        if size * TILE > count:
            break

        @pl.when((blocks > least) & (blocks <= size))
        def _(size=size):
            act(size * TILE)

        least = size


def split_pair(block):
    lane = lax.broadcasted_iota(jnp.int32, block.shape, 1)
    even = lane < HEAD
    zero = jnp.zeros_like(block)
    return jnp.concatenate([jnp.where(even, block, zero), jnp.where(even, zero, block)], axis=0)


def join_pair(both):
    rows = both.shape[0] // 2
    lane = lax.broadcasted_iota(jnp.int32, (rows, both.shape[1]), 1)
    return jnp.where(lane < HEAD, both[:rows], both[rows:])


def write_bias(bias_ref, lo_ref, hi_ref, row, first, span):
    place = lax.broadcasted_iota(jnp.int32, (TILE, span), 1) + first
    low = lo_ref[pl.ds(row, TILE), :]
    high = hi_ref[pl.ds(row, TILE), :]
    bias_ref[:, :span] = jnp.where((place >= low) & (place < high), 0.0, masked_score)


def pair_weights(q2, k, bias):
    span = k.shape[0]
    scores = mm(q2, k, NT)
    scores = (scores.reshape(2, TILE, span) + bias[None]).reshape(2 * TILE, span)
    top = jnp.max(scores, axis=1, keepdims=True)
    raised = jnp.exp(scores - top)
    total = jnp.sum(raised, axis=1, keepdims=True)
    return raised * (1.0 / total)


def forward_kernel(halo, tiles_ref, lo_ref, hi_ref, q_ref, k_ref, v_ref, out_ref, bias_ref):
    count = k_ref.shape[0]
    pairs = q_ref.shape[1] // TILE
    tiles = q_ref.shape[0] // TILE

    def tile_step(tile, carry):
        here = tile + halo // TILE
        blocks = tiles_ref[1, here]

        def act(span):
            first = jnp.minimum(tiles_ref[0, here], count - span)
            first = pl.multiple_of(first, ALIGN)
            row = pl.multiple_of(tile * TILE, TILE)
            write_bias(bias_ref, lo_ref, hi_ref, pl.multiple_of(row + halo, TILE), first, span)

            def pair_step(pair, inner):
                lanes = pl.ds(pl.multiple_of(pair * TILE, TILE), TILE)
                q2 = split_pair(q_ref[pl.ds(row, TILE), lanes])
                k = k_ref[pl.ds(first, span), lanes]
                v = v_ref[pl.ds(first, span), lanes]
                weights = pair_weights(q2, k, bias_ref[:, :span]).astype(bf16)
                out_ref[pl.ds(row, TILE), lanes] = join_pair(mm(weights, v)).astype(bf16)
                return inner

            lax.fori_loop(0, pairs, pair_step, 0, unroll=2)

        by_span(blocks, count, act)
        return carry

    lax.fori_loop(0, tiles, tile_step, 0)


def attend_forward(bounds, queries, keys, values, halo):
    tiles, low, high = bounds
    vmem = pl.BlockSpec(memory_space=pltpu.VMEM)
    return pl.pallas_call(
        functools.partial(forward_kernel, halo),
        out_shape=jax.ShapeDtypeStruct(queries.shape, bf16),
        in_specs=[pl.BlockSpec(memory_space=pltpu.SMEM)] + [vmem] * 5,
        out_specs=vmem,
        scratch_shapes=[pltpu.VMEM((TILE, keys.shape[0]), f32)],
        compiler_params=pltpu.CompilerParams(vmem_limit_bytes=32 * 2**20),
        name="attend_forward",
    )(tiles, low, high, queries, keys, values)


def backward_kernel(
    halo, tiles_ref, lo_ref, hi_ref, q_ref, k_ref, v_ref, g_ref,
    dq_ref, dk_ref, dv_ref, bias_ref, dk_sum, dv_sum,
):
    count = k_ref.shape[0]
    own = dq_ref.shape[0]
    pairs = q_ref.shape[1] // TILE
    dk_sum[...] = jnp.zeros_like(dk_sum)
    dv_sum[...] = jnp.zeros_like(dv_sum)

    def tile_step(tile, carry):
        blocks = tiles_ref[2, tile]
        mine = (tile >= halo // TILE) & (tile < (halo + own) // TILE)

        def act(span):
            first = jnp.minimum(tiles_ref[0, tile], count - span)
            first = pl.multiple_of(first, ALIGN)
            row = pl.multiple_of(tile * TILE, TILE)
            write_bias(bias_ref, lo_ref, hi_ref, row, first, span)

            def pair_step(pair, inner):
                lanes = pl.ds(pl.multiple_of(pair * TILE, TILE), TILE)
                q2 = split_pair(q_ref[pl.ds(row, TILE), lanes])
                g2 = split_pair(g_ref[pl.ds(row, TILE), lanes])
                k = k_ref[pl.ds(first, span), lanes]
                v = v_ref[pl.ds(first, span), lanes]
                weights = pair_weights(q2, k, bias_ref[:, :span])
                slopes = mm(g2, v, NT)
                inner_sum = jnp.sum(weights * slopes, axis=1, keepdims=True)
                scores = (weights * (slopes - inner_sum)).astype(bf16)
                dv_sum[pl.ds(first, span), lanes] += mm(weights.astype(bf16), g2, TN)
                dk_sum[pl.ds(first, span), lanes] += mm(scores, q2, TN)

                @pl.when(mine)
                def _():
                    grad = join_pair(mm(scores, k)).astype(bf16)
                    to = pl.multiple_of(row - halo, TILE)
                    dq_ref[pl.ds(to, TILE), lanes] = grad * jnp.asarray(1.0 / math.sqrt(HEAD), bf16)

                return inner

            lax.fori_loop(0, pairs, pair_step, 0)

        by_span(blocks, count, act)
        return carry

    lax.fori_loop(0, count // TILE, tile_step, 0)
    dk_ref[...] = dk_sum[pl.ds(halo, own), :].astype(bf16)
    dv_ref[...] = dv_sum[pl.ds(halo, own), :].astype(bf16)


def attend_backward(bounds, queries, keys, values, grads, halo):
    tiles, low, high = bounds
    count, width = keys.shape
    vmem = pl.BlockSpec(memory_space=pltpu.VMEM)
    out = jax.ShapeDtypeStruct((count - 2 * halo, width), bf16)
    return pl.pallas_call(
        functools.partial(backward_kernel, halo),
        out_shape=(out, out, out),
        in_specs=[pl.BlockSpec(memory_space=pltpu.SMEM)] + [vmem] * 6,
        out_specs=(vmem, vmem, vmem),
        scratch_shapes=[
            pltpu.VMEM((TILE, count), f32),
            pltpu.VMEM((count, width), f32),
            pltpu.VMEM((count, width), f32),
        ],
        compiler_params=pltpu.CompilerParams(vmem_limit_bytes=44 * 2**20),
        name="attend_backward",
    )(tiles, low, high, queries, keys, values, grads)


def norm_parts(values):
    center = values - jnp.mean(values, axis=-1, keepdims=True)
    spread = jnp.mean(center * center, axis=-1, keepdims=True)
    return center, lax.rsqrt(spread + epsilon)


def norm_pull(grad, unit, inverse, gain):
    scaled = grad * gain
    mean = jnp.mean(scaled, axis=-1, keepdims=True)
    along = jnp.mean(scaled * unit, axis=-1, keepdims=True)
    return inverse * (scaled - mean - unit * along)


def gelu_both(before):
    half = 0.5 * (1.0 + lax.erf(before * math.sqrt(0.5)))
    bell = jnp.exp(-0.5 * before * before) * (1.0 / math.sqrt(2.0 * math.pi))
    return before * half, half + before * bell


def turn(ways, step):
    return [(i, (i - step) % ways) for i in range(ways)]


def halo_rows(values, halo):
    ways = lax.axis_size("mp")
    before = lax.ppermute(values[-halo:], "mp", [(i, i + 1) for i in range(ways - 1)])
    after = lax.ppermute(values[:halo], "mp", [(i + 1, i) for i in range(ways - 1)])
    return jnp.concatenate([before, values, after], axis=0)


def ring_stack(values):
    ways = lax.axis_size("mp")
    held = [values] + [lax.ppermute(values, "mp", turn(ways, step)) for step in range(1, ways)]
    return jnp.roll(jnp.stack(held), lax.axis_index("mp"), axis=0)


def group_tables(table):
    ways = lax.axis_size("mp")
    data_ways = lax.axis_size("dp")
    total = table
    for step in range(1, ways):
        total = total + lax.ppermute(table, "mp", turn(ways, step))
    held = total[None]
    data_index = lax.axis_index("dp")
    level = 1
    while level < data_ways:
        other = lax.ppermute(held, "dp", [(i, i ^ level) for i in range(data_ways)])
        first = (data_index & level) == 0
        held = jnp.where(
            first, jnp.concatenate([held, other]), jnp.concatenate([other, held])
        )
        level *= 2
    return held


def gather_rows(shard):
    data_ways = lax.axis_size("dp")
    ways = lax.axis_size("mp")
    rows = shard.shape[0] // data_ways
    own = lax.dynamic_slice_in_dim(shard, lax.axis_index("dp") * rows, rows, 0)
    full = lax.all_gather(own, ("dp", "mp"), axis=0, tiled=True)
    return full.reshape(data_ways, ways, rows, shard.shape[1])


def reduce_rows(grads):
    data_ways, ways, rows, width = grads.shape
    own = lax.psum_scatter(
        grads.reshape(data_ways * ways * rows, width), ("dp", "mp"), scatter_dimension=0, tiled=True
    )
    return lax.all_gather(own, "dp", axis=0, tiled=True)


def shards(
    tokens, grad_out, pass_len, labels, w_query, w_key, w_value, b_query, b_value, w_out, b_out,
    ln1_gain, ln1_shift, w_in, b_in, w_back, b_back, ln2_gain, ln2_shift,
):
    ways = lax.axis_size("mp")
    data_ways = lax.axis_size("dp")
    mp_index = lax.axis_index("mp")
    data_index = lax.axis_index("dp")
    own_rows, width = tokens.shape
    rows_here = pass_len.shape[0]
    inner = w_query.shape[1]
    units = w_in.shape[1]
    halo = ROW_LEN // 4
    count = own_rows + 2 * halo
    scale = 1.0 / math.sqrt(HEAD)
    temper = 2.0 / math.sqrt(width)

    attn_shard = jnp.concatenate([w_query.T, w_key.T, w_value.T, w_out], axis=0)
    attn_all = gather_rows(attn_shard)
    in_all = gather_rows(w_in.T).reshape(ways * units, width)
    back_all = gather_rows(w_back).reshape(ways * units, width)
    attn_all = attn_all.transpose(1, 0, 2, 3).reshape(ways, 4, inner, width)
    attn_all = attn_all.transpose(1, 0, 2, 3).reshape(4, ways * inner, width)
    biases = ring_stack(jnp.concatenate([b_query, b_value, b_in]))
    bias_query = biases[:, :inner].reshape(-1)
    bias_value = biases[:, inner : 2 * inner].reshape(-1)
    bias_in = biases[:, 2 * inner :].reshape(ways, data_ways, units // data_ways)
    bias_in = bias_in.transpose(1, 0, 2).reshape(-1)

    low, high = segment_bounds(pass_len, mp_index * own_rows - halo, count)
    tile_low = low[::TILE] // ALIGN * ALIGN
    tile_high = high[TILE - 1 :: TILE]
    blocks = (tile_high - tile_low + TILE - 1) // TILE
    tile = jnp.arange(count // TILE, dtype=jnp.int32)
    before_own = tile < halo // TILE
    after_own = tile >= (halo + own_rows) // TILE
    reach = (~before_own | (tile_high > halo)) & (~after_own | (low[::TILE] < halo + own_rows))
    tiles = jnp.stack([tile_low, blocks, jnp.where(reach, blocks, 0)])
    bounds = (tiles, low[:, None], high[:, None])

    window = halo_rows(tokens, halo)
    queries = ((mm(window, attn_all[0], NT) + bias_query) * scale).astype(bf16)
    keys = mm(window, attn_all[1], NT).astype(bf16)
    values = (mm(window, attn_all[2], NT) + bias_value).astype(bf16)
    context = attend_forward(bounds, queries[halo : halo + own_rows], keys, values, halo)
    first_sum = tokens.astype(f32) + mm(context, attn_all[3]) + b_out
    center_one, inverse_one = norm_parts(first_sum)
    unit_one = center_one * inverse_one
    hidden = unit_one * ln1_gain + ln1_shift
    hidden_low = hidden.astype(bf16)

    active, slope = gelu_both(mm(hidden_low, in_all, NT) + bias_in)
    active = active.astype(bf16)
    slope = slope.astype(bf16)
    second_sum = hidden + mm(active, back_all) + b_back
    center_two, inverse_two = norm_parts(second_sum)
    unit_two = center_two * inverse_two
    mixed = (unit_two * ln2_gain + ln2_shift).astype(bf16)

    query_count = PAIRS * rows_here
    places = cls_places(pass_len) + (jnp.arange(rows_here, dtype=jnp.int32) * ROW_LEN)[:, None]
    table_places = jnp.concatenate([places[:, :PAIRS].reshape(-1), places[:, PAIRS:].reshape(-1)])
    table_places = table_places - mp_index * own_rows
    picker = table_places[:, None] == jnp.arange(own_rows, dtype=jnp.int32)[None, :]
    table = mm(picker.astype(bf16), mixed).astype(bf16)
    digits = jnp.concatenate([labels // 32, labels % 32]).astype(bf16)
    digits = jnp.where(mp_index == 0, digits, 0)
    extra = jnp.zeros((8, width), bf16).at[0, : 2 * query_count].set(digits)
    tables = group_tables(jnp.concatenate([table, extra]))
    all_count = data_ways * query_count
    query_cls = tables[:, :query_count].reshape(all_count, width)
    passage_cls = tables[:, query_count : 2 * query_count].reshape(all_count, width)
    digits = tables[:, 2 * query_count, : 2 * query_count].astype(jnp.int32)
    all_labels = (digits[:, :query_count] * 32 + digits[:, query_count:]).reshape(-1)

    logits = mm(query_cls, passage_cls, NT) * temper
    targets = all_labels[:, None] == jnp.arange(all_count, dtype=jnp.int32)[None, :]
    top = jnp.max(logits, axis=1, keepdims=True)
    raised = jnp.exp(logits - top)
    total = jnp.sum(raised, axis=1, keepdims=True)
    losses = top[:, 0] + jnp.log(total[:, 0]) - jnp.sum(jnp.where(targets, logits, 0.0), axis=1)
    query_losses = lax.dynamic_slice_in_dim(losses, data_index * query_count, query_count)
    grad_logits = (raised / total - targets.astype(f32)) * temper
    rows_of = lax.dynamic_slice_in_dim(grad_logits, data_index * query_count, query_count, 0)
    columns_of = lax.dynamic_slice_in_dim(grad_logits, data_index * query_count, query_count, 1)
    grad_cls = jnp.concatenate(
        [
            jnp.dot(rows_of, passage_cls.astype(f32), precision=highest),
            jnp.dot(columns_of.T, query_cls.astype(f32), precision=highest),
        ]
    )
    grad_mixed = grad_out.astype(f32) + jnp.dot(
        picker.astype(f32).T, grad_cls, precision=highest
    )

    grad_second = norm_pull(grad_mixed, unit_two, inverse_two, ln2_gain)
    stats = [
        jnp.sum(grad_mixed * unit_two, axis=0),
        jnp.sum(grad_mixed, axis=0),
        jnp.sum(grad_second, axis=0),
    ]
    second_low = grad_second.astype(bf16)
    grad_before = (mm(second_low, back_all, NT) * slope.astype(f32)).astype(bf16)
    grad_hidden = grad_second + mm(grad_before, in_all)
    grad_first = norm_pull(grad_hidden, unit_one, inverse_one, ln1_gain)
    stats += [
        jnp.sum(grad_hidden * unit_one, axis=0),
        jnp.sum(grad_hidden, axis=0),
        jnp.sum(grad_first, axis=0),
    ]
    first_low = grad_first.astype(bf16)
    first_window = halo_rows(first_low, halo)
    d_back = mm(active, second_low, TN).astype(bf16)
    d_in = mm(grad_before, hidden_low, TN).astype(bf16)
    unit_rows = units // data_ways
    back_sum = reduce_rows(d_back.reshape(data_ways, ways, unit_rows, width))
    in_sum = reduce_rows(d_in.reshape(data_ways, ways, unit_rows, width))
    d_b_in = jnp.sum(grad_before, axis=0, dtype=f32)
    d_b_in = d_b_in.reshape(data_ways, ways, unit_rows).transpose(1, 0, 2).reshape(ways, units)

    grad_context = mm(first_window, attn_all[3], NT).astype(bf16)
    grad_queries, grad_keys, grad_values = attend_backward(
        bounds, queries, keys, values, grad_context, halo
    )
    d_attn = jnp.stack(
        [
            mm(grad_queries, tokens, TN),
            mm(grad_keys, tokens, TN),
            mm(grad_values, tokens, TN),
            mm(context, first_low, TN),
        ]
    ).astype(bf16)
    d_attn = d_attn.reshape(4, ways, inner, width).transpose(1, 0, 2, 3)
    d_attn = d_attn.reshape(ways, data_ways, 4 * inner // data_ways, width).transpose(1, 0, 2, 3)
    attn_sum = reduce_rows(d_attn).astype(f32).reshape(4, inner, width)
    d_b_query = jnp.sum(grad_queries, axis=0, dtype=f32)
    d_b_value = jnp.sum(grad_values, axis=0, dtype=f32)
    d_tokens = (
        grad_first
        + mm(grad_queries, attn_all[0])
        + mm(grad_keys, attn_all[1])
        + mm(grad_values, attn_all[2])
    )

    vectors = [v.reshape(ways, -1) for v in [*stats, d_b_query, d_b_value]] + [d_b_in]
    vectors = lax.psum(jnp.concatenate(vectors, axis=1), ("dp", "mp"))
    vectors = lax.dynamic_index_in_dim(vectors, mp_index, 0, keepdims=False)
    part = width // ways
    pieces = [vectors[i * part : (i + 1) * part] for i in range(8)]
    return (
        mixed,
        query_losses,
        d_tokens,
        attn_sum[0].T,
        attn_sum[1].T,
        attn_sum[2].T,
        pieces[6],
        pieces[7],
        attn_sum[3],
        pieces[5],
        pieces[3],
        pieces[4],
        in_sum.astype(f32).T,
        vectors[8 * part :],
        back_sum.astype(f32),
        pieces[2],
        pieces[0],
        pieces[1],
    )


def solution(mesh):
    return jax.shard_map(
        shards,
        mesh=mesh,
        in_specs=(
            P(("dp", "mp"), None), P(("dp", "mp"), None), P("dp", None), P("dp"),
            P(None, "mp"), P(None, "mp"), P(None, "mp"), P("mp"), P("mp"), P("mp", None), P(),
            P(), P(), P(None, "mp"), P("mp"), P("mp", None), P(), P(), P(),
        ),
        out_specs=(
            P(("dp", "mp"), None), P("dp"), P(("dp", "mp"), None),
            P(None, "mp"), P(None, "mp"), P(None, "mp"), P("mp"), P("mp"), P("mp", None),
            P("mp"), P("mp"), P("mp"), P(None, "mp"), P("mp"), P("mp", None), P("mp"), P("mp"), P("mp"),
        ),
        check_vma=False,
    )
```

```python
import functools
import math

import jax
import jax.numpy as jnp
from jax import lax
from jax.experimental import pallas as pl
from jax.experimental.pallas import tpu as pltpu
from jax.sharding import PartitionSpec as P

HEAD = 64
ROW_LEN = 1024
PAIRS = 4
QLEN = 32
TILE = 128
ALIGN = 32
BLOCKS = (2, 3, 4, 5, 7, 10)

epsilon = 1e-12
masked_score = -1e30
highest = lax.Precision.HIGHEST
f32 = jnp.float32
bf16 = jnp.bfloat16
NT = (((1,), (1,)), ((), ()))
TN = (((0,), (0,)), ((), ()))
NN = (((1,), (0,)), ((), ()))


def mm(a, b, dims=NN):
    return lax.dot_general(a, b, dims, preferred_element_type=f32)


def segment_bounds(pass_len, start, count):
    rows = pass_len.shape[0]
    lens = [pass_len[:, j] for j in range(PAIRS)]
    cuts = [jnp.full((rows,), j * QLEN, jnp.int32) for j in range(PAIRS + 1)]
    for j in range(PAIRS):
        cuts.append(cuts[-1] + lens[j])
    cuts = jnp.stack(cuts, axis=1) + (jnp.arange(rows, dtype=jnp.int32) * ROW_LEN)[:, None]
    cuts = cuts.reshape(-1)
    place = start + jnp.arange(count, dtype=jnp.int32)
    below = cuts[None, :] <= place[:, None]
    low = jnp.max(jnp.where(below, cuts[None, :], start), axis=1)
    high = jnp.min(jnp.where(below, rows * ROW_LEN, cuts[None, :]), axis=1)
    outside = place >= rows * ROW_LEN
    low = jnp.where(outside, rows * ROW_LEN, low)
    high = jnp.where(outside, start + count, high)
    return jnp.clip(low - start, 0, count), jnp.clip(high - start, 0, count)


def cls_places(pass_len):
    lens = [pass_len[:, j] for j in range(PAIRS)]
    starts = [jnp.full_like(lens[0], j * QLEN) for j in range(PAIRS)]
    at = jnp.full_like(lens[0], PAIRS * QLEN)
    for j in range(PAIRS):
        starts.append(at)
        at = at + lens[j]
    return jnp.stack(starts, axis=1)


def by_span(blocks, count, act):
    least = 0
    for size in BLOCKS:
        if size * TILE > count:
            break

        @pl.when((blocks > least) & (blocks <= size))
        def _(size=size):
            act(size * TILE)

        least = size


def split_pair(block):
    lane = lax.broadcasted_iota(jnp.int32, block.shape, 1)
    even = lane < HEAD
    zero = jnp.zeros_like(block)
    return jnp.concatenate([jnp.where(even, block, zero), jnp.where(even, zero, block)], axis=0)


def join_pair(both):
    rows = both.shape[0] // 2
    lane = lax.broadcasted_iota(jnp.int32, (rows, both.shape[1]), 1)
    return jnp.where(lane < HEAD, both[:rows], both[rows:])


def write_bias(bias_ref, lo_ref, hi_ref, row, first, span):
    place = lax.broadcasted_iota(jnp.int32, (TILE, span), 1) + first
    low = lo_ref[pl.ds(row, TILE), :]
    high = hi_ref[pl.ds(row, TILE), :]
    bias_ref[:, :span] = jnp.where((place >= low) & (place < high), 0.0, masked_score)


def pair_weights(q2, k, bias):
    span = k.shape[0]
    scores = mm(q2, k, NT)
    scores = (scores.reshape(2, TILE, span) + bias[None]).reshape(2 * TILE, span)
    top = jnp.max(scores, axis=1, keepdims=True)
    raised = jnp.exp(scores - top)
    total = jnp.sum(raised, axis=1, keepdims=True)
    return raised * (1.0 / total)


def forward_kernel(halo, tiles_ref, lo_ref, hi_ref, q_ref, k_ref, v_ref, out_ref, bias_ref):
    count = k_ref.shape[0]
    pairs = q_ref.shape[1] // TILE
    tiles = q_ref.shape[0] // TILE

    def tile_step(tile, carry):
        here = tile + halo // TILE
        blocks = tiles_ref[1, here]

        def act(span):
            first = jnp.minimum(tiles_ref[0, here], count - span)
            first = pl.multiple_of(first, ALIGN)
            row = pl.multiple_of(tile * TILE, TILE)
            write_bias(bias_ref, lo_ref, hi_ref, pl.multiple_of(row + halo, TILE), first, span)

            def pair_step(pair, inner):
                lanes = pl.ds(pl.multiple_of(pair * TILE, TILE), TILE)
                q2 = split_pair(q_ref[pl.ds(row, TILE), lanes])
                k = k_ref[pl.ds(first, span), lanes]
                v = v_ref[pl.ds(first, span), lanes]
                weights = pair_weights(q2, k, bias_ref[:, :span]).astype(bf16)
                out_ref[pl.ds(row, TILE), lanes] = join_pair(mm(weights, v)).astype(bf16)
                return inner

            lax.fori_loop(0, pairs, pair_step, 0, unroll=pairs)

        by_span(blocks, count, act)
        return carry

    lax.fori_loop(0, tiles, tile_step, 0)


def lasting(micros):
    return pl.CostEstimate(flops=int(micros * 1e9), bytes_accessed=int(micros * 3.5e6), transcendentals=0)


def lane_group(array, group, groups):
    return pl.BlockSpec((array.shape[0], array.shape[1] // groups), lambda i: (0, group))


def whole(array):
    return pl.BlockSpec(array.shape, lambda i: (0, 0))


def attend_forward(bounds, queries, keys, values, halo, group, groups):
    tiles, low, high = bounds
    rows, width = queries.shape
    arrays = (queries, keys, values)
    return pl.pallas_call(
        functools.partial(forward_kernel, halo),
        grid=(1,),
        out_shape=jax.ShapeDtypeStruct((rows, width // groups), bf16),
        in_specs=[pl.BlockSpec(memory_space=pltpu.SMEM), whole(low), whole(high)]
        + [lane_group(a, group, groups) for a in arrays],
        out_specs=pl.BlockSpec((rows, width // groups), lambda i: (0, 0)),
        scratch_shapes=[pltpu.VMEM((TILE, keys.shape[0]), f32)],
        compiler_params=pltpu.CompilerParams(vmem_limit_bytes=32 * 2**20),
        cost_estimate=lasting(18 / groups),
        name="attend_forward",
    )(tiles, low, high, *arrays)


def backward_kernel(
    halo, tiles_ref, lo_ref, hi_ref, q_ref, k_ref, v_ref, g_ref,
    dq_ref, dk_ref, dv_ref, bias_ref, dk_sum, dv_sum,
):
    count = k_ref.shape[0]
    own = dq_ref.shape[0]
    pairs = q_ref.shape[1] // TILE
    dk_sum[...] = jnp.zeros_like(dk_sum)
    dv_sum[...] = jnp.zeros_like(dv_sum)

    def tile_step(tile, carry):
        blocks = tiles_ref[2, tile]
        mine = (tile >= halo // TILE) & (tile < (halo + own) // TILE)

        def act(span):
            first = jnp.minimum(tiles_ref[0, tile], count - span)
            first = pl.multiple_of(first, ALIGN)
            row = pl.multiple_of(tile * TILE, TILE)
            write_bias(bias_ref, lo_ref, hi_ref, row, first, span)

            def pair_step(pair, inner):
                lanes = pl.ds(pl.multiple_of(pair * TILE, TILE), TILE)
                q2 = split_pair(q_ref[pl.ds(row, TILE), lanes])
                g2 = split_pair(g_ref[pl.ds(row, TILE), lanes])
                k = k_ref[pl.ds(first, span), lanes]
                v = v_ref[pl.ds(first, span), lanes]
                weights = pair_weights(q2, k, bias_ref[:, :span])
                slopes = mm(g2, v, NT)
                inner_sum = jnp.sum(weights * slopes, axis=1, keepdims=True)
                scores = (weights * (slopes - inner_sum)).astype(bf16)
                dv_sum[pl.ds(first, span), lanes] += mm(weights.astype(bf16), g2, TN)
                dk_sum[pl.ds(first, span), lanes] += mm(scores, q2, TN)

                @pl.when(mine)
                def _():
                    grad = join_pair(mm(scores, k)).astype(bf16)
                    to = pl.multiple_of(row - halo, TILE)
                    dq_ref[pl.ds(to, TILE), lanes] = grad * jnp.asarray(1.0 / math.sqrt(HEAD), bf16)

                return inner

            lax.fori_loop(0, pairs, pair_step, 0, unroll=pairs)

        by_span(blocks, count, act)
        return carry

    lax.fori_loop(0, count // TILE, tile_step, 0)
    dk_ref[...] = dk_sum[pl.ds(halo, own), :].astype(bf16)
    dv_ref[...] = dv_sum[pl.ds(halo, own), :].astype(bf16)


def attend_backward(bounds, queries, keys, values, grads, halo, group, groups):
    tiles, low, high = bounds
    count, width = keys.shape
    lanes = width // groups
    arrays = (queries, keys, values, grads)
    out = jax.ShapeDtypeStruct((count - 2 * halo, lanes), bf16)
    return pl.pallas_call(
        functools.partial(backward_kernel, halo),
        grid=(1,),
        out_shape=(out, out, out),
        in_specs=[pl.BlockSpec(memory_space=pltpu.SMEM), whole(low), whole(high)]
        + [lane_group(a, group, groups) for a in arrays],
        out_specs=(pl.BlockSpec(out.shape, lambda i: (0, 0)),) * 3,
        scratch_shapes=[
            pltpu.VMEM((TILE, count), f32),
            pltpu.VMEM((count, lanes), f32),
            pltpu.VMEM((count, lanes), f32),
        ],
        compiler_params=pltpu.CompilerParams(vmem_limit_bytes=32 * 2**20),
        cost_estimate=lasting(42 / groups),
        name="attend_backward",
    )(tiles, low, high, *arrays)


SMEM = pl.BlockSpec(memory_space=pltpu.SMEM)
VMEM = pl.BlockSpec(memory_space=pltpu.VMEM)
PLANE = 8


def local(kernel, place, arrays, outs, scratch, micros, name):
    return pl.pallas_call(
        kernel,
        out_shape=tuple(jax.ShapeDtypeStruct(shape, dtype) for shape, dtype in outs),
        in_specs=[SMEM] + [VMEM] * len(arrays),
        out_specs=(VMEM,) * len(outs),
        scratch_shapes=[pltpu.VMEM(shape, dtype) for shape, dtype in scratch],
        compiler_params=pltpu.CompilerParams(vmem_limit_bytes=48 * 2**20),
        cost_estimate=lasting(micros),
        name=name,
    )(place, *arrays)


def own_heads_kernel(place_ref, q_ref, k_ref, v_ref, out_ref, rows_ref):
    place = place_ref[0]
    eighths = q_ref.shape[0] // PLANE
    slabs = q_ref.shape[0] // 8
    for i, ref in enumerate((q_ref, k_ref, v_ref)):
        rows_ref[pl.ds(i * slabs, slabs)] = ref[...].astype(f32).reshape(slabs, 8, -1)
    heads = 3 * eighths // 8
    for j in range(PLANE):
        held = [rows_ref[h * PLANE + (place ^ j)] for h in range(heads)]
        out_ref[j] = jnp.concatenate(held, axis=0).astype(bf16)


def own_units_kernel(place_ref, o_ref, i_ref, b_ref, out_ref, in_ref, back_ref, rows_ref, units_ref):
    place = place_ref[0]
    rows = in_ref.shape[1]
    heads = out_ref.shape[1] // 8
    rows_ref[...] = o_ref[...].astype(f32).reshape(rows_ref.shape)
    units_ref[...] = i_ref[...].astype(f32).T.reshape(units_ref.shape)
    for j in range(PLANE):
        held = [rows_ref[h * PLANE + (place ^ j)] for h in range(heads)]
        out_ref[j] = jnp.concatenate(held, axis=0).astype(bf16)
        in_ref[j] = units_ref[place ^ j].astype(bf16)
        back_ref[j] = b_ref[pl.ds(pl.multiple_of((place ^ j) * rows, rows), rows), :]


def stage_eighths(own_ref, near_ref, far_ref, member, first, stage_ref):
    rows = stage_ref.shape[1]
    for j in range(PLANE):
        if member == 0:
            stage_ref[j] = own_ref[j].astype(f32)
        else:
            ref = near_ref if j < 4 else far_ref
            stage_ref[j] = ref[j % 4, member - 1, pl.ds(first, rows), :].astype(f32)


def head_block(stage_ref, head):
    return jnp.concatenate([stage_ref[j, pl.ds(head * 8, 8), :] for j in range(PLANE)], axis=0)


def project_kernel(
    place_ref, left_ref, tokens_ref, right_ref, own_ref, near_ref, far_ref, bq_ref, bv_ref,
    q_ref, k_ref, v_ref, w_ref, x_ref, stage_ref,
):
    ways = near_ref.shape[1] + 1
    heads = own_ref.shape[1] // 24
    halo = left_ref.shape[0]
    own = tokens_ref.shape[0]
    width = tokens_ref.shape[1]
    inner = heads * HEAD
    x_ref[:halo] = left_ref[...]
    x_ref[pl.ds(halo, own)] = tokens_ref[...]
    x_ref[pl.ds(halo + own, halo)] = right_ref[...]
    for member in range(ways):
        stage_eighths(own_ref, near_ref, far_ref, member, 0, stage_ref)
        for kind in range(3):
            blocks = [head_block(stage_ref, kind * heads + h) for h in range(heads)]
            at = kind * width + member * inner
            w_ref[pl.ds(at, inner)] = jnp.concatenate(blocks, axis=0).astype(bf16)

    def step(i, carry):
        rows = pl.ds(pl.multiple_of(i * 256, 256), 256)
        x = x_ref[rows, :]
        q = mm(x, w_ref[:width], NT) + bq_ref[...]
        q_ref[rows, :] = (q * (1.0 / math.sqrt(HEAD))).astype(bf16)
        k_ref[rows, :] = mm(x, w_ref[pl.ds(width, width)], NT).astype(bf16)
        v_ref[rows, :] = (mm(x, w_ref[pl.ds(2 * width, width)], NT) + bv_ref[...]).astype(bf16)
        return carry

    lax.fori_loop(0, x_ref.shape[0] // 256, step, 0)


def join_units_kernel(place_ref, own_ref, near_ref, far_ref, out_ref):
    rows = own_ref.shape[1]
    ways = near_ref.shape[1] + 1
    for j in range(PLANE):
        ref = near_ref if j < 4 else far_ref
        out_ref[pl.ds(j * ways * rows, rows), :] = own_ref[j]
        for member in range(1, ways):
            at = (j * ways + member) * rows
            out_ref[pl.ds(at, rows), :] = ref[j % 4, member - 1, :rows, :]


def join_in_out_kernel(place_ref, own_ref, own_out_ref, near_ref, far_ref, in_ref, out_ref, stage_ref):
    join_units_kernel(place_ref, own_ref, near_ref, far_ref, in_ref)
    rows = own_ref.shape[1]
    heads = own_out_ref.shape[1] // 8
    for member in range(near_ref.shape[1] + 1):
        stage_eighths(own_out_ref, near_ref, far_ref, member, rows, stage_ref)
        for h in range(heads):
            block = head_block(stage_ref, h)
            out_ref[pl.ds((member * heads + h) * HEAD, HEAD), :] = block.astype(bf16)


def piece_grads_kernel(groups, place_ref, *refs):
    grad_refs, context_refs = refs[: 3 * groups], refs[3 * groups : 3 * groups + 2]
    tokens_ref, first_ref, vectors_ref, keep_ref, send_ref, sum_ref = refs[3 * groups + 2 :]
    place = place_ref[0]
    ways = vectors_ref.shape[0]
    width = tokens_ref.shape[1]
    inner = width // ways
    heads = inner // HEAD

    def put(kind, first_head, block):
        for i in range(block.shape[0] // HEAD):
            member, h = divmod(first_head + i, heads)
            for j in range(PLANE):
                part = block[i * HEAD + j * 8 : i * HEAD + j * 8 + 8]
                sum_ref[j * ways + member, pl.ds((kind * heads + h) * 8, 8), :] = part

    lanes = width // groups
    for kind in range(3):
        for g in range(groups):
            put(kind, g * lanes // HEAD, mm(grad_refs[kind * groups + g][...], tokens_ref[...], TN))
    for g, ref in enumerate(context_refs):
        put(3, g * width // 2 // HEAD, mm(ref[...], first_ref[...], TN))
    lane = lax.broadcasted_iota(jnp.int32, (width, width), 0)
    to = lax.broadcasted_iota(jnp.int32, (width, width), 1)
    member = sum((lane >= i * inner).astype(jnp.int32) for i in range(1, ways))
    within = lane - member * inner
    spot = (within & ~(HEAD - 8)) | ((((within >> 3) & 7) ^ place) << 3)
    row = lax.broadcasted_iota(jnp.int32, (8, width), 0)
    column = lax.broadcasted_iota(jnp.int32, (8, width), 1)
    of = sum((column >= i * inner).astype(jnp.int32) for i in range(1, ways))
    ones = jnp.ones((8, tokens_ref.shape[0]), bf16)
    lines = jnp.zeros((8, width), f32)
    for kind, first in ((0, width - 2 * inner), (2, width - inner)):
        sums = [mm(ones, grad_refs[kind * groups + g][...]) for g in range(groups)]
        sums = jnp.where(of == row, jnp.concatenate(sums, axis=1), 0.0)
        chosen = jnp.where(spot + first == to, 1.0, 0.0).astype(bf16)
        lines = lines + mm(sums.astype(bf16), chosen)
    below = 4 * heads * 8
    for i in range(ways):
        block = vectors_ref[i] + jnp.where(row == 2, lines[i : i + 1], 0.0)
        for j in range(PLANE):
            sum_ref[j * ways + i, pl.ds(below, 8), :] = block
    half = keep_ref.shape[0]
    for i in range(half):
        keep_ref[i] = sum_ref[i].astype(bf16)
        send_ref[i] = sum_ref[half + i].astype(bf16)


def finish_heads_kernel(place_ref, near_ref, far_ref, q_ref, k_ref, v_ref, o_ref, rows_ref):
    place = place_ref[0]
    heads = o_ref.shape[0] // HEAD
    rows_ref[:4] = near_ref[...].astype(f32)
    rows_ref[4:] = far_ref[...].astype(f32)
    for kind, ref in enumerate((q_ref, k_ref, v_ref, o_ref)):
        held = []
        for h in range(heads):
            for p in range(PLANE):
                held.append(rows_ref[place ^ p, pl.ds((kind * heads + h) * 8, 8), :])
        block = jnp.concatenate(held, axis=0)
        ref[...] = block


def finish_units_kernel(
    place_ref, back_near_ref, back_far_ref, in_near_ref, in_far_ref, back_ref, in_ref, rows_ref, turned_ref
):
    place = place_ref[0]
    rows = back_near_ref.shape[1]
    rows_ref[:4] = back_near_ref[...].astype(f32)
    rows_ref[4:] = back_far_ref[...].astype(f32)
    for p in range(PLANE):
        back_ref[pl.ds(p * rows, rows), :] = rows_ref[place ^ p]
    rows_ref[:4] = in_near_ref[...].astype(f32)
    rows_ref[4:] = in_far_ref[...].astype(f32)
    for p in range(PLANE):
        turned_ref[pl.ds(p * rows, rows), :] = rows_ref[place ^ p]
    in_ref[...] = turned_ref[...].T


def norm_parts(values):
    center = values - jnp.mean(values, axis=-1, keepdims=True)
    spread = jnp.mean(center * center, axis=-1, keepdims=True)
    return center, lax.rsqrt(spread + epsilon)


def norm_pull(grad, unit, inverse, gain):
    scaled = grad * gain
    mean = jnp.mean(scaled, axis=-1, keepdims=True)
    along = jnp.mean(scaled * unit, axis=-1, keepdims=True)
    return inverse * (scaled - mean - unit * along)


def gelu_both(before):
    half = 0.5 * (1.0 + lax.erf(before * math.sqrt(0.5)))
    bell = jnp.exp(-0.5 * before * before) * (1.0 / math.sqrt(2.0 * math.pi))
    return before * half, half + before * bell


def turn(ways, step):
    return [(i, (i - step) % ways) for i in range(ways)]


def halo_rows(values, halo):
    ways = lax.axis_size("mp")
    before = lax.ppermute(values[-halo:], "mp", [(i, i + 1) for i in range(ways - 1)])
    after = lax.ppermute(values[:halo], "mp", [(i + 1, i) for i in range(ways - 1)])
    return before, after


def group_tables(table):
    ways = lax.axis_size("mp")
    data_ways = lax.axis_size("dp")
    total = table
    for step in range(1, ways):
        total = total + lax.ppermute(table, "mp", turn(ways, step))
    held = total[None]
    data_index = lax.axis_index("dp")
    level = 1
    while level < data_ways:
        other = lax.ppermute(held, "dp", [(i, i ^ level) for i in range(data_ways)])
        first = (data_index & level) == 0
        held = jnp.where(
            first, jnp.concatenate([held, other]), jnp.concatenate([other, held])
        )
        level *= 2
    return held


CORE, NEAR_X, NEAR_Y = 1, 2, 4


def swap(values, bit):
    ways = lax.axis_size("dp")
    return lax.ppermute(values, "dp", [(i, i ^ bit) for i in range(ways)])


def along(piece):
    ways = lax.axis_size("mp")
    return [lax.ppermute(piece, "mp", turn(ways, step)) for step in range(1, ways)]


def spread_at_once(values):
    others = [swap(values, bit) for bit in (NEAR_X, NEAR_Y, NEAR_X | NEAR_Y)]
    near = jnp.stack([values, *others])
    return near, swap(near, CORE)


def spread_x_first(values):
    both = jnp.stack([values, swap(values, NEAR_X)])
    return jnp.stack([both, swap(both, NEAR_Y)]).reshape(4, *values.shape)


def spread_y_first(values):
    both = jnp.stack([values, swap(values, NEAR_Y)])
    return jnp.stack([both, swap(both, NEAR_X)], axis=1).reshape(4, *values.shape)


def add(first, second):
    return (first.astype(f32) + second.astype(f32)).astype(bf16)


def sum_along(parts):
    ways = lax.axis_size("mp")
    data_ways = lax.axis_size("dp")
    total = parts[0].astype(f32)
    for step in range(1, ways):
        total = total + lax.ppermute(parts[step], "mp", turn(ways, -step)).astype(f32)
    level = PLANE
    while level < data_ways:
        total = total + swap(total, level)
        level *= 2
    return total


def shards(
    tokens, grad_out, pass_len, labels, w_query, w_key, w_value, b_query, b_value, w_out, b_out,
    ln1_gain, ln1_shift, w_in, b_in, w_back, b_back, ln2_gain, ln2_shift,
):
    ways = lax.axis_size("mp")
    data_ways = lax.axis_size("dp")
    mp_index = lax.axis_index("mp")
    data_index = lax.axis_index("dp")
    own_rows, width = tokens.shape
    rows_here = pass_len.shape[0]
    inner = w_query.shape[1]
    units = w_in.shape[1]
    halo = ROW_LEN // 4
    count = own_rows + 2 * halo
    scale = 1.0 / math.sqrt(HEAD)
    temper = 2.0 / math.sqrt(width)

    piece_rows = units // PLANE
    heads = inner // HEAD
    part = inner // PLANE
    place = ((data_index & CORE) << 2 | (data_index % PLANE) >> 1).reshape(1)
    (qkv_own,) = local(
        own_heads_kernel, place, (w_query.T, w_key.T, w_value.T), [((PLANE, 3 * part, width), bf16)],
        [((3 * heads * PLANE, 8, width), f32)], 4, "own_heads",
    )
    biases = jnp.concatenate([b_in, b_query, b_value])
    digits, rest = [], biases
    for _ in range(3):
        digits.append(lax.reduce_precision(rest, 8, 7))
        rest = rest - digits[-1]
    digits = jnp.stack(digits)
    lines = jnp.concatenate(
        [digits[:, :units], jnp.pad(digits[:, units:], ((0, 0), (0, width - 2 * inner)))]
    )
    lines = jnp.pad(lines, ((0, 2), (0, 0))).astype(bf16)
    qkv_along = along(jnp.concatenate([qkv_own[0], lines]))
    tokens_before, tokens_after = halo_rows(tokens, halo)
    w_out, w_in, w_back, place = lax.optimization_barrier((w_out, w_in, w_back, place, qkv_own))[:4]
    out_own, in_own, back_own = local(
        own_units_kernel, place, (w_out, w_in, w_back),
        [((PLANE, part, width), bf16), ((PLANE, piece_rows, width), bf16), ((PLANE, piece_rows, width), bf16)],
        [((heads * PLANE, 8, width), f32), ((PLANE, piece_rows, width), f32)], 5, "own_units",
    )
    in_piece = jnp.concatenate([in_own[0], out_own[0]])
    back_piece = back_own[0]
    qkv_along, in_piece, back_piece = lax.optimization_barrier((qkv_along, in_piece, back_piece))
    bias_rest = jnp.stack([piece[3 * part :] for piece in qkv_along]).astype(f32)
    bias_in_rest = bias_rest[:, 0] + bias_rest[:, 1] + bias_rest[:, 2]
    bias_head_rest = bias_rest[:, 3] + bias_rest[:, 4] + bias_rest[:, 5]
    bias_in_all = jnp.concatenate([b_in[None], bias_in_rest])
    bias_heads = jnp.concatenate(
        [jnp.concatenate([b_query, b_value])[None], bias_head_rest[:, : 2 * inner]]
    )
    qkv_near, qkv_far = spread_at_once(jnp.stack([piece[: 3 * part] for piece in qkv_along]))
    in_along = jnp.stack(along(in_piece))
    back_along = jnp.stack(along(back_piece))

    def in_order(parts):
        split = parts.reshape(*parts.shape[:-2], 2, 2, 2, parts.shape[-1])
        for axis, bit in ((-4, CORE), (-3, NEAR_Y), (-2, NEAR_X)):
            split = jnp.where((data_index & bit) != 0, jnp.flip(split, axis), split)
        return split.reshape(parts.shape)

    bias_heads = in_order(bias_heads.reshape(ways, 2 * heads, PLANE, 8)).reshape(ways, 2, inner)
    bias_query = bias_heads[:, 0].reshape(1, width)
    bias_value = bias_heads[:, 1].reshape(1, width)
    bias_in = in_order(bias_in_all.reshape(ways, PLANE, piece_rows))
    bias_in = bias_in.transpose(1, 0, 2).reshape(-1)

    low, high = segment_bounds(pass_len, mp_index * own_rows - halo, count)
    tile_low = low[::TILE] // ALIGN * ALIGN
    tile_high = high[TILE - 1 :: TILE]
    blocks = (tile_high - tile_low + TILE - 1) // TILE
    tile = jnp.arange(count // TILE, dtype=jnp.int32)
    before_own = tile < halo // TILE
    after_own = tile >= (halo + own_rows) // TILE
    reach = (~before_own | (tile_high > halo)) & (~after_own | (low[::TILE] < halo + own_rows))
    tiles = jnp.stack([tile_low, blocks, jnp.where(reach, blocks, 0)])
    bounds = (tiles, low[:, None], high[:, None])

    qkv = (tokens_before, tokens, tokens_after, qkv_own, qkv_near, qkv_far, bias_query, bias_value)
    queries, keys, values, qkv_all = local(
        project_kernel, place, qkv, [((count, width), bf16)] * 3 + [((3 * width, width), bf16)],
        [((count, width), bf16), ((PLANE, 3 * part, width), f32)], 10, "project",
    )
    in_near = spread_x_first(in_along)
    back_near = spread_y_first(back_along)
    in_far = swap(in_near, CORE)
    back_far = swap(back_near, CORE)
    own_queries = queries[halo : halo + own_rows]
    context = [attend_forward(bounds, own_queries, keys, values, halo, i, 2) for i in range(2)]
    in_all, out_all = local(
        join_in_out_kernel, place, (in_own, out_own, in_near, in_far),
        [((ways * units, width), bf16), ((width, width), bf16)],
        [((PLANE, part, width), f32)], 5, "join_in_out",
    )
    (back_all,) = local(
        join_units_kernel, place, (back_own, back_near, back_far),
        [((ways * units, width), bf16)], [], 4, "join_back",
    )
    attended = mm(context[0], out_all[: width // 2]) + mm(context[1], out_all[width // 2 :])
    first_sum = tokens.astype(f32) + attended + b_out
    center_one, inverse_one = norm_parts(first_sum)
    unit_one = center_one * inverse_one
    hidden = unit_one * ln1_gain + ln1_shift
    hidden_low = hidden.astype(bf16)

    active, slope = gelu_both(mm(hidden_low, in_all, NT) + bias_in)
    active, slope = lax.optimization_barrier((active.astype(bf16), slope.astype(bf16)))
    second_sum = hidden + mm(active, back_all) + b_back
    center_two, inverse_two = norm_parts(second_sum)
    unit_two = center_two * inverse_two
    mixed = (unit_two * ln2_gain + ln2_shift).astype(bf16)

    query_count = PAIRS * rows_here
    places = cls_places(pass_len) + (jnp.arange(rows_here, dtype=jnp.int32) * ROW_LEN)[:, None]
    table_places = jnp.concatenate([places[:, :PAIRS].reshape(-1), places[:, PAIRS:].reshape(-1)])
    table_places = table_places - mp_index * own_rows
    picker = table_places[:, None] == jnp.arange(own_rows, dtype=jnp.int32)[None, :]
    table = mm(picker.astype(bf16), mixed).astype(bf16)
    digits = jnp.concatenate([labels // 32, labels % 32]).astype(bf16)
    digits = jnp.where(mp_index == 0, digits, 0)
    extra = jnp.zeros((8, width), bf16).at[0, : 2 * query_count].set(digits)
    tables = group_tables(jnp.concatenate([table, extra]))
    all_count = data_ways * query_count
    query_cls = tables[:, :query_count].reshape(all_count, width)
    passage_cls = tables[:, query_count : 2 * query_count].reshape(all_count, width)
    digits = tables[:, 2 * query_count, : 2 * query_count].astype(jnp.int32)
    all_labels = (digits[:, :query_count] * 32 + digits[:, query_count:]).reshape(-1)

    logits = mm(query_cls, passage_cls, NT) * temper
    targets = all_labels[:, None] == jnp.arange(all_count, dtype=jnp.int32)[None, :]
    top = jnp.max(logits, axis=1, keepdims=True)
    raised = jnp.exp(logits - top)
    total = jnp.sum(raised, axis=1, keepdims=True)
    losses = top[:, 0] + jnp.log(total[:, 0]) - jnp.sum(jnp.where(targets, logits, 0.0), axis=1)
    query_losses = lax.dynamic_slice_in_dim(losses, data_index * query_count, query_count)
    grad_logits = (raised / total - targets.astype(f32)) * temper
    rows_of = lax.dynamic_slice_in_dim(grad_logits, data_index * query_count, query_count, 0)
    columns_of = lax.dynamic_slice_in_dim(grad_logits, data_index * query_count, query_count, 1)
    grad_cls = jnp.concatenate(
        [
            jnp.dot(rows_of, passage_cls.astype(f32), precision=highest),
            jnp.dot(columns_of.T, query_cls.astype(f32), precision=highest),
        ]
    )
    grad_mixed = grad_out.astype(f32) + jnp.dot(
        picker.astype(f32).T, grad_cls, precision=highest
    )

    grad_second = norm_pull(grad_mixed, unit_two, inverse_two, ln2_gain)
    stats = [
        jnp.sum(grad_mixed * unit_two, axis=0),
        jnp.sum(grad_mixed, axis=0),
        jnp.sum(grad_second, axis=0),
    ]
    second_low = grad_second.astype(bf16)

    def to_core(left, right):
        return mm(left[:, left.shape[1] // 2 :], right, TN).astype(bf16)

    def chip_sum(left, right, arrived):
        own = mm(left[:, : left.shape[1] // 2], right, TN)
        return add(own, arrived).reshape(2, 2, ways, piece_rows, width)

    back_sent = to_core(active, second_low)
    back_arrived = swap(back_sent, CORE)
    pulled, back_sent = lax.optimization_barrier((second_low, back_sent))
    grad_before = (mm(pulled, back_all, NT) * slope.astype(f32)).astype(bf16)
    back_sum = chip_sum(active, second_low, back_arrived)
    back_half = swap(back_sum[1], NEAR_Y)
    in_sent = to_core(grad_before, hidden_low)
    in_arrived = swap(in_sent, CORE)
    pulled, in_sent = lax.optimization_barrier((grad_before, in_sent))
    grad_hidden = grad_second + mm(pulled, in_all)
    grad_first = norm_pull(grad_hidden, unit_one, inverse_one, ln1_gain)
    stats += [
        jnp.sum(grad_hidden * unit_one, axis=0),
        jnp.sum(grad_hidden, axis=0),
        jnp.sum(grad_first, axis=0),
    ]
    first_low = grad_first.astype(bf16)
    first_before, first_after = halo_rows(first_low, halo)
    in_sum = chip_sum(grad_before, hidden_low, in_arrived)
    in_half = swap(in_sum[:, 1], NEAR_X)
    d_b_in = jnp.sum(grad_before, axis=0, dtype=f32).reshape(PLANE, ways, piece_rows)

    d_b_in = in_order(d_b_in.transpose(1, 0, 2)).reshape(ways, 1, units)
    turned = jnp.roll(jnp.stack(stats).reshape(6, ways, inner), -mp_index, axis=1).transpose(1, 0, 2)
    turned = jnp.pad(turned.reshape(ways, -1), ((0, 0), (0, 2 * inner))).reshape(ways, 2, width)
    vectors = jnp.concatenate([d_b_in, turned, jnp.zeros((ways, 5, width), f32)], axis=1)

    first_window = jnp.concatenate([first_before, first_low, first_after])
    grad_context = mm(first_window, out_all, NT).astype(bf16)
    groups = 3
    parts = []

    def attend(grads, group):
        return attend_backward(bounds, queries, keys, values, grads, halo, group, groups)

    grad_context, back_half, vectors = lax.optimization_barrier((grad_context, back_half, vectors))
    parts.append(attend(grad_context, 0))
    back_sum = add(back_sum[0], back_half)
    back_half = swap(back_sum[1], NEAR_X)
    grad_context, in_half, _ = lax.optimization_barrier((grad_context, in_half, parts[0]))
    parts.append(attend(grad_context, 1))
    in_sum = add(in_sum[:, 0], in_half)
    in_half = swap(in_sum[1], NEAR_Y)
    grad_context, back_half, in_half, _ = lax.optimization_barrier(
        (grad_context, back_half, in_half, parts[1])
    )
    parts.append(attend(grad_context, 2))
    early_sum = jnp.concatenate([add(back_sum[0], back_half), add(in_sum[0], in_half)], axis=1)
    early_own = sum_along([early_sum[i] for i in range(ways)]).astype(bf16)

    grad_parts = [g[i] for i in range(3) for g in parts]
    late_keep, late_sent = local(
        functools.partial(piece_grads_kernel, groups), place,
        (*grad_parts, *context, tokens, first_low, vectors),
        [((4 * ways, 4 * part + 8, width), bf16)] * 2,
        [((8 * ways, 4 * part + 8, width), f32)], 10, "piece_grads",
    )
    late_sum = add(late_keep, swap(late_sent, CORE)).reshape(4, ways, 4 * part + 8, width)
    arrived = [swap(late_sum[j], bit) for j, bit in ((1, NEAR_X), (2, NEAR_Y), (3, NEAR_X | NEAR_Y))]
    late_sum = sum((a.astype(f32) for a in arrived), late_sum[0].astype(f32)).astype(bf16)
    late_total = sum_along([late_sum[i] for i in range(ways)])
    late_near, late_far = spread_at_once(late_total[: 4 * part].astype(bf16))
    line = late_total[4 * part :]
    back_near = spread_x_first(early_own[:piece_rows])
    in_near = spread_y_first(early_own[piece_rows:])
    early_far = swap(jnp.stack([back_near, in_near]), CORE)
    grad_queries, grad_keys, grad_values = (jnp.concatenate(p, axis=1) for p in zip(*parts))
    d_tokens = (
        grad_first
        + mm(grad_queries, qkv_all[:width])
        + mm(grad_keys, qkv_all[width : 2 * width])
        + mm(grad_values, qkv_all[2 * width :])
    )

    d_query, d_key, d_value, d_out = local(
        finish_heads_kernel, place, (late_near, late_far),
        [((inner, width), f32)] * 4,
        [((PLANE, 4 * part, width), f32)], 5, "finish_heads",
    )
    d_back, d_in = local(
        finish_units_kernel, place, (back_near, early_far[0], in_near, early_far[1]),
        [((units, width), f32), ((width, units), f32)],
        [((PLANE, piece_rows, width), f32), ((units, width), f32)], 6, "finish_units",
    )
    norms = [line[1 + i // ways, i % ways * inner : (i % ways + 1) * inner] for i in range(8)]
    return (
        mixed,
        query_losses,
        d_tokens,
        d_query.T,
        d_key.T,
        d_value.T,
        norms[6],
        norms[7],
        d_out,
        norms[5],
        norms[3],
        norms[4],
        d_in,
        line[0],
        d_back,
        norms[2],
        norms[0],
        norms[1],
    )


def solution(mesh):
    return jax.shard_map(
        shards,
        mesh=mesh,
        in_specs=(
            P(("dp", "mp"), None), P(("dp", "mp"), None), P("dp", None), P("dp"),
            P(None, "mp"), P(None, "mp"), P(None, "mp"), P("mp"), P("mp"), P("mp", None), P(),
            P(), P(), P(None, "mp"), P("mp"), P("mp", None), P(), P(), P(),
        ),
        out_specs=(
            P(("dp", "mp"), None), P("dp"), P(("dp", "mp"), None),
            P(None, "mp"), P(None, "mp"), P(None, "mp"), P("mp"), P("mp"), P("mp", None),
            P("mp"), P("mp"), P("mp"), P(None, "mp"), P("mp"), P("mp", None), P("mp"), P("mp"), P("mp"),
        ),
        check_vma=False,
    )
```

```python
import functools
import math

import jax
import jax.numpy as jnp
from jax import lax
from jax.experimental import pallas as pl
from jax.experimental.pallas import tpu as pltpu
from jax.sharding import PartitionSpec as P

HEAD = 64
ROW_LEN = 1024
PAIRS = 4
QLEN = 32
TILE = 128
ALIGN = 32
BLOCKS = (2, 3, 4, 5, 7, 10)

epsilon = 1e-12
masked_score = -1e30
highest = lax.Precision.HIGHEST
f32 = jnp.float32
bf16 = jnp.bfloat16
NT = (((1,), (1,)), ((), ()))
TN = (((0,), (0,)), ((), ()))
NN = (((1,), (0,)), ((), ()))


def mm(a, b, dims=NN):
    return lax.dot_general(a, b, dims, preferred_element_type=f32)


def segment_bounds(pass_len, start, count):
    rows = pass_len.shape[0]
    lens = [pass_len[:, j] for j in range(PAIRS)]
    cuts = [jnp.full((rows,), j * QLEN, jnp.int32) for j in range(PAIRS + 1)]
    for j in range(PAIRS):
        cuts.append(cuts[-1] + lens[j])
    cuts = jnp.stack(cuts, axis=1) + (jnp.arange(rows, dtype=jnp.int32) * ROW_LEN)[:, None]
    cuts = cuts.reshape(-1)
    place = start + jnp.arange(count, dtype=jnp.int32)
    below = cuts[None, :] <= place[:, None]
    low = jnp.max(jnp.where(below, cuts[None, :], start), axis=1)
    high = jnp.min(jnp.where(below, rows * ROW_LEN, cuts[None, :]), axis=1)
    outside = place >= rows * ROW_LEN
    low = jnp.where(outside, rows * ROW_LEN, low)
    high = jnp.where(outside, start + count, high)
    return jnp.clip(low - start, 0, count), jnp.clip(high - start, 0, count)


def cls_places(pass_len):
    lens = [pass_len[:, j] for j in range(PAIRS)]
    starts = [jnp.full_like(lens[0], j * QLEN) for j in range(PAIRS)]
    at = jnp.full_like(lens[0], PAIRS * QLEN)
    for j in range(PAIRS):
        starts.append(at)
        at = at + lens[j]
    return jnp.stack(starts, axis=1)


def by_span(blocks, count, act):
    least = 0
    for size in BLOCKS:
        if size * TILE > count:
            break

        @pl.when((blocks > least) & (blocks <= size))
        def _(size=size):
            act(size * TILE)

        least = size


def split_pair(block):
    lane = lax.broadcasted_iota(jnp.int32, block.shape, 1)
    even = lane < HEAD
    zero = jnp.zeros_like(block)
    return jnp.concatenate([jnp.where(even, block, zero), jnp.where(even, zero, block)], axis=0)


def join_pair(both):
    rows = both.shape[0] // 2
    lane = lax.broadcasted_iota(jnp.int32, (rows, both.shape[1]), 1)
    return jnp.where(lane < HEAD, both[:rows], both[rows:])


def write_bias(bias_ref, lo_ref, hi_ref, row, first, span):
    place = lax.broadcasted_iota(jnp.int32, (TILE, span), 1) + first
    low = lo_ref[pl.ds(row, TILE), :]
    high = hi_ref[pl.ds(row, TILE), :]
    bias_ref[:, :span] = jnp.where((place >= low) & (place < high), 0.0, masked_score)


def pair_weights(q2, k, bias):
    span = k.shape[0]
    scores = mm(q2, k, NT)
    scores = (scores.reshape(2, TILE, span) + bias[None]).reshape(2 * TILE, span)
    top = jnp.max(scores, axis=1, keepdims=True)
    raised = jnp.exp(scores - top)
    total = jnp.sum(raised, axis=1, keepdims=True)
    return raised * (1.0 / total)


def forward_kernel(halo, tiles_ref, lo_ref, hi_ref, q_ref, k_ref, v_ref, out_ref, bias_ref):
    count = k_ref.shape[0]
    pairs = q_ref.shape[1] // TILE
    tiles = q_ref.shape[0] // TILE

    def tile_step(tile, carry):
        here = tile + halo // TILE
        blocks = tiles_ref[1, here]

        def act(span):
            first = jnp.minimum(tiles_ref[0, here], count - span)
            first = pl.multiple_of(first, ALIGN)
            row = pl.multiple_of(tile * TILE, TILE)
            write_bias(bias_ref, lo_ref, hi_ref, pl.multiple_of(row + halo, TILE), first, span)

            def pair_step(pair, inner):
                lanes = pl.ds(pl.multiple_of(pair * TILE, TILE), TILE)
                q2 = split_pair(q_ref[pl.ds(row, TILE), lanes])
                k = k_ref[pl.ds(first, span), lanes]
                v = v_ref[pl.ds(first, span), lanes]
                weights = pair_weights(q2, k, bias_ref[:, :span]).astype(bf16)
                out_ref[pl.ds(row, TILE), lanes] = join_pair(mm(weights, v)).astype(bf16)
                return inner

            lax.fori_loop(0, pairs, pair_step, 0, unroll=pairs)

        by_span(blocks, count, act)
        return carry

    lax.fori_loop(0, tiles, tile_step, 0)


def lasting(micros):
    return pl.CostEstimate(flops=int(micros * 1e9), bytes_accessed=int(micros * 3.5e6), transcendentals=0)


def lane_group(array, group, groups):
    return pl.BlockSpec((array.shape[0], array.shape[1] // groups), lambda i: (0, group))


def whole(array):
    return pl.BlockSpec(array.shape, lambda i: (0, 0))


def attend_forward(bounds, queries, keys, values, halo, group, groups):
    tiles, low, high = bounds
    rows, width = queries.shape
    arrays = (queries, keys, values)
    return pl.pallas_call(
        functools.partial(forward_kernel, halo),
        grid=(1,),
        out_shape=jax.ShapeDtypeStruct((rows, width // groups), bf16),
        in_specs=[pl.BlockSpec(memory_space=pltpu.SMEM), whole(low), whole(high)]
        + [lane_group(a, group, groups) for a in arrays],
        out_specs=pl.BlockSpec((rows, width // groups), lambda i: (0, 0)),
        scratch_shapes=[pltpu.VMEM((TILE, keys.shape[0]), f32)],
        compiler_params=pltpu.CompilerParams(vmem_limit_bytes=32 * 2**20),
        cost_estimate=lasting(18 / groups),
        name="attend_forward",
    )(tiles, low, high, *arrays)


def backward_kernel(
    halo, tiles_ref, lo_ref, hi_ref, q_ref, k_ref, v_ref, g_ref,
    dq_ref, dk_ref, dv_ref, bias_ref, dk_sum, dv_sum,
):
    count = k_ref.shape[0]
    own = dq_ref.shape[0]
    pairs = q_ref.shape[1] // TILE
    dk_sum[...] = jnp.zeros_like(dk_sum)
    dv_sum[...] = jnp.zeros_like(dv_sum)

    def tile_step(tile, carry):
        blocks = tiles_ref[2, tile]
        mine = (tile >= halo // TILE) & (tile < (halo + own) // TILE)

        def act(span):
            first = jnp.minimum(tiles_ref[0, tile], count - span)
            first = pl.multiple_of(first, ALIGN)
            row = pl.multiple_of(tile * TILE, TILE)
            write_bias(bias_ref, lo_ref, hi_ref, row, first, span)

            def pair_step(pair, inner):
                lanes = pl.ds(pl.multiple_of(pair * TILE, TILE), TILE)
                q2 = split_pair(q_ref[pl.ds(row, TILE), lanes])
                g2 = split_pair(g_ref[pl.ds(row, TILE), lanes])
                k = k_ref[pl.ds(first, span), lanes]
                v = v_ref[pl.ds(first, span), lanes]
                weights = pair_weights(q2, k, bias_ref[:, :span])
                slopes = mm(g2, v, NT)
                inner_sum = jnp.sum(weights * slopes, axis=1, keepdims=True)
                scores = (weights * (slopes - inner_sum)).astype(bf16)
                dv_sum[pl.ds(first, span), lanes] += mm(weights.astype(bf16), g2, TN)
                dk_sum[pl.ds(first, span), lanes] += mm(scores, q2, TN)

                @pl.when(mine)
                def _():
                    grad = join_pair(mm(scores, k)).astype(bf16)
                    to = pl.multiple_of(row - halo, TILE)
                    dq_ref[pl.ds(to, TILE), lanes] = grad * jnp.asarray(1.0 / math.sqrt(HEAD), bf16)

                return inner

            lax.fori_loop(0, pairs, pair_step, 0, unroll=pairs)

        by_span(blocks, count, act)
        return carry

    lax.fori_loop(0, count // TILE, tile_step, 0)
    dk_ref[...] = dk_sum[pl.ds(halo, own), :].astype(bf16)
    dv_ref[...] = dv_sum[pl.ds(halo, own), :].astype(bf16)


def attend_backward(bounds, queries, keys, values, grads, halo, group, groups):
    tiles, low, high = bounds
    count, width = keys.shape
    lanes = width // groups
    arrays = (queries, keys, values, grads)
    out = jax.ShapeDtypeStruct((count - 2 * halo, lanes), bf16)
    return pl.pallas_call(
        functools.partial(backward_kernel, halo),
        grid=(1,),
        out_shape=(out, out, out),
        in_specs=[pl.BlockSpec(memory_space=pltpu.SMEM), whole(low), whole(high)]
        + [lane_group(a, group, groups) for a in arrays],
        out_specs=(pl.BlockSpec(out.shape, lambda i: (0, 0)),) * 3,
        scratch_shapes=[
            pltpu.VMEM((TILE, count), f32),
            pltpu.VMEM((count, lanes), f32),
            pltpu.VMEM((count, lanes), f32),
        ],
        compiler_params=pltpu.CompilerParams(vmem_limit_bytes=32 * 2**20),
        cost_estimate=lasting(42 / groups),
        name="attend_backward",
    )(tiles, low, high, *arrays)


SMEM = pl.BlockSpec(memory_space=pltpu.SMEM)
VMEM = pl.BlockSpec(memory_space=pltpu.VMEM)
PLANE = 8


def local(kernel, place, arrays, outs, scratch, micros, name):
    return pl.pallas_call(
        kernel,
        out_shape=tuple(jax.ShapeDtypeStruct(shape, dtype) for shape, dtype in outs),
        in_specs=[SMEM] + [VMEM] * len(arrays),
        out_specs=(VMEM,) * len(outs),
        scratch_shapes=[pltpu.VMEM(shape, dtype) for shape, dtype in scratch],
        compiler_params=pltpu.CompilerParams(vmem_limit_bytes=48 * 2**20),
        cost_estimate=lasting(micros),
        name=name,
    )(place, *arrays)


def own_heads_kernel(place_ref, q_ref, k_ref, v_ref, out_ref, rows_ref):
    place = place_ref[0]
    eighths = q_ref.shape[0] // PLANE
    slabs = q_ref.shape[0] // 8
    for i, ref in enumerate((q_ref, k_ref, v_ref)):
        rows_ref[pl.ds(i * slabs, slabs)] = ref[...].astype(f32).reshape(slabs, 8, -1)
    heads = 3 * eighths // 8
    for j in range(PLANE):
        held = [rows_ref[h * PLANE + (place ^ j)] for h in range(heads)]
        out_ref[j] = jnp.concatenate(held, axis=0).astype(bf16)


def own_units_kernel(place_ref, o_ref, i_ref, b_ref, out_ref, in_ref, back_ref, rows_ref, units_ref):
    place = place_ref[0]
    rows = in_ref.shape[1]
    heads = out_ref.shape[1] // 8
    rows_ref[...] = o_ref[...].astype(f32).reshape(rows_ref.shape)
    units_ref[...] = i_ref[...].astype(f32).T.reshape(units_ref.shape)
    for j in range(PLANE):
        held = [rows_ref[h * PLANE + (place ^ j)] for h in range(heads)]
        out_ref[j] = jnp.concatenate(held, axis=0).astype(bf16)
        in_ref[j] = units_ref[place ^ j].astype(bf16)
        back_ref[j] = b_ref[pl.ds(pl.multiple_of((place ^ j) * rows, rows), rows), :]


def by_eighth(refs):
    first, second = [], []
    for j in range(PLANE):
        far, y, x = j // 4, j // 2 % 2, j % 2
        first.append(refs[4].at[y, x] if far else refs[y].at[x])
        second.append(refs[4].at[2 + x, y] if far else refs[2 + x].at[y])
    return first, second


def eighth_rows(halves, j, member, start, count):
    first, second = halves[0][j], halves[1][j]
    middle = first.shape[1]
    pieces = []
    if start < middle:
        pieces.append(first[member, pl.ds(start, min(count, middle - start)), :])
    if start + count > middle:
        at = max(start, middle)
        pieces.append(second[member, pl.ds(at - middle, start + count - at), :])
    return pieces


def stage_eighths(own_ref, halves, member, start, stage_ref):
    for j in range(PLANE):
        if own_ref is not None and member == 0:
            stage_ref[j] = own_ref[j].astype(f32)
            continue
        at = 0
        of = member if own_ref is None else member - 1
        for piece in eighth_rows(halves, j, of, start, stage_ref.shape[1]):
            stage_ref[j, pl.ds(at, piece.shape[0]), :] = piece.astype(f32)
            at += piece.shape[0]


def head_block(stage_ref, head):
    return jnp.concatenate([stage_ref[j, pl.ds(head * 8, 8), :] for j in range(PLANE)], axis=0)


def project_kernel(
    place_ref, left_ref, tokens_ref, right_ref, own_ref, *refs
):
    halves, refs = by_eighth(refs[:5]), refs[5:]
    bq_ref, bv_ref, q_ref, k_ref, v_ref, w_ref, x_ref, stage_ref = refs
    ways = halves[0][0].shape[0] + 1
    heads = own_ref.shape[1] // 24
    halo = left_ref.shape[0]
    own = tokens_ref.shape[0]
    width = tokens_ref.shape[1]
    inner = heads * HEAD
    x_ref[:halo] = left_ref[...]
    x_ref[pl.ds(halo, own)] = tokens_ref[...]
    x_ref[pl.ds(halo + own, halo)] = right_ref[...]
    for member in range(ways):
        stage_eighths(own_ref, halves, member, 0, stage_ref)
        for kind in range(3):
            blocks = [head_block(stage_ref, kind * heads + h) for h in range(heads)]
            at = kind * width + member * inner
            w_ref[pl.ds(at, inner)] = jnp.concatenate(blocks, axis=0).astype(bf16)

    def step(i, carry):
        rows = pl.ds(pl.multiple_of(i * 256, 256), 256)
        x = x_ref[rows, :]
        q = mm(x, w_ref[:width], NT) + bq_ref[...]
        q_ref[rows, :] = (q * (1.0 / math.sqrt(HEAD))).astype(bf16)
        k_ref[rows, :] = mm(x, w_ref[pl.ds(width, width)], NT).astype(bf16)
        v_ref[rows, :] = (mm(x, w_ref[pl.ds(2 * width, width)], NT) + bv_ref[...]).astype(bf16)
        return carry

    lax.fori_loop(0, x_ref.shape[0] // 256, step, 0)


def join_units(own_ref, halves, out_ref):
    rows = own_ref.shape[1]
    ways = halves[0][0].shape[0] + 1
    for j in range(PLANE):
        out_ref[pl.ds(j * ways * rows, rows), :] = own_ref[j]
        for member in range(1, ways):
            at = (j * ways + member) * rows
            for piece in eighth_rows(halves, j, member - 1, 0, rows):
                out_ref[pl.ds(at, piece.shape[0]), :] = piece
                at += piece.shape[0]


def join_units_kernel(place_ref, own_ref, *refs):
    join_units(own_ref, by_eighth(refs[:5]), refs[5])


def join_in_out_kernel(place_ref, own_ref, own_out_ref, *refs):
    halves = by_eighth(refs[:5])
    in_ref, out_ref, stage_ref = refs[5:]
    join_units(own_ref, halves, in_ref)
    heads = own_out_ref.shape[1] // 8
    for member in range(halves[0][0].shape[0] + 1):
        stage_eighths(own_out_ref, halves, member, own_ref.shape[1], stage_ref)
        for h in range(heads):
            block = head_block(stage_ref, h)
            out_ref[pl.ds((member * heads + h) * HEAD, HEAD), :] = block.astype(bf16)


def put_heads(ways, heads, sum_ref, kind, first_head, block):
    for i in range(block.shape[0] // HEAD):
        member, h = divmod(first_head + i, heads)
        for j in range(PLANE):
            part = block[i * HEAD + j * 8 : i * HEAD + j * 8 + 8]
            sum_ref[j * ways + member, pl.ds((kind * heads + h) * 8, 8), :] = part


def part_pieces(sum_ref, keep_ref, send_ref):
    half = keep_ref.shape[0]
    for i in range(half):
        keep_ref[i] = sum_ref[i].astype(bf16)
        send_ref[i] = sum_ref[half + i].astype(bf16)


def out_grads_kernel(ways, place_ref, left_ref, right_ref, first_ref, keep_ref, send_ref, sum_ref):
    width = first_ref.shape[1]
    heads = width // ways // HEAD
    sum_ref[:, heads * 8 :, :] = jnp.zeros((PLANE * ways, 8, width), f32)
    for g, ref in enumerate((left_ref, right_ref)):
        block = mm(ref[...], first_ref[...], TN)
        put_heads(ways, heads, sum_ref, 0, g * width // 2 // HEAD, block)
    part_pieces(sum_ref, keep_ref, send_ref)


def piece_grads_kernel(groups, place_ref, *refs):
    grad_refs = refs[: 3 * groups]
    tokens_ref, vectors_ref, keep_ref, send_ref, sum_ref = refs[3 * groups :]
    place = place_ref[0]
    ways = vectors_ref.shape[0]
    width = tokens_ref.shape[1]
    inner = width // ways
    heads = inner // HEAD
    lanes = width // groups
    for kind in range(3):
        for g in range(groups):
            block = mm(grad_refs[kind * groups + g][...], tokens_ref[...], TN)
            put_heads(ways, heads, sum_ref, kind, g * lanes // HEAD, block)
    lane = lax.broadcasted_iota(jnp.int32, (width, width), 0)
    to = lax.broadcasted_iota(jnp.int32, (width, width), 1)
    member = sum((lane >= i * inner).astype(jnp.int32) for i in range(1, ways))
    within = lane - member * inner
    spot = (within & ~(HEAD - 8)) | ((((within >> 3) & 7) ^ place) << 3)
    row = lax.broadcasted_iota(jnp.int32, (8, width), 0)
    column = lax.broadcasted_iota(jnp.int32, (8, width), 1)
    of = sum((column >= i * inner).astype(jnp.int32) for i in range(1, ways))
    ones = jnp.ones((8, tokens_ref.shape[0]), bf16)
    lines = jnp.zeros((8, width), f32)
    for kind, first in ((0, width - 2 * inner), (2, width - inner)):
        sums = [mm(ones, grad_refs[kind * groups + g][...]) for g in range(groups)]
        sums = jnp.where(of == row, jnp.concatenate(sums, axis=1), 0.0)
        chosen = jnp.where(spot + first == to, 1.0, 0.0).astype(bf16)
        lines = lines + mm(sums.astype(bf16), chosen)
    below = 3 * heads * 8
    for i in range(ways):
        block = vectors_ref[i] + jnp.where(row == 2, lines[i : i + 1], 0.0)
        for j in range(PLANE):
            sum_ref[j * ways + i, pl.ds(below, 8), :] = block
    part_pieces(sum_ref, keep_ref, send_ref)


def gather_heads(place, rows_ref, first, out_ref):
    held = []
    for h in range(out_ref.shape[0] // HEAD):
        for p in range(PLANE):
            held.append(rows_ref[place ^ p, pl.ds(first + h * 8, 8), :])
    out_ref[...] = jnp.concatenate(held, axis=0)


def finish_heads_kernel(place_ref, *refs):
    q_ref, k_ref, v_ref, rows_ref = refs[5:]
    stage_eighths(None, by_eighth(refs[:5]), 0, 0, rows_ref)
    for kind, ref in enumerate((q_ref, k_ref, v_ref)):
        gather_heads(place_ref[0], rows_ref, kind * ref.shape[0] // PLANE, ref)


def finish_units_kernel(place_ref, *refs):
    back_ref, in_ref, out_ref, rows_ref, turned_ref = refs[5:]
    place = place_ref[0]
    rows = back_ref.shape[0] // PLANE
    stage_eighths(None, by_eighth(refs[:5]), 0, 0, rows_ref)
    for p in range(PLANE):
        back_ref[pl.ds(p * rows, rows), :] = rows_ref[place ^ p, :rows, :]
        turned_ref[pl.ds(p * rows, rows), :] = rows_ref[place ^ p, pl.ds(rows, rows), :]
    in_ref[...] = turned_ref[...].T
    gather_heads(place, rows_ref, 2 * rows, out_ref)


def norm_parts(values):
    center = values - jnp.mean(values, axis=-1, keepdims=True)
    spread = jnp.mean(center * center, axis=-1, keepdims=True)
    return center, lax.rsqrt(spread + epsilon)


def norm_pull(grad, unit, inverse, gain):
    scaled = grad * gain
    mean = jnp.mean(scaled, axis=-1, keepdims=True)
    along = jnp.mean(scaled * unit, axis=-1, keepdims=True)
    return inverse * (scaled - mean - unit * along)


def gelu_both(before):
    half = 0.5 * (1.0 + lax.erf(before * math.sqrt(0.5)))
    bell = jnp.exp(-0.5 * before * before) * (1.0 / math.sqrt(2.0 * math.pi))
    return before * half, half + before * bell


def partner(values, step):
    ways = lax.axis_size("mp")
    return lax.ppermute(values, "mp", [(i, i ^ step) for i in range(ways)])


def halo_rows(values, halo):
    ways = lax.axis_size("mp")
    before = lax.ppermute(values[-halo:], "mp", [(i, i + 1) for i in range(ways - 1)])
    after = lax.ppermute(values[:halo], "mp", [(i + 1, i) for i in range(ways - 1)])
    return before, after


def group_tables(table):
    ways = lax.axis_size("mp")
    data_ways = lax.axis_size("dp")
    total = table
    for step in range(1, ways):
        total = total + partner(table, step)
    held = total[None]
    data_index = lax.axis_index("dp")
    level = 1
    while level < data_ways:
        other = lax.ppermute(held, "dp", [(i, i ^ level) for i in range(data_ways)])
        first = (data_index & level) == 0
        held = jnp.where(
            first, jnp.concatenate([held, other]), jnp.concatenate([other, held])
        )
        level *= 2
    return held


CORE, NEAR_X, NEAR_Y = 1, 2, 4


def swap(values, bit):
    ways = lax.axis_size("dp")
    return lax.ppermute(values, "dp", [(i, i ^ bit) for i in range(ways)])


def along(piece):
    return [partner(piece, step) for step in range(1, lax.axis_size("mp"))]


def bit_step(held, level):
    order = sorted(held)
    other = partner(jnp.stack([held[i] for i in order]), level)
    return held | {i | level: other[at] for at, i in enumerate(order)}


def others_of(held):
    return jnp.stack([held[i] for i in sorted(held)[1:]])


def first_step(values):
    middle = values.shape[1] // 2
    first, second = values[:, :middle], values[:, middle:]
    return [jnp.stack([first, swap(first, NEAR_X)]), jnp.stack([second, swap(second, NEAR_Y)])]


def second_step(pairs):
    first, second = pairs
    return [first, swap(first, NEAR_Y), second, swap(second, NEAR_X)]


def core_step(held):
    return [*held, swap(jnp.stack(held), CORE)]


def after(value, *others):
    return lax.optimization_barrier((value, others))[0]


def add(first, second):
    return (first.astype(f32) + second.astype(f32)).astype(bf16)


def first_sum_step(sums):
    half = sums.shape[2] // 2
    first, second = sums[:, :, :half], sums[:, :, half:]
    return [(first[0], swap(first[1], NEAR_Y)), (second[:, 0], swap(second[:, 1], NEAR_X))]


def second_sum_step(halves):
    first, second = (add(*half) for half in halves)
    return [(first[0], swap(first[1], NEAR_X)), (second[0], swap(second[1], NEAR_Y))]


def over_groups(total):
    level = PLANE
    while level < lax.axis_size("dp"):
        total = total + swap(total, level)
        level *= 2
    return total


def sum_along(parts):
    total = parts[0].astype(f32)
    for step in range(1, len(parts)):
        total = total + partner(parts[step], step).astype(f32)
    return over_groups(total)


def shards(
    tokens, grad_out, pass_len, labels, w_query, w_key, w_value, b_query, b_value, w_out, b_out,
    ln1_gain, ln1_shift, w_in, b_in, w_back, b_back, ln2_gain, ln2_shift,
):
    ways = lax.axis_size("mp")
    data_ways = lax.axis_size("dp")
    mp_index = lax.axis_index("mp")
    data_index = lax.axis_index("dp")
    own_rows, width = tokens.shape
    rows_here = pass_len.shape[0]
    inner = w_query.shape[1]
    units = w_in.shape[1]
    halo = ROW_LEN // 4
    count = own_rows + 2 * halo
    scale = 1.0 / math.sqrt(HEAD)
    temper = 2.0 / math.sqrt(width)

    piece_rows = units // PLANE
    heads = inner // HEAD
    part = inner // PLANE
    place = ((data_index & CORE) << 2 | (data_index % PLANE) >> 1).reshape(1)
    (qkv_own,) = local(
        own_heads_kernel, place, (w_query.T, w_key.T, w_value.T), [((PLANE, 3 * part, width), bf16)],
        [((3 * heads * PLANE, 8, width), f32)], 4, "own_heads",
    )
    biases = jnp.concatenate([b_in, b_query, b_value])
    digits, rest = [], biases
    for _ in range(3):
        digits.append(lax.reduce_precision(rest, 8, 7))
        rest = rest - digits[-1]
    digits = jnp.stack(digits)
    lines = jnp.concatenate(
        [digits[:, :units], jnp.pad(digits[:, units:], ((0, 0), (0, width - 2 * inner)))]
    )
    lines = jnp.pad(lines, ((0, 2), (0, 0))).astype(bf16)
    qkv_along = along(jnp.concatenate([qkv_own[0], lines]))
    tokens_before, tokens_after = halo_rows(tokens, halo)
    w_out, w_in, w_back, place = lax.optimization_barrier((w_out, w_in, w_back, place, qkv_own))[:4]
    out_own, in_own, back_own = local(
        own_units_kernel, place, (w_out, w_in, w_back),
        [((PLANE, part, width), bf16), ((PLANE, piece_rows, width), bf16), ((PLANE, piece_rows, width), bf16)],
        [((heads * PLANE, 8, width), f32), ((PLANE, piece_rows, width), f32)], 5, "own_units",
    )
    in_piece = jnp.concatenate([in_own[0], out_own[0], jnp.zeros((8, width), bf16)])
    back_piece = back_own[0]
    in_piece, back_piece = after((in_piece, back_piece), qkv_along)
    qkv_along = jnp.stack(qkv_along)
    qkv_pairs = first_step(qkv_along)
    in_held = {0: in_piece}
    level = ways // 2
    while level > 1:
        in_held = bit_step(in_held, level)
        level //= 2
    qkv_held = second_step(after(qkv_pairs, in_held))
    in_along = others_of(bit_step(in_held, 1))
    qkv_parts = core_step(after(qkv_held, in_along))
    back_held = bit_step({0: after(back_piece, in_along, qkv_held)}, ways // 2)
    in_along = after(in_along, qkv_parts)
    in_pairs = first_step(in_along)
    bias_rest = after(qkv_along, qkv_parts)[:, 3 * part :].astype(f32)
    bias_in_rest = bias_rest[:, 0] + bias_rest[:, 1] + bias_rest[:, 2]
    bias_head_rest = bias_rest[:, 3] + bias_rest[:, 4] + bias_rest[:, 5]
    bias_in_all = jnp.concatenate([b_in[None], bias_in_rest])
    bias_heads = jnp.concatenate(
        [jnp.concatenate([b_query, b_value])[None], bias_head_rest[:, : 2 * inner]]
    )

    def in_order(parts):
        split = parts.reshape(*parts.shape[:-2], 2, 2, 2, parts.shape[-1])
        for axis, bit in ((-4, CORE), (-3, NEAR_Y), (-2, NEAR_X)):
            split = jnp.where((data_index & bit) != 0, jnp.flip(split, axis), split)
        return split.reshape(parts.shape)

    bias_heads = in_order(bias_heads.reshape(ways, 2 * heads, PLANE, 8)).reshape(ways, 2, inner)
    bias_query = bias_heads[:, 0].reshape(1, width)
    bias_value = bias_heads[:, 1].reshape(1, width)
    bias_in = in_order(bias_in_all.reshape(ways, PLANE, piece_rows))
    bias_in = bias_in.transpose(1, 0, 2).reshape(-1)

    low, high = segment_bounds(pass_len, mp_index * own_rows - halo, count)
    tile_low = low[::TILE] // ALIGN * ALIGN
    tile_high = high[TILE - 1 :: TILE]
    blocks = (tile_high - tile_low + TILE - 1) // TILE
    tile = jnp.arange(count // TILE, dtype=jnp.int32)
    before_own = tile < halo // TILE
    after_own = tile >= (halo + own_rows) // TILE
    reach = (~before_own | (tile_high > halo)) & (~after_own | (low[::TILE] < halo + own_rows))
    tiles = jnp.stack([tile_low, blocks, jnp.where(reach, blocks, 0)])
    bounds = (tiles, low[:, None], high[:, None])

    tokens_before = after(tokens_before, in_along)
    qkv = (tokens_before, tokens, tokens_after, qkv_own, *qkv_parts, bias_query, bias_value)
    queries, keys, values, qkv_all = local(
        project_kernel, place, qkv, [((count, width), bf16)] * 3 + [((3 * width, width), bf16)],
        [((count, width), bf16), ((PLANE, 3 * part, width), f32)], 10, "project",
    )
    own_queries = queries[halo : halo + own_rows]
    back_held = after(back_held, queries)
    level = ways // 4
    while level:
        back_held = bit_step(back_held, level)
        level //= 2
    back_along = others_of(back_held)
    own_queries = after(own_queries, in_pairs)
    context = [attend_forward(bounds, own_queries, keys, values, halo, 0, 2)]
    in_held = second_step(in_pairs)
    back_along = after(back_along, in_held, context[0])
    back_pairs = first_step(back_along)
    own_queries = after(own_queries, in_held, context[0])
    in_parts = core_step(in_held)
    context.append(attend_forward(bounds, own_queries, keys, values, halo, 1, 2))
    in_own = after(in_own, back_pairs, context[1])
    in_all, out_all = local(
        join_in_out_kernel, place, (in_own, out_own, *in_parts),
        [((ways * units, width), bf16), ((width, width), bf16)],
        [((PLANE, part, width), f32)], 5, "join_in_out",
    )
    back_held = second_step(back_pairs)
    back_parts = core_step(back_held)
    (back_all,) = local(
        join_units_kernel, place, (back_own, *back_parts),
        [((ways * units, width), bf16)], [], 4, "join_back",
    )
    attended = mm(context[0], out_all[: width // 2]) + mm(context[1], out_all[width // 2 :])
    first_sum = tokens.astype(f32) + attended + b_out
    center_one, inverse_one = norm_parts(first_sum)
    unit_one = center_one * inverse_one
    hidden = unit_one * ln1_gain + ln1_shift
    hidden_low = after(hidden.astype(bf16), back_held)

    active, slope = gelu_both(mm(hidden_low, in_all, NT) + bias_in)
    active, slope = lax.optimization_barrier((active.astype(bf16), slope.astype(bf16)))
    second_sum = hidden + mm(active, back_all) + b_back
    center_two, inverse_two = norm_parts(second_sum)
    unit_two = center_two * inverse_two
    mixed = (unit_two * ln2_gain + ln2_shift).astype(bf16)

    query_count = PAIRS * rows_here
    places = cls_places(pass_len) + (jnp.arange(rows_here, dtype=jnp.int32) * ROW_LEN)[:, None]
    table_places = jnp.concatenate([places[:, :PAIRS].reshape(-1), places[:, PAIRS:].reshape(-1)])
    table_places = table_places - mp_index * own_rows
    picker = table_places[:, None] == jnp.arange(own_rows, dtype=jnp.int32)[None, :]
    table = mm(picker.astype(bf16), mixed).astype(bf16)
    digits = jnp.concatenate([labels // 32, labels % 32]).astype(bf16)
    digits = jnp.where(mp_index == 0, digits, 0)
    extra = jnp.zeros((8, width), bf16).at[0, : 2 * query_count].set(digits)
    tables = group_tables(jnp.concatenate([table, extra]))
    all_count = data_ways * query_count
    query_cls = tables[:, :query_count].reshape(all_count, width)
    passage_cls = tables[:, query_count : 2 * query_count].reshape(all_count, width)
    digits = tables[:, 2 * query_count, : 2 * query_count].astype(jnp.int32)
    all_labels = (digits[:, :query_count] * 32 + digits[:, query_count:]).reshape(-1)

    logits = mm(query_cls, passage_cls, NT) * temper
    targets = all_labels[:, None] == jnp.arange(all_count, dtype=jnp.int32)[None, :]
    top = jnp.max(logits, axis=1, keepdims=True)
    raised = jnp.exp(logits - top)
    total = jnp.sum(raised, axis=1, keepdims=True)
    losses = top[:, 0] + jnp.log(total[:, 0]) - jnp.sum(jnp.where(targets, logits, 0.0), axis=1)
    query_losses = lax.dynamic_slice_in_dim(losses, data_index * query_count, query_count)
    grad_logits = (raised / total - targets.astype(f32)) * temper
    rows_of = lax.dynamic_slice_in_dim(grad_logits, data_index * query_count, query_count, 0)
    columns_of = lax.dynamic_slice_in_dim(grad_logits, data_index * query_count, query_count, 1)
    grad_cls = jnp.concatenate(
        [
            jnp.dot(rows_of, passage_cls.astype(f32), precision=highest),
            jnp.dot(columns_of.T, query_cls.astype(f32), precision=highest),
        ]
    )
    grad_mixed = grad_out.astype(f32) + jnp.dot(
        picker.astype(f32).T, grad_cls, precision=highest
    )

    grad_second = norm_pull(grad_mixed, unit_two, inverse_two, ln2_gain)
    stats = [
        jnp.sum(grad_mixed * unit_two, axis=0),
        jnp.sum(grad_mixed, axis=0),
        jnp.sum(grad_second, axis=0),
    ]
    second_low = grad_second.astype(bf16)

    def to_core(left, right):
        return mm(left[:, left.shape[1] // 2 :], right, TN).astype(bf16)

    def chip_sum(left, right, arrived):
        own = mm(left[:, : left.shape[1] // 2], right, TN)
        return add(own, arrived).reshape(2, 2, ways, piece_rows, width)

    back_sent = to_core(active, second_low)
    back_arrived = swap(back_sent, CORE)
    pulled, back_sent = lax.optimization_barrier((second_low, back_sent))
    grad_before = (mm(pulled, back_all, NT) * slope.astype(f32)).astype(bf16)
    back_sum = chip_sum(active, second_low, back_arrived)
    back_half = swap(back_sum[1], NEAR_Y)
    in_sent = to_core(grad_before, hidden_low)
    in_arrived = swap(in_sent, CORE)
    pulled = after(grad_before, in_sent, back_sum)
    grad_hidden = grad_second + mm(pulled, in_all)
    grad_first = norm_pull(grad_hidden, unit_one, inverse_one, ln1_gain)
    stats += [
        jnp.sum(grad_hidden * unit_one, axis=0),
        jnp.sum(grad_hidden, axis=0),
        jnp.sum(grad_first, axis=0),
    ]
    first_low = grad_first.astype(bf16)
    first_before, first_after = halo_rows(first_low, halo)
    out_keep, out_sent = local(
        functools.partial(out_grads_kernel, ways), place, (*context, first_low),
        [((4 * ways, part + 8, width), bf16)] * 2, [((8 * ways, part + 8, width), f32)], 3, "out_grads",
    )
    out_arrived = swap(out_sent, CORE)
    in_sum = chip_sum(after(grad_before, out_sent), hidden_low, in_arrived)
    out_sum = add(out_keep, out_arrived).reshape(2, 2, ways, part + 8, width)
    in_sum = jnp.concatenate([in_sum, out_sum], axis=3)
    in_half = swap(in_sum[:, 1], NEAR_X)
    d_b_in = jnp.sum(grad_before, axis=0, dtype=f32).reshape(PLANE, ways, piece_rows)

    d_b_in = in_order(d_b_in.transpose(1, 0, 2)).reshape(ways, 1, units)
    turned = jnp.stack(stats).reshape(6, ways, inner).transpose(1, 0, 2)
    level = 1
    while level < ways:
        split = turned.reshape(-1, 2, level, *turned.shape[1:])
        flipped = jnp.where((mp_index & level) != 0, jnp.flip(split, 1), split)
        turned = flipped.reshape(turned.shape)
        level *= 2
    turned = jnp.pad(turned.reshape(ways, -1), ((0, 0), (0, 2 * inner))).reshape(ways, 2, width)
    vectors = jnp.concatenate([d_b_in, turned, jnp.zeros((ways, 5, width), f32)], axis=1)

    first_window = jnp.concatenate([first_before, first_low, first_after])
    grad_context = mm(first_window, out_all, NT).astype(bf16)
    groups = 3
    parts = []

    def attend(grads, group):
        return attend_backward(bounds, queries, keys, values, grads, halo, group, groups)

    grad_context = after(grad_context, in_sum, back_sum, vectors)
    parts.append(attend(grad_context, 0))
    grad_context = after(grad_context, parts[0])
    parts.append(attend(grad_context, 1))
    back_half, in_half = after((back_half, in_half), parts[1])
    back_sum = add(back_sum[0], back_half)
    in_sum = add(in_sum[:, 0], in_half)
    back_half = swap(back_sum[1], NEAR_X)
    in_half = swap(in_sum[1], NEAR_Y)
    grad_context = after(grad_context, back_sum, in_sum, parts[1])
    parts.append(attend(grad_context, 2))
    back_half, in_half = after((back_half, in_half), parts[2])
    early_sum = jnp.concatenate([add(back_sum[0], back_half), add(in_sum[0], in_half)], axis=1)
    early_parts = [early_sum[i] for i in range(ways)]
    early_odd = partner(jnp.stack(early_parts[1::2]), 1)
    tokens_low = after(tokens, early_parts)

    grad_parts = [g[i] for i in range(3) for g in parts]
    late_rows = 3 * part + 8
    late_keep, late_sent = local(
        functools.partial(piece_grads_kernel, groups), place, (*grad_parts, tokens_low, vectors),
        [((4 * ways, late_rows, width), bf16)] * 2, [((8 * ways, late_rows, width), f32)], 8, "piece_grads",
    )
    late_sum = add(late_keep, swap(late_sent, CORE)).reshape(2, 2, ways, late_rows, width)
    halves = first_sum_step(late_sum)
    early_odd = after(early_odd, halves)
    early_parts = [add(even, odd) for even, odd in zip(early_parts[::2], early_odd)]
    halves = second_sum_step(halves)
    late_parts = [half[i] for half in (add(*h) for h in halves) for i in range(ways // 2)]
    level, early_own = 2, early_parts[0].astype(f32)
    while level < ways:
        early_own = early_own + after(partner(early_parts[level // 2], level), late_parts).astype(f32)
        level *= 2
    early_own = over_groups(early_own).astype(bf16)
    early_held = second_step(first_step(after(early_own, late_parts)[None]))
    late_total = sum_along(late_parts)
    late_held = second_step(first_step(late_total.astype(bf16)[None]))
    late_pieces = core_step(late_held)
    early_pieces = core_step(early_held)
    line = late_total[3 * part :]
    grad_queries, grad_keys, grad_values = (jnp.concatenate(p, axis=1) for p in zip(*parts))
    d_tokens = (
        grad_first
        + mm(grad_queries, qkv_all[:width])
        + mm(grad_keys, qkv_all[width : 2 * width])
        + mm(grad_values, qkv_all[2 * width :])
    )

    d_query, d_key, d_value = local(
        finish_heads_kernel, place, late_pieces, [((inner, width), f32)] * 3,
        [((PLANE, 3 * part, width), f32)], 4, "finish_heads",
    )
    d_back, d_in, d_out = local(
        finish_units_kernel, place, early_pieces,
        [((units, width), f32), ((width, units), f32), ((inner, width), f32)],
        [((PLANE, 2 * piece_rows + part + 8, width), f32), ((units, width), f32)], 6, "finish_units",
    )
    norms = [line[1 + i // ways, i % ways * inner : (i % ways + 1) * inner] for i in range(8)]
    return (
        mixed,
        query_losses,
        d_tokens,
        d_query.T,
        d_key.T,
        d_value.T,
        norms[6],
        norms[7],
        d_out,
        norms[5],
        norms[3],
        norms[4],
        d_in,
        line[0],
        d_back,
        norms[2],
        norms[0],
        norms[1],
    )


def solution(mesh):
    return jax.shard_map(
        shards,
        mesh=mesh,
        in_specs=(
            P(("dp", "mp"), None), P(("dp", "mp"), None), P("dp", None), P("dp"),
            P(None, "mp"), P(None, "mp"), P(None, "mp"), P("mp"), P("mp"), P("mp", None), P(),
            P(), P(), P(None, "mp"), P("mp"), P("mp", None), P(), P(), P(),
        ),
        out_specs=(
            P(("dp", "mp"), None), P("dp"), P(("dp", "mp"), None),
            P(None, "mp"), P(None, "mp"), P(None, "mp"), P("mp"), P("mp"), P("mp", None),
            P("mp"), P("mp"), P("mp"), P(None, "mp"), P("mp"), P("mp", None), P("mp"), P("mp"), P("mp"),
        ),
        check_vma=False,
    )
```

```python
import functools
import math

import jax
import jax.numpy as jnp
from jax import lax
from jax.experimental import pallas as pl
from jax.experimental.pallas import tpu as pltpu
from jax.sharding import PartitionSpec as P

HEAD = 64
ROW_LEN = 1024
PAIRS = 4
QLEN = 32
TILE = 128
ALIGN = 32
BLOCKS = (2, 3, 4, 5, 7, 10)

epsilon = 1e-12
masked_score = -1e30
highest = lax.Precision.HIGHEST
f32 = jnp.float32
bf16 = jnp.bfloat16
NT = (((1,), (1,)), ((), ()))
TN = (((0,), (0,)), ((), ()))
NN = (((1,), (0,)), ((), ()))


def mm(a, b, dims=NN):
    return lax.dot_general(a, b, dims, preferred_element_type=f32)


def bounds_kernel(halo, own, start_ref, pass_ref, tiles_ref, low_ref, high_ref):
    start = start_ref[0]
    count = low_ref.shape[0]
    rows = pass_ref.shape[0]
    last = rows * ROW_LEN
    cuts = []
    for row in range(rows):
        cuts += [jnp.int32(row * ROW_LEN + j * QLEN) for j in range(PAIRS + 1)]
        for j in range(PAIRS):
            cuts.append(cuts[-1] + pass_ref[row, j])

    def low_of(place):
        low = jnp.full_like(place, start)
        for cut in cuts:
            low = jnp.where(cut <= place, cut, low)
        return jnp.clip(jnp.where(place >= last, last, low) - start, 0, count)

    def high_of(place):
        high = jnp.full_like(place, last)
        for cut in reversed(cuts):
            high = jnp.where(cut > place, cut, high)
        return jnp.clip(jnp.where(place >= last, start + count, high) - start, 0, count)

    place = start + lax.broadcasted_iota(jnp.int32, (count, 1), 0)
    low_ref[...] = low_of(place)
    high_ref[...] = high_of(place)
    for tile in range(count // TILE):
        first = low_of(start + tile * TILE)
        after_last = high_of(start + tile * TILE + TILE - 1)
        low = first // ALIGN * ALIGN
        blocks = (after_last - low + TILE - 1) // TILE
        tiles_ref[0, tile] = low
        tiles_ref[1, tile] = blocks
        if tile * TILE < halo:
            blocks = jnp.where(after_last > halo, blocks, 0)
        if tile * TILE >= halo + own:
            blocks = jnp.where(first < halo + own, blocks, 0)
        tiles_ref[2, tile] = blocks


def segment_bounds(pass_len, start, halo, own):
    count = own + 2 * halo
    smem = pl.BlockSpec(memory_space=pltpu.SMEM)
    vmem = pl.BlockSpec(memory_space=pltpu.VMEM)
    column = jax.ShapeDtypeStruct((count, 1), jnp.int32)
    return pl.pallas_call(
        functools.partial(bounds_kernel, halo, own),
        out_shape=(jax.ShapeDtypeStruct((3, count // TILE), jnp.int32), column, column),
        in_specs=[smem, smem],
        out_specs=(smem, vmem, vmem),
        compiler_params=pltpu.CompilerParams(vmem_limit_bytes=8 * 2**20),
        name="bounds",
    )(start.reshape(1), pass_len)


def cls_places(pass_len):
    lens = [pass_len[:, j] for j in range(PAIRS)]
    starts = [jnp.full_like(lens[0], j * QLEN) for j in range(PAIRS)]
    at = jnp.full_like(lens[0], PAIRS * QLEN)
    for j in range(PAIRS):
        starts.append(at)
        at = at + lens[j]
    return jnp.stack(starts, axis=1)


def by_span(blocks, count, act):
    least = 0
    for size in BLOCKS:
        if size * TILE > count:
            break

        @pl.when((blocks > least) & (blocks <= size))
        def _(size=size):
            act(size * TILE)

        least = size


def split_pair(block):
    lane = lax.broadcasted_iota(jnp.int32, block.shape, 1)
    even = lane < HEAD
    zero = jnp.zeros_like(block)
    return jnp.concatenate([jnp.where(even, block, zero), jnp.where(even, zero, block)], axis=0)


def join_pair(both):
    rows = both.shape[0] // 2
    lane = lax.broadcasted_iota(jnp.int32, (rows, both.shape[1]), 1)
    return jnp.where(lane < HEAD, both[:rows], both[rows:])


def write_bias(bias_ref, lo_ref, hi_ref, row, first, span):
    place = lax.broadcasted_iota(jnp.int32, (TILE, span), 1) + first
    low = lo_ref[pl.ds(row, TILE), :]
    high = hi_ref[pl.ds(row, TILE), :]
    bias_ref[:, :span] = jnp.where((place >= low) & (place < high), 0.0, masked_score)


def pair_weights(q2, k, bias):
    span = k.shape[0]
    scores = mm(q2, k, NT)
    scores = (scores.reshape(2, TILE, span) + bias[None]).reshape(2 * TILE, span)
    top = jnp.max(scores, axis=1, keepdims=True)
    raised = jnp.exp(scores - top)
    total = jnp.sum(raised, axis=1, keepdims=True)
    return raised * (1.0 / total)


def forward_kernel(halo, tiles_ref, lo_ref, hi_ref, q_ref, k_ref, v_ref, out_ref, bias_ref):
    count = k_ref.shape[0]
    pairs = q_ref.shape[1] // TILE
    tiles = q_ref.shape[0] // TILE

    def tile_step(tile, carry):
        here = tile + halo // TILE
        blocks = tiles_ref[1, here]

        def act(span):
            first = jnp.minimum(tiles_ref[0, here], count - span)
            first = pl.multiple_of(first, ALIGN)
            row = pl.multiple_of(tile * TILE, TILE)
            write_bias(bias_ref, lo_ref, hi_ref, pl.multiple_of(row + halo, TILE), first, span)

            def pair_step(pair, inner):
                lanes = pl.ds(pl.multiple_of(pair * TILE, TILE), TILE)
                q2 = split_pair(q_ref[pl.ds(row, TILE), lanes])
                k = k_ref[pl.ds(first, span), lanes]
                v = v_ref[pl.ds(first, span), lanes]
                weights = pair_weights(q2, k, bias_ref[:, :span]).astype(bf16)
                out_ref[pl.ds(row, TILE), lanes] = join_pair(mm(weights, v)).astype(bf16)
                return inner

            lax.fori_loop(0, pairs, pair_step, 0, unroll=pairs)

        by_span(blocks, count, act)
        return carry

    lax.fori_loop(0, tiles, tile_step, 0)


def lasting(micros):
    return pl.CostEstimate(flops=int(micros * 2e7), bytes_accessed=int(micros * 7e4), transcendentals=0)


def lane_group(array, group, groups):
    return pl.BlockSpec((array.shape[0], array.shape[1] // groups), lambda i: (0, group))


def whole(array):
    return pl.BlockSpec(array.shape, lambda i: (0, 0))


def attend_forward(bounds, queries, keys, values, halo, group, groups):
    tiles, low, high = bounds
    rows, width = queries.shape
    arrays = (queries, keys, values)
    return pl.pallas_call(
        functools.partial(forward_kernel, halo),
        grid=(1,),
        out_shape=jax.ShapeDtypeStruct((rows, width // groups), bf16),
        in_specs=[pl.BlockSpec(memory_space=pltpu.SMEM), whole(low), whole(high)]
        + [lane_group(a, group, groups) for a in arrays],
        out_specs=pl.BlockSpec((rows, width // groups), lambda i: (0, 0)),
        scratch_shapes=[pltpu.VMEM((TILE, keys.shape[0]), f32)],
        compiler_params=pltpu.CompilerParams(vmem_limit_bytes=14 * 2**20),
        cost_estimate=lasting(18 / groups),
        name="attend_forward",
    )(tiles, low, high, *arrays)


def backward_kernel(
    halo, tiles_ref, lo_ref, hi_ref, q_ref, k_ref, v_ref, g_ref,
    dq_ref, dk_ref, dv_ref, bias_ref, dk_sum, dv_sum,
):
    count = k_ref.shape[0]
    own = dq_ref.shape[0]
    pairs = q_ref.shape[1] // TILE
    dk_sum[...] = jnp.zeros_like(dk_sum)
    dv_sum[...] = jnp.zeros_like(dv_sum)

    def tile_step(tile, carry):
        blocks = tiles_ref[2, tile]
        mine = (tile >= halo // TILE) & (tile < (halo + own) // TILE)

        def act(span):
            first = jnp.minimum(tiles_ref[0, tile], count - span)
            first = pl.multiple_of(first, ALIGN)
            row = pl.multiple_of(tile * TILE, TILE)
            write_bias(bias_ref, lo_ref, hi_ref, row, first, span)

            def pair_step(pair, inner):
                lanes = pl.ds(pl.multiple_of(pair * TILE, TILE), TILE)
                q2 = split_pair(q_ref[pl.ds(row, TILE), lanes])
                g2 = split_pair(g_ref[pl.ds(row, TILE), lanes])
                k = k_ref[pl.ds(first, span), lanes]
                v = v_ref[pl.ds(first, span), lanes]
                weights = pair_weights(q2, k, bias_ref[:, :span])
                slopes = mm(g2, v, NT)
                inner_sum = jnp.sum(weights * slopes, axis=1, keepdims=True)
                scores = (weights * (slopes - inner_sum)).astype(bf16)
                dv_sum[pl.ds(first, span), lanes] += mm(weights.astype(bf16), g2, TN)
                dk_sum[pl.ds(first, span), lanes] += mm(scores, q2, TN)

                @pl.when(mine)
                def _():
                    grad = join_pair(mm(scores, k)).astype(bf16)
                    to = pl.multiple_of(row - halo, TILE)
                    dq_ref[pl.ds(to, TILE), lanes] = grad * jnp.asarray(1.0 / math.sqrt(HEAD), bf16)

                return inner

            lax.fori_loop(0, pairs, pair_step, 0, unroll=pairs)

        by_span(blocks, count, act)
        return carry

    lax.fori_loop(0, count // TILE, tile_step, 0)
    dk_ref[...] = dk_sum[pl.ds(halo, own), :].astype(bf16)
    dv_ref[...] = dv_sum[pl.ds(halo, own), :].astype(bf16)


def attend_backward(bounds, queries, keys, values, grads, halo, group, groups):
    tiles, low, high = bounds
    count, width = keys.shape
    lanes = width // groups
    arrays = (queries, keys, values, grads)
    out = jax.ShapeDtypeStruct((count - 2 * halo, lanes), bf16)
    return pl.pallas_call(
        functools.partial(backward_kernel, halo),
        grid=(1,),
        out_shape=(out, out, out),
        in_specs=[pl.BlockSpec(memory_space=pltpu.SMEM), whole(low), whole(high)]
        + [lane_group(a, group, groups) for a in arrays],
        out_specs=(pl.BlockSpec(out.shape, lambda i: (0, 0)),) * 3,
        scratch_shapes=[
            pltpu.VMEM((TILE, count), f32),
            pltpu.VMEM((count, lanes), f32),
            pltpu.VMEM((count, lanes), f32),
        ],
        compiler_params=pltpu.CompilerParams(vmem_limit_bytes=20 * 2**20),
        cost_estimate=lasting(42 / groups),
        name="attend_backward",
    )(tiles, low, high, *arrays)


SMEM = pl.BlockSpec(memory_space=pltpu.SMEM)
VMEM = pl.BlockSpec(memory_space=pltpu.VMEM)
PLANE = 8


def local(kernel, place, arrays, outs, scratch, micros, name, mib=20):
    return pl.pallas_call(
        kernel,
        out_shape=tuple(jax.ShapeDtypeStruct(shape, dtype) for shape, dtype in outs),
        in_specs=[SMEM] + [VMEM] * len(arrays),
        out_specs=(VMEM,) * len(outs),
        scratch_shapes=[pltpu.VMEM(shape, dtype) for shape, dtype in scratch],
        compiler_params=pltpu.CompilerParams(vmem_limit_bytes=mib * 2**20),
        cost_estimate=lasting(micros),
        name=name,
    )(place, *arrays)


def own_heads_kernel(place_ref, q_ref, k_ref, v_ref, out_ref, rows_ref):
    place = place_ref[0]
    eighths = q_ref.shape[0] // PLANE
    slabs = q_ref.shape[0] // 8
    for i, ref in enumerate((q_ref, k_ref, v_ref)):
        rows_ref[pl.ds(i * slabs, slabs)] = ref[...].astype(f32).reshape(slabs, 8, -1)
    heads = 3 * eighths // 8
    for j in range(PLANE):
        held = [rows_ref[h * PLANE + (place ^ j)] for h in range(heads)]
        out_ref[j] = jnp.concatenate(held, axis=0).astype(bf16)


def own_units_kernel(place_ref, o_ref, i_ref, b_ref, out_ref, in_ref, back_ref, rows_ref, units_ref):
    place = place_ref[0]
    rows = in_ref.shape[1]
    heads = out_ref.shape[1] // 8
    rows_ref[...] = o_ref[...].astype(f32).reshape(rows_ref.shape)
    units_ref[...] = i_ref[...].astype(f32).T.reshape(units_ref.shape)
    for j in range(PLANE):
        held = [rows_ref[h * PLANE + (place ^ j)] for h in range(heads)]
        out_ref[j] = jnp.concatenate(held, axis=0).astype(bf16)
        in_ref[j] = units_ref[place ^ j].astype(bf16)
        back_ref[j] = b_ref[pl.ds(pl.multiple_of((place ^ j) * rows, rows), rows), :]


def by_eighth(refs):
    first, second = [], []
    for j in range(PLANE):
        far, y, x = j // 4, j // 2 % 2, j % 2
        first.append(refs[4].at[y, x] if far else refs[y].at[x])
        second.append(refs[4].at[2 + x, y] if far else refs[2 + x].at[y])
    return first, second


def eighth_rows(halves, j, member, start, count):
    first, second = halves[0][j], halves[1][j]
    middle = first.shape[1]
    pieces = []
    if start < middle:
        pieces.append(first[member, pl.ds(start, min(count, middle - start)), :])
    if start + count > middle:
        at = max(start, middle)
        pieces.append(second[member, pl.ds(at - middle, start + count - at), :])
    return pieces


def stage_eighths(own_ref, halves, member, start, stage_ref):
    for j in range(PLANE):
        if own_ref is not None and member == 0:
            stage_ref[j] = own_ref[j].astype(f32)
            continue
        at = 0
        of = member if own_ref is None else member - 1
        for piece in eighth_rows(halves, j, of, start, stage_ref.shape[1]):
            stage_ref[j, pl.ds(at, piece.shape[0]), :] = piece.astype(f32)
            at += piece.shape[0]


def head_block(stage_ref, head):
    return jnp.concatenate([stage_ref[j, pl.ds(head * 8, 8), :] for j in range(PLANE)], axis=0)


def project_kernel(
    place_ref, left_ref, tokens_ref, right_ref, own_ref, *refs
):
    halves, refs = by_eighth(refs[:5]), refs[5:]
    bias_ref, q_ref, k_ref, v_ref, w_ref, x_ref, stage_ref = refs
    ways = halves[0][0].shape[0] + 1
    heads = own_ref.shape[1] // 24
    halo = left_ref.shape[0]
    own = tokens_ref.shape[0]
    width = tokens_ref.shape[1]
    inner = heads * HEAD
    x_ref[:halo] = left_ref[...]
    x_ref[pl.ds(halo, own)] = tokens_ref[...]
    x_ref[pl.ds(halo + own, halo)] = right_ref[...]
    for member in range(ways):
        stage_eighths(own_ref, halves, member, 0, stage_ref)
        for kind in range(3):
            blocks = [head_block(stage_ref, kind * heads + h) for h in range(heads)]
            at = kind * width + member * inner
            w_ref[pl.ds(at, inner)] = jnp.concatenate(blocks, axis=0).astype(bf16)

    def step(i, carry):
        rows = pl.ds(pl.multiple_of(i * 256, 256), 256)
        x = x_ref[rows, :]
        q = mm(x, w_ref[:width], NT) + bias_ref[0:1]
        q_ref[rows, :] = (q * (1.0 / math.sqrt(HEAD))).astype(bf16)
        k_ref[rows, :] = mm(x, w_ref[pl.ds(width, width)], NT).astype(bf16)
        v_ref[rows, :] = (mm(x, w_ref[pl.ds(2 * width, width)], NT) + bias_ref[1:2]).astype(bf16)
        return carry

    lax.fori_loop(0, x_ref.shape[0] // 256, step, 0)


def join_units(own_ref, halves, out_ref):
    rows = own_ref.shape[1]
    ways = halves[0][0].shape[0] + 1
    for j in range(PLANE):
        out_ref[pl.ds(j * ways * rows, rows), :] = own_ref[j]
        for member in range(1, ways):
            at = (j * ways + member) * rows
            for piece in eighth_rows(halves, j, member - 1, 0, rows):
                out_ref[pl.ds(at, piece.shape[0]), :] = piece
                at += piece.shape[0]


def join_units_kernel(place_ref, own_ref, *refs):
    join_units(own_ref, by_eighth(refs[:5]), refs[5])


def join_in_out_kernel(place_ref, own_ref, own_out_ref, *refs):
    halves = by_eighth(refs[:5])
    in_ref, out_ref, stage_ref = refs[5:]
    join_units(own_ref, halves, in_ref)
    heads = own_out_ref.shape[1] // 8
    for member in range(halves[0][0].shape[0] + 1):
        stage_eighths(own_out_ref, halves, member, own_ref.shape[1], stage_ref)
        for h in range(heads):
            block = head_block(stage_ref, h)
            out_ref[pl.ds((member * heads + h) * HEAD, HEAD), :] = block.astype(bf16)


def split_digits(values):
    digits = []
    for _ in range(3):
        digits.append(values.astype(bf16))
        values = values - digits[-1].astype(f32)
    return digits


def biases_kernel(place_ref, along_ref, in_ref, q_ref, v_ref, heads_ref, units_ref, line_ref):
    place = place_ref[0]
    ways = along_ref.shape[0] + 1
    inner = q_ref.shape[1]
    rows = in_ref.shape[1] // PLANE
    first = along_ref.shape[1] - 8
    others = along_ref[:, first:, :].astype(f32)
    digits = split_digits(jnp.concatenate([q_ref[...], v_ref[...]], axis=1))
    digits = [digit.astype(f32) for digit in digits]
    for member in range(ways - 1):
        digits.append(others[member, 3:6, : 2 * inner])
    digits = jnp.concatenate(digits, axis=0).astype(bf16)
    lane = lax.broadcasted_iota(jnp.int32, (2 * inner, 2 * inner), 0)
    to = lax.broadcasted_iota(jnp.int32, (2 * inner, 2 * inner), 1)
    chosen = jnp.where((lane ^ (place << 3)) == to, 1.0, 0.0).astype(bf16)
    moved = mm(digits, chosen)
    sums = [moved[3 * m : 3 * m + 1] + moved[3 * m + 1 : 3 * m + 2] + moved[3 * m + 2 : 3 * m + 3] for m in range(ways)]
    heads_ref[0:1] = jnp.concatenate([value[:, :inner] for value in sums], axis=1)
    heads_ref[1:2] = jnp.concatenate([value[:, inner:] for value in sums], axis=1)
    for member in range(ways):
        if member == 0:
            value = in_ref[...]
        else:
            three = others[member - 1]
            value = three[0:1] + three[1:2] + three[2:3]
        for p in range(PLANE):
            line_ref[member * PLANE + p, 0:1, :rows] = value[:, p * rows : (p + 1) * rows]
    held = [
        line_ref[member * PLANE + (place ^ j), 0:1, :rows] for j in range(PLANE) for member in range(ways)
    ]
    units_ref[...] = jnp.concatenate(held, axis=1)


def vectors_kernel(place_ref, *refs):
    stat_refs, (units_ref, out_ref, line_ref) = refs[:6], refs[6:]
    place, own = place_ref[0], place_ref[1]
    ways, _, width = out_ref.shape
    inner = width // ways
    rows = units_ref.shape[1] // PLANE // ways
    for j in range(PLANE):
        for member in range(ways):
            at = j * ways + member
            line_ref[at, 0:1, :rows] = units_ref[:, at * rows : (at + 1) * rows]
    stats = jnp.concatenate([ref[...] for ref in stat_refs], axis=0)
    parts = [stats[:, i * inner : (i + 1) * inner] for i in range(ways)]
    for member in range(ways):
        held = [line_ref[(place ^ p) * ways + member, 0:1, :rows] for p in range(PLANE)]
        mine = parts[0]
        for i in range(1, ways):
            mine = jnp.where((own ^ member) == i, parts[i], mine)
        norms = jnp.concatenate([mine[i : i + 1] for i in range(6)], axis=1)
        norms = jnp.concatenate([norms, jnp.zeros((1, 2 * inner), f32)], axis=1)
        lines = [jnp.concatenate(held, axis=1), norms[:, :width], norms[:, width:]]
        out_ref[member] = jnp.concatenate([*lines, jnp.zeros((5, width), f32)], axis=0)


def put_heads(ways, heads, sum_ref, kind, first_head, block):
    for i in range(block.shape[0] // HEAD):
        member, h = divmod(first_head + i, heads)
        for j in range(PLANE):
            part = block[i * HEAD + j * 8 : i * HEAD + j * 8 + 8]
            sum_ref[j * ways + member, pl.ds((kind * heads + h) * 8, 8), :] = part


def part_pieces(sum_ref, keep_ref, send_ref):
    half = keep_ref.shape[0]
    for i in range(half):
        keep_ref[i] = sum_ref[i].astype(bf16)
        send_ref[i] = sum_ref[half + i].astype(bf16)


def out_grads_kernel(ways, place_ref, left_ref, right_ref, first_ref, keep_ref, send_ref, sum_ref):
    width = first_ref.shape[1]
    heads = width // ways // HEAD
    sum_ref[:, heads * 8 :, :] = jnp.zeros((PLANE * ways, 8, width), f32)
    for g, ref in enumerate((left_ref, right_ref)):
        block = mm(ref[...], first_ref[...], TN)
        put_heads(ways, heads, sum_ref, 0, g * width // 2 // HEAD, block)
    part_pieces(sum_ref, keep_ref, send_ref)


def piece_grads_kernel(groups, place_ref, *refs):
    grad_refs = refs[: 3 * groups]
    tokens_ref, vectors_ref, keep_ref, send_ref, sum_ref = refs[3 * groups :]
    place = place_ref[0]
    ways = vectors_ref.shape[0]
    width = tokens_ref.shape[1]
    inner = width // ways
    heads = inner // HEAD
    lanes = width // groups
    for kind in range(3):
        for g in range(groups):
            block = mm(grad_refs[kind * groups + g][...], tokens_ref[...], TN)
            put_heads(ways, heads, sum_ref, kind, g * lanes // HEAD, block)
    lane = lax.broadcasted_iota(jnp.int32, (width, width), 0)
    to = lax.broadcasted_iota(jnp.int32, (width, width), 1)
    member = sum((lane >= i * inner).astype(jnp.int32) for i in range(1, ways))
    within = lane - member * inner
    spot = within ^ (place << 3)
    row = lax.broadcasted_iota(jnp.int32, (8, width), 0)
    column = lax.broadcasted_iota(jnp.int32, (8, width), 1)
    of = sum((column >= i * inner).astype(jnp.int32) for i in range(1, ways))
    ones = jnp.ones((8, tokens_ref.shape[0]), bf16)
    lines = jnp.zeros((8, width), f32)
    for kind, first in ((0, width - 2 * inner), (2, width - inner)):
        sums = [mm(ones, grad_refs[kind * groups + g][...]) for g in range(groups)]
        sums = jnp.where(of == row, jnp.concatenate(sums, axis=1), 0.0)
        chosen = jnp.where(spot + first == to, 1.0, 0.0).astype(bf16)
        lines = lines + mm(sums.astype(bf16), chosen)
    below = 3 * heads * 8
    for i in range(ways):
        block = vectors_ref[i] + jnp.where(row == 2, lines[i : i + 1], 0.0)
        for j in range(PLANE):
            sum_ref[j * ways + i, pl.ds(below, 8), :] = block
    part_pieces(sum_ref, keep_ref, send_ref)


def gather_heads(place, rows_ref, first, out_ref):
    held = []
    for h in range(out_ref.shape[0] // HEAD):
        for p in range(PLANE):
            held.append(rows_ref[place ^ p, pl.ds(first + h * 8, 8), :])
    out_ref[...] = jnp.concatenate(held, axis=0)


def finish_heads_kernel(place_ref, *refs):
    q_ref, k_ref, v_ref, rows_ref = refs[5:]
    stage_eighths(None, by_eighth(refs[:5]), 0, 0, rows_ref)
    for kind, ref in enumerate((q_ref, k_ref, v_ref)):
        gather_heads(place_ref[0], rows_ref, kind * ref.shape[0] // PLANE, ref)


def finish_units_kernel(place_ref, *refs):
    back_ref, in_ref, out_ref, rows_ref, turned_ref = refs[5:]
    place = place_ref[0]
    rows = back_ref.shape[0] // PLANE
    stage_eighths(None, by_eighth(refs[:5]), 0, 0, rows_ref)
    for p in range(PLANE):
        back_ref[pl.ds(p * rows, rows), :] = rows_ref[place ^ p, :rows, :]
        turned_ref[pl.ds(p * rows, rows), :] = rows_ref[place ^ p, pl.ds(rows, rows), :]
    in_ref[...] = turned_ref[...].T
    gather_heads(place, rows_ref, 2 * rows, out_ref)


def norm_parts(values):
    center = values - jnp.mean(values, axis=-1, keepdims=True)
    spread = jnp.mean(center * center, axis=-1, keepdims=True)
    return center, lax.rsqrt(spread + epsilon)


def norm_pull(grad, unit, inverse, gain):
    scaled = grad * gain
    mean = jnp.mean(scaled, axis=-1, keepdims=True)
    along = jnp.mean(scaled * unit, axis=-1, keepdims=True)
    return inverse * (scaled - mean - unit * along)


def gelu_both(before):
    half = 0.5 * (1.0 + lax.erf(before * math.sqrt(0.5)))
    bell = jnp.exp(-0.5 * before * before) * (1.0 / math.sqrt(2.0 * math.pi))
    return before * half, half + before * bell


def partner(values, step):
    ways = lax.axis_size("mp")
    return lax.ppermute(values, "mp", [(i, i ^ step) for i in range(ways)])


def halo_rows(values, halo):
    ways = lax.axis_size("mp")
    before = lax.ppermute(values[-halo:], "mp", [(i, i + 1) for i in range(ways - 1)])
    after = lax.ppermute(values[:halo], "mp", [(i + 1, i) for i in range(ways - 1)])
    return before, after


def group_tables(table):
    ways = lax.axis_size("mp")
    data_ways = lax.axis_size("dp")
    total = table
    for step in range(1, ways):
        total = total + partner(table, step)
    held = total[None]
    data_index = lax.axis_index("dp")
    level = 1
    while level < data_ways:
        other = lax.ppermute(held, "dp", [(i, i ^ level) for i in range(data_ways)])
        first = (data_index & level) == 0
        held = jnp.where(
            first, jnp.concatenate([held, other]), jnp.concatenate([other, held])
        )
        level *= 2
    return held


CORE, NEAR_X, NEAR_Y = 1, 2, 4


def swap(values, bit):
    ways = lax.axis_size("dp")
    return lax.ppermute(values, "dp", [(i, i ^ bit) for i in range(ways)])


def along(piece):
    return [partner(piece, step) for step in range(1, lax.axis_size("mp"))]


def bit_step(held, level):
    order = sorted(held)
    other = partner(jnp.stack([held[i] for i in order]), level)
    return held | {i | level: other[at] for at, i in enumerate(order)}


def others_of(held):
    return jnp.stack([held[i] for i in sorted(held)[1:]])


def first_step(values):
    middle = values.shape[1] // 2
    first, second = values[:, :middle], values[:, middle:]
    return [jnp.stack([first, swap(first, NEAR_X)]), jnp.stack([second, swap(second, NEAR_Y)])]


def second_step(pairs):
    first, second = pairs
    return [first, swap(first, NEAR_Y), second, swap(second, NEAR_X)]


def core_step(held):
    return [*held, swap(jnp.stack(held), CORE)]


def after(value, *others):
    return lax.optimization_barrier((value, others))[0]


def add(first, second):
    return (first.astype(f32) + second.astype(f32)).astype(bf16)


def first_sum_step(sums):
    half = sums.shape[2] // 2
    first, second = sums[:, :, :half], sums[:, :, half:]
    return [(first[0], swap(first[1], NEAR_Y)), (second[:, 0], swap(second[:, 1], NEAR_X))]


def second_sum_step(halves):
    first, second = (add(*half) for half in halves)
    return [(first[0], swap(first[1], NEAR_X)), (second[0], swap(second[1], NEAR_Y))]


def over_groups(total):
    level = PLANE
    while level < lax.axis_size("dp"):
        total = total + swap(total, level)
        level *= 2
    return total


def sum_along(parts):
    total = parts[0].astype(f32)
    for step in range(1, len(parts)):
        total = total + partner(parts[step], step).astype(f32)
    return over_groups(total)


def shards(
    tokens, grad_out, pass_len, labels, w_query, w_key, w_value, b_query, b_value, w_out, b_out,
    ln1_gain, ln1_shift, w_in, b_in, w_back, b_back, ln2_gain, ln2_shift,
):
    ways = lax.axis_size("mp")
    data_ways = lax.axis_size("dp")
    mp_index = lax.axis_index("mp")
    data_index = lax.axis_index("dp")
    own_rows, width = tokens.shape
    rows_here = pass_len.shape[0]
    inner = w_query.shape[1]
    units = w_in.shape[1]
    halo = ROW_LEN // 4
    count = own_rows + 2 * halo
    scale = 1.0 / math.sqrt(HEAD)
    temper = 2.0 / math.sqrt(width)

    piece_rows = units // PLANE
    heads = inner // HEAD
    part = inner // PLANE
    place = jnp.stack([(data_index & CORE) << 2 | (data_index % PLANE) >> 1, mp_index])
    (qkv_own,) = local(
        own_heads_kernel, place, (w_query.T, w_key.T, w_value.T), [((PLANE, 3 * part, width), bf16)],
        [((3 * heads * PLANE, 8, width), f32)], 4, "own_heads",
    )
    biases = jnp.concatenate([b_in, b_query, b_value])
    digits, rest = [], biases
    for _ in range(3):
        digits.append(lax.reduce_precision(rest, 8, 7))
        rest = rest - digits[-1]
    digits = jnp.stack(digits)
    lines = jnp.concatenate(
        [digits[:, :units], jnp.pad(digits[:, units:], ((0, 0), (0, width - 2 * inner)))]
    )
    lines = jnp.pad(lines, ((0, 2), (0, 0))).astype(bf16)
    qkv_along = along(jnp.concatenate([qkv_own[0], lines]))
    tokens_before, tokens_after = halo_rows(tokens, halo)
    w_out, w_in, w_back, place = lax.optimization_barrier((w_out, w_in, w_back, place, qkv_own))[:4]
    out_own, in_own, back_own = local(
        own_units_kernel, place, (w_out, w_in, w_back),
        [((PLANE, part, width), bf16), ((PLANE, piece_rows, width), bf16), ((PLANE, piece_rows, width), bf16)],
        [((heads * PLANE, 8, width), f32), ((PLANE, piece_rows, width), f32)], 5, "own_units",
    )
    in_piece = jnp.concatenate([in_own[0], out_own[0], jnp.zeros((8, width), bf16)])
    back_piece = back_own[0]
    in_piece, back_piece = after((in_piece, back_piece), qkv_along)
    qkv_along = jnp.stack(qkv_along)
    qkv_pairs = first_step(qkv_along)
    in_held = {0: in_piece}
    level = ways // 2
    while level > 1:
        in_held = bit_step(in_held, level)
        level //= 2
    qkv_held = second_step(after(qkv_pairs, in_held, tokens_before, tokens_after))
    in_along = others_of(bit_step(in_held, 1))
    qkv_parts = core_step(after(qkv_held, in_along))
    back_held = bit_step({0: after(back_piece, in_along, qkv_held)}, ways // 2)
    in_along = after(in_along, qkv_parts)
    in_pairs = first_step(in_along)
    bias_heads, bias_in = local(
        biases_kernel, place,
        (after(qkv_along, qkv_held), b_in[None], b_query[None], b_value[None]),
        [((2, width), f32), ((1, ways * units), f32)], [((ways * PLANE, 8, 128), f32)], 2, "biases",
    )

    bounds = segment_bounds(pass_len, mp_index * own_rows - halo, halo, own_rows)

    tokens_before = after(tokens_before, in_along)
    qkv = (tokens_before, tokens, tokens_after, qkv_own, *qkv_parts, bias_heads)
    queries, keys, values, qkv_all = local(
        project_kernel, place, qkv, [((count, width), bf16)] * 3 + [((3 * width, width), bf16)],
        [((count, width), bf16), ((PLANE, 3 * part, width), f32)], 10, "project", 32,
    )
    own_queries = queries[halo : halo + own_rows]
    back_held = after(back_held, queries)
    level = ways // 4
    while level:
        back_held = bit_step(back_held, level)
        level //= 2
    back_along = others_of(back_held)
    own_queries = after(own_queries, in_pairs)
    context = [attend_forward(bounds, own_queries, keys, values, halo, 0, 2)]
    in_held = after(second_step(in_pairs), context[0])
    back_along = after(back_along, in_held)
    back_pairs = first_step(back_along)
    own_queries = after(own_queries, in_held, context[0])
    in_parts = core_step(in_held)
    context.append(attend_forward(bounds, own_queries, keys, values, halo, 1, 2))
    in_own = after(in_own, back_pairs, context[1])
    in_all, out_all = local(
        join_in_out_kernel, place, (in_own, out_own, *in_parts),
        [((ways * units, width), bf16), ((width, width), bf16)],
        [((PLANE, part, width), f32)], 5, "join_in_out",
    )
    back_held = second_step(back_pairs)
    back_parts = core_step(back_held)
    (back_all,) = local(
        join_units_kernel, place, (back_own, *back_parts),
        [((ways * units, width), bf16)], [], 4, "join_back",
    )
    attended = mm(context[0], out_all[: width // 2]) + mm(context[1], out_all[width // 2 :])
    first_sum = tokens.astype(f32) + attended + b_out
    center_one, inverse_one = norm_parts(first_sum)
    unit_one = center_one * inverse_one
    hidden = unit_one * ln1_gain + ln1_shift
    hidden_low = after(hidden.astype(bf16), back_held)

    active, slope = gelu_both(mm(hidden_low, in_all, NT) + bias_in)
    active, slope = lax.optimization_barrier((active.astype(bf16), slope.astype(bf16)))
    second_sum = hidden + mm(active, back_all) + b_back
    center_two, inverse_two = norm_parts(second_sum)
    unit_two = center_two * inverse_two
    mixed = (unit_two * ln2_gain + ln2_shift).astype(bf16)

    query_count = PAIRS * rows_here
    places = cls_places(pass_len) + (jnp.arange(rows_here, dtype=jnp.int32) * ROW_LEN)[:, None]
    table_places = jnp.concatenate([places[:, :PAIRS].reshape(-1), places[:, PAIRS:].reshape(-1)])
    table_places = table_places - mp_index * own_rows
    picker = table_places[:, None] == jnp.arange(own_rows, dtype=jnp.int32)[None, :]
    table = mm(picker.astype(bf16), mixed).astype(bf16)
    digits = jnp.concatenate([labels // 32, labels % 32]).astype(bf16)
    digits = jnp.where(mp_index == 0, digits, 0)
    extra = jnp.zeros((8, width), bf16).at[0, : 2 * query_count].set(digits)
    tables = group_tables(jnp.concatenate([table, extra]))
    all_count = data_ways * query_count
    query_cls = tables[:, :query_count].reshape(all_count, width)
    passage_cls = tables[:, query_count : 2 * query_count].reshape(all_count, width)
    digits = tables[:, 2 * query_count, : 2 * query_count].astype(jnp.int32)
    all_labels = (digits[:, :query_count] * 32 + digits[:, query_count:]).reshape(-1)

    logits = mm(query_cls, passage_cls, NT) * temper
    targets = all_labels[:, None] == jnp.arange(all_count, dtype=jnp.int32)[None, :]
    top = jnp.max(logits, axis=1, keepdims=True)
    raised = jnp.exp(logits - top)
    total = jnp.sum(raised, axis=1, keepdims=True)
    losses = top[:, 0] + jnp.log(total[:, 0]) - jnp.sum(jnp.where(targets, logits, 0.0), axis=1)
    query_losses = lax.dynamic_slice_in_dim(losses, data_index * query_count, query_count)
    grad_logits = (raised / total - targets.astype(f32)) * temper
    rows_of = lax.dynamic_slice_in_dim(grad_logits, data_index * query_count, query_count, 0)
    columns_of = lax.dynamic_slice_in_dim(grad_logits, data_index * query_count, query_count, 1)
    grad_cls = jnp.concatenate(
        [
            jnp.dot(rows_of, passage_cls.astype(f32), precision=highest),
            jnp.dot(columns_of.T, query_cls.astype(f32), precision=highest),
        ]
    )
    grad_mixed = grad_out.astype(f32) + jnp.dot(
        picker.astype(f32).T, grad_cls, precision=highest
    )

    grad_second = norm_pull(grad_mixed, unit_two, inverse_two, ln2_gain)
    stats = [
        jnp.sum(grad_mixed * unit_two, axis=0, keepdims=True),
        jnp.sum(grad_mixed, axis=0, keepdims=True),
        jnp.sum(grad_second, axis=0, keepdims=True),
    ]
    second_low = grad_second.astype(bf16)

    def to_core(left, right):
        return mm(left[:, left.shape[1] // 2 :], right, TN).astype(bf16)

    def chip_sum(left, right, arrived):
        own = mm(left[:, : left.shape[1] // 2], right, TN)
        return add(own, arrived).reshape(2, 2, ways, piece_rows, width)

    back_sent = to_core(active, second_low)
    back_arrived = swap(back_sent, CORE)
    pulled, back_sent = lax.optimization_barrier((second_low, back_sent))
    grad_before = (mm(pulled, back_all, NT) * slope.astype(f32)).astype(bf16)
    back_sum = chip_sum(active, second_low, back_arrived)
    back_half = swap(back_sum[1], NEAR_Y)
    in_sent = to_core(grad_before, hidden_low)
    in_arrived = swap(in_sent, CORE)
    in_sum = chip_sum(grad_before, hidden_low, in_arrived)
    in_half = swap(in_sum[:, 1], NEAR_X)
    pulled = after(grad_before, back_sum, in_sum)
    grad_hidden = grad_second + mm(pulled, in_all)
    grad_first = norm_pull(grad_hidden, unit_one, inverse_one, ln1_gain)
    stats += [
        jnp.sum(grad_hidden * unit_one, axis=0, keepdims=True),
        jnp.sum(grad_hidden, axis=0, keepdims=True),
        jnp.sum(grad_first, axis=0, keepdims=True),
    ]
    first_low = grad_first.astype(bf16)
    first_before, first_after = halo_rows(first_low, halo)
    out_keep, out_sent = local(
        functools.partial(out_grads_kernel, ways), place, (*context, first_low),
        [((4 * ways, part + 8, width), bf16)] * 2, [((8 * ways, part + 8, width), f32)], 3, "out_grads",
    )
    out_sum = add(out_keep, swap(out_sent, CORE)).reshape(2, 2, ways, part + 8, width)
    out_half = swap(out_sum[1], NEAR_Y)

    d_b_in = jnp.sum(grad_before, axis=0, dtype=f32, keepdims=True)
    (vectors,) = local(
        vectors_kernel, place, (*stats, d_b_in), [((ways, 8, width), f32)],
        [((ways * PLANE, 8, 128), f32)], 2, "vectors",
    )

    first_window = jnp.concatenate([first_before, first_low, first_after])
    grad_context = mm(first_window, out_all, NT).astype(bf16)
    groups = 3
    parts = []

    def attend(grads, group):
        return attend_backward(bounds, queries, keys, values, grads, halo, group, groups)

    grad_context = after(grad_context, in_sum, back_sum, out_sum, vectors)
    parts.append(attend(grad_context, 0))
    back_half, in_half, out_half = after((back_half, in_half, out_half), parts[0])
    back_sum = add(back_sum[0], back_half)
    in_sum = add(in_sum[:, 0], in_half)
    out_sum = add(out_sum[0], out_half)
    back_half = swap(back_sum[1], NEAR_X)
    in_half = swap(in_sum[1], NEAR_Y)
    out_half = swap(out_sum[1], NEAR_X)
    grad_context = after(grad_context, back_sum, in_sum, out_sum, parts[0])
    parts.append(attend(grad_context, 1))
    halves = [(back_sum[0], back_half), (in_sum[0], in_half), (out_sum[0], out_half)]
    halves = after(halves, parts[1])
    early_sum = jnp.concatenate([add(*half) for half in halves], axis=1)
    early_parts = [early_sum[i] for i in range(ways)]
    early_odd = jnp.stack(early_parts[1::2])
    grad_context, early_odd = lax.optimization_barrier((grad_context, early_odd))
    early_odd = partner(early_odd, 1)
    parts.append(attend(grad_context, 2))
    early_odd = after(early_odd, parts[2])
    early_parts = [add(even, odd) for even, odd in zip(early_parts[::2], early_odd)]
    tokens_low = after(tokens, early_parts)

    grad_parts = [g[i] for i in range(3) for g in parts]
    late_rows = 3 * part + 8
    late_keep, late_sent = local(
        functools.partial(piece_grads_kernel, groups), place, (*grad_parts, tokens_low, vectors),
        [((4 * ways, late_rows, width), bf16)] * 2, [((8 * ways, late_rows, width), f32)], 8, "piece_grads", 36,
    )
    late_sum = add(late_keep, swap(late_sent, CORE)).reshape(2, 2, ways, late_rows, width)
    level, early_own = 2, early_parts[0].astype(f32)
    while level < ways:
        early_own = early_own + after(partner(early_parts[level // 2], level), late_keep).astype(f32)
        level *= 2
    early_held = first_step(over_groups(early_own).astype(bf16)[None])
    halves = first_sum_step(late_sum)
    early_held = second_step(after(early_held, late_sum))
    halves = second_sum_step(halves)
    late_parts = [half[i] for half in (add(*h) for h in halves) for i in range(ways // 2)]
    early_pieces = core_step(after(early_held, late_parts))
    late_total = sum_along(late_parts)
    late_pieces = core_step(second_step(first_step(late_total.astype(bf16)[None])))
    line = late_total[3 * part :]
    grad_queries, grad_keys, grad_values = (jnp.concatenate(p, axis=1) for p in zip(*parts))
    d_tokens = (
        grad_first
        + mm(grad_queries, qkv_all[:width])
        + mm(grad_keys, qkv_all[width : 2 * width])
        + mm(grad_values, qkv_all[2 * width :])
    )

    d_query, d_key, d_value = local(
        finish_heads_kernel, place, late_pieces, [((inner, width), f32)] * 3,
        [((PLANE, 3 * part, width), f32)], 4, "finish_heads",
    )
    d_back, d_in, d_out = local(
        finish_units_kernel, place, early_pieces,
        [((units, width), f32), ((width, units), f32), ((inner, width), f32)],
        [((PLANE, 2 * piece_rows + part + 8, width), f32), ((units, width), f32)], 6, "finish_units",
    )
    norms = [line[1 + i // ways, i % ways * inner : (i % ways + 1) * inner] for i in range(8)]
    return (
        mixed,
        query_losses,
        d_tokens,
        d_query.T,
        d_key.T,
        d_value.T,
        norms[6],
        norms[7],
        d_out,
        norms[5],
        norms[3],
        norms[4],
        d_in,
        line[0],
        d_back,
        norms[2],
        norms[0],
        norms[1],
    )


def solution(mesh):
    return jax.shard_map(
        shards,
        mesh=mesh,
        in_specs=(
            P(("dp", "mp"), None), P(("dp", "mp"), None), P("dp", None), P("dp"),
            P(None, "mp"), P(None, "mp"), P(None, "mp"), P("mp"), P("mp"), P("mp", None), P(),
            P(), P(), P(None, "mp"), P("mp"), P("mp", None), P(), P(), P(),
        ),
        out_specs=(
            P(("dp", "mp"), None), P("dp"), P(("dp", "mp"), None),
            P(None, "mp"), P(None, "mp"), P(None, "mp"), P("mp"), P("mp"), P("mp", None),
            P("mp"), P("mp"), P("mp"), P(None, "mp"), P("mp"), P("mp", None), P("mp"), P("mp"), P("mp"),
        ),
        check_vma=False,
    )
```

```python
import functools
import math

import jax
import jax.numpy as jnp
from jax import lax
from jax.experimental import pallas as pl
from jax.experimental.pallas import tpu as pltpu
from jax.sharding import PartitionSpec as P

HEAD = 64
ROW_LEN = 1024
PAIRS = 4
QLEN = 32
TILE = 128
ALIGN = 32
BLOCKS = (2, 3, 4, 5, 7, 10)

epsilon = 1e-12
masked_score = -1e30
highest = lax.Precision.HIGHEST
f32 = jnp.float32
bf16 = jnp.bfloat16
NT = (((1,), (1,)), ((), ()))
TN = (((0,), (0,)), ((), ()))
NN = (((1,), (0,)), ((), ()))


def mm(a, b, dims=NN):
    return lax.dot_general(a, b, dims, preferred_element_type=f32)


def bounds_kernel(halo, own, start_ref, pass_ref, tiles_ref, low_ref, high_ref):
    start = start_ref[0]
    count = low_ref.shape[0]
    rows = pass_ref.shape[0]
    last = rows * ROW_LEN
    cuts = []
    for row in range(rows):
        cuts += [jnp.int32(row * ROW_LEN + j * QLEN) for j in range(PAIRS + 1)]
        for j in range(PAIRS):
            cuts.append(cuts[-1] + pass_ref[row, j])

    def low_of(place):
        low = jnp.full_like(place, start)
        for cut in cuts:
            low = jnp.where(cut <= place, cut, low)
        return jnp.clip(jnp.where(place >= last, last, low) - start, 0, count)

    def high_of(place):
        high = jnp.full_like(place, last)
        for cut in reversed(cuts):
            high = jnp.where(cut > place, cut, high)
        return jnp.clip(jnp.where(place >= last, start + count, high) - start, 0, count)

    place = start + lax.broadcasted_iota(jnp.int32, (count, 1), 0)
    low_ref[...] = low_of(place)
    high_ref[...] = high_of(place)
    for tile in range(count // TILE):
        first = low_of(start + tile * TILE)
        after_last = high_of(start + tile * TILE + TILE - 1)
        low = first // ALIGN * ALIGN
        blocks = (after_last - low + TILE - 1) // TILE
        tiles_ref[0, tile] = low
        tiles_ref[1, tile] = blocks
        if tile * TILE < halo:
            blocks = jnp.where(after_last > halo, blocks, 0)
        if tile * TILE >= halo + own:
            blocks = jnp.where(first < halo + own, blocks, 0)
        tiles_ref[2, tile] = blocks


def segment_bounds(pass_len, start, halo, own):
    count = own + 2 * halo
    smem = pl.BlockSpec(memory_space=pltpu.SMEM)
    vmem = pl.BlockSpec(memory_space=pltpu.VMEM)
    column = jax.ShapeDtypeStruct((count, 1), jnp.int32)
    return pl.pallas_call(
        functools.partial(bounds_kernel, halo, own),
        out_shape=(jax.ShapeDtypeStruct((3, count // TILE), jnp.int32), column, column),
        in_specs=[smem, smem],
        out_specs=(smem, vmem, vmem),
        compiler_params=pltpu.CompilerParams(vmem_limit_bytes=8 * 2**20),
        name="bounds",
    )(start.reshape(1), pass_len)


def cls_places(pass_len):
    lens = [pass_len[:, j] for j in range(PAIRS)]
    starts = [jnp.full_like(lens[0], j * QLEN) for j in range(PAIRS)]
    at = jnp.full_like(lens[0], PAIRS * QLEN)
    for j in range(PAIRS):
        starts.append(at)
        at = at + lens[j]
    return jnp.stack(starts, axis=1)


def by_span(blocks, count, act):
    least = 0
    for size in BLOCKS:
        if size * TILE > count:
            break

        @pl.when((blocks > least) & (blocks <= size))
        def _(size=size):
            act(size * TILE)

        least = size


def split_pair(block):
    lane = lax.broadcasted_iota(jnp.int32, block.shape, 1)
    even = lane < HEAD
    zero = jnp.zeros_like(block)
    return jnp.concatenate([jnp.where(even, block, zero), jnp.where(even, zero, block)], axis=0)


def join_pair(both):
    rows = both.shape[0] // 2
    lane = lax.broadcasted_iota(jnp.int32, (rows, both.shape[1]), 1)
    return jnp.where(lane < HEAD, both[:rows], both[rows:])


def write_bias(bias_ref, lo_ref, hi_ref, row, first, span):
    place = lax.broadcasted_iota(jnp.int32, (TILE, span), 1) + first
    low = lo_ref[pl.ds(row, TILE), :]
    high = hi_ref[pl.ds(row, TILE), :]
    bias_ref[:, :span] = jnp.where((place >= low) & (place < high), 0.0, masked_score)


def pair_weights(q2, k, bias):
    span = k.shape[0]
    scores = mm(q2, k, NT)
    scores = (scores.reshape(2, TILE, span) + bias[None]).reshape(2 * TILE, span)
    top = jnp.max(scores, axis=1, keepdims=True)
    raised = jnp.exp(scores - top)
    total = jnp.sum(raised, axis=1, keepdims=True)
    return raised * (1.0 / total)


def forward_kernel(halo, tiles_ref, lo_ref, hi_ref, q_ref, k_ref, v_ref, out_ref, bias_ref):
    count = k_ref.shape[0]
    pairs = q_ref.shape[1] // TILE
    tiles = q_ref.shape[0] // TILE

    def tile_step(tile, carry):
        here = tile + halo // TILE
        blocks = tiles_ref[1, here]

        def act(span):
            first = jnp.minimum(tiles_ref[0, here], count - span)
            first = pl.multiple_of(first, ALIGN)
            row = pl.multiple_of(tile * TILE, TILE)
            write_bias(bias_ref, lo_ref, hi_ref, pl.multiple_of(row + halo, TILE), first, span)

            def pair_step(pair, inner):
                lanes = pl.ds(pl.multiple_of(pair * TILE, TILE), TILE)
                q2 = split_pair(q_ref[pl.ds(row, TILE), lanes])
                k = k_ref[pl.ds(first, span), lanes]
                v = v_ref[pl.ds(first, span), lanes]
                weights = pair_weights(q2, k, bias_ref[:, :span]).astype(bf16)
                out_ref[pl.ds(row, TILE), lanes] = join_pair(mm(weights, v)).astype(bf16)
                return inner

            lax.fori_loop(0, pairs, pair_step, 0, unroll=pairs)

        by_span(blocks, count, act)
        return carry

    lax.fori_loop(0, tiles, tile_step, 0)


def lasting(micros):
    return pl.CostEstimate(flops=int(micros * 2e7), bytes_accessed=int(micros * 7e4), transcendentals=0)


def lane_group(array, group, groups):
    return pl.BlockSpec((array.shape[0], array.shape[1] // groups), lambda i: (0, group))


def whole(array):
    return pl.BlockSpec(array.shape, lambda i: (0, 0))


def attend_forward(bounds, queries, keys, values, halo, group, groups):
    tiles, low, high = bounds
    rows, width = queries.shape
    arrays = (queries, keys, values)
    return pl.pallas_call(
        functools.partial(forward_kernel, halo),
        grid=(1,),
        out_shape=jax.ShapeDtypeStruct((rows, width // groups), bf16),
        in_specs=[pl.BlockSpec(memory_space=pltpu.SMEM), whole(low), whole(high)]
        + [lane_group(a, group, groups) for a in arrays],
        out_specs=pl.BlockSpec((rows, width // groups), lambda i: (0, 0)),
        scratch_shapes=[pltpu.VMEM((TILE, keys.shape[0]), f32)],
        compiler_params=pltpu.CompilerParams(vmem_limit_bytes=14 * 2**20),
        cost_estimate=lasting(18 / groups),
        name="attend_forward",
    )(tiles, low, high, *arrays)


def backward_kernel(
    halo, tiles_ref, lo_ref, hi_ref, q_ref, k_ref, v_ref, g_ref,
    dq_ref, dk_ref, dv_ref, bias_ref, dk_sum, dv_sum,
):
    count = k_ref.shape[0]
    own = dq_ref.shape[0]
    pairs = q_ref.shape[1] // TILE
    dk_sum[...] = jnp.zeros_like(dk_sum)
    dv_sum[...] = jnp.zeros_like(dv_sum)

    def tile_step(tile, carry):
        blocks = tiles_ref[2, tile]
        mine = (tile >= halo // TILE) & (tile < (halo + own) // TILE)

        def act(span):
            first = jnp.minimum(tiles_ref[0, tile], count - span)
            first = pl.multiple_of(first, ALIGN)
            row = pl.multiple_of(tile * TILE, TILE)
            write_bias(bias_ref, lo_ref, hi_ref, row, first, span)

            def pair_step(pair, inner):
                lanes = pl.ds(pl.multiple_of(pair * TILE, TILE), TILE)
                q2 = split_pair(q_ref[pl.ds(row, TILE), lanes])
                g2 = split_pair(g_ref[pl.ds(row, TILE), lanes])
                k = k_ref[pl.ds(first, span), lanes]
                v = v_ref[pl.ds(first, span), lanes]
                weights = pair_weights(q2, k, bias_ref[:, :span])
                slopes = mm(g2, v, NT)
                inner_sum = jnp.sum(weights * slopes, axis=1, keepdims=True)
                scores = (weights * (slopes - inner_sum)).astype(bf16)
                dv_sum[pl.ds(first, span), lanes] += mm(weights.astype(bf16), g2, TN)
                dk_sum[pl.ds(first, span), lanes] += mm(scores, q2, TN)

                @pl.when(mine)
                def _():
                    grad = join_pair(mm(scores, k)).astype(bf16)
                    to = pl.multiple_of(row - halo, TILE)
                    dq_ref[pl.ds(to, TILE), lanes] = grad * jnp.asarray(1.0 / math.sqrt(HEAD), bf16)

                return inner

            lax.fori_loop(0, pairs, pair_step, 0, unroll=pairs)

        by_span(blocks, count, act)
        return carry

    lax.fori_loop(0, count // TILE, tile_step, 0)
    dk_ref[...] = dk_sum[pl.ds(halo, own), :].astype(bf16)
    dv_ref[...] = dv_sum[pl.ds(halo, own), :].astype(bf16)


def attend_backward(bounds, queries, keys, values, grads, halo, group, groups):
    tiles, low, high = bounds
    count, width = keys.shape
    lanes = width // groups
    arrays = (queries, keys, values, grads)
    out = jax.ShapeDtypeStruct((count - 2 * halo, lanes), bf16)
    return pl.pallas_call(
        functools.partial(backward_kernel, halo),
        grid=(1,),
        out_shape=(out, out, out),
        in_specs=[pl.BlockSpec(memory_space=pltpu.SMEM), whole(low), whole(high)]
        + [lane_group(a, group, groups) for a in arrays],
        out_specs=(pl.BlockSpec(out.shape, lambda i: (0, 0)),) * 3,
        scratch_shapes=[
            pltpu.VMEM((TILE, count), f32),
            pltpu.VMEM((count, lanes), f32),
            pltpu.VMEM((count, lanes), f32),
        ],
        compiler_params=pltpu.CompilerParams(vmem_limit_bytes=20 * 2**20),
        cost_estimate=lasting(42 / groups),
        name="attend_backward",
    )(tiles, low, high, *arrays)


SMEM = pl.BlockSpec(memory_space=pltpu.SMEM)
VMEM = pl.BlockSpec(memory_space=pltpu.VMEM)
PLANE = 8


def local(kernel, place, arrays, outs, scratch, micros, name, mib=20):
    return pl.pallas_call(
        kernel,
        out_shape=tuple(jax.ShapeDtypeStruct(shape, dtype) for shape, dtype in outs),
        in_specs=[SMEM] + [VMEM] * len(arrays),
        out_specs=(VMEM,) * len(outs),
        scratch_shapes=[pltpu.VMEM(shape, dtype) for shape, dtype in scratch],
        compiler_params=pltpu.CompilerParams(vmem_limit_bytes=mib * 2**20),
        cost_estimate=lasting(micros),
        name=name,
    )(place, *arrays)


def own_heads_kernel(place_ref, q_ref, k_ref, v_ref, out_ref, rows_ref):
    place = place_ref[0]
    eighths = q_ref.shape[0] // PLANE
    slabs = q_ref.shape[0] // 8
    for i, ref in enumerate((q_ref, k_ref, v_ref)):
        rows_ref[pl.ds(i * slabs, slabs)] = ref[...].astype(f32).reshape(slabs, 8, -1)
    heads = 3 * eighths // 8
    for j in range(PLANE):
        held = [rows_ref[h * PLANE + (place ^ j)] for h in range(heads)]
        out_ref[j] = jnp.concatenate(held, axis=0).astype(bf16)


def own_units_kernel(place_ref, o_ref, i_ref, b_ref, out_ref, in_ref, back_ref, rows_ref, units_ref):
    place = place_ref[0]
    rows = in_ref.shape[1]
    heads = out_ref.shape[1] // 8
    rows_ref[...] = o_ref[...].astype(f32).reshape(rows_ref.shape)
    units_ref[...] = i_ref[...].astype(f32).T.reshape(units_ref.shape)
    for j in range(PLANE):
        held = [rows_ref[h * PLANE + (place ^ j)] for h in range(heads)]
        out_ref[j] = jnp.concatenate(held, axis=0).astype(bf16)
        in_ref[j] = units_ref[place ^ j].astype(bf16)
        back_ref[j] = b_ref[pl.ds(pl.multiple_of((place ^ j) * rows, rows), rows), :]


def by_eighth(refs):
    first, second = [], []
    for j in range(PLANE):
        far, y, x = j // 4, j // 2 % 2, j % 2
        first.append(refs[4].at[y, x] if far else refs[y].at[x])
        second.append(refs[4].at[2 + x, y] if far else refs[2 + x].at[y])
    return first, second


def eighth_rows(halves, j, member, start, count):
    first, second = halves[0][j], halves[1][j]
    middle = first.shape[1]
    pieces = []
    if start < middle:
        pieces.append(first[member, pl.ds(start, min(count, middle - start)), :])
    if start + count > middle:
        at = max(start, middle)
        pieces.append(second[member, pl.ds(at - middle, start + count - at), :])
    return pieces


def stage_eighths(own_ref, halves, member, start, stage_ref):
    for j in range(PLANE):
        if own_ref is not None and member == 0:
            stage_ref[j] = own_ref[j].astype(f32)
            continue
        at = 0
        of = member if own_ref is None else member - 1
        for piece in eighth_rows(halves, j, of, start, stage_ref.shape[1]):
            stage_ref[j, pl.ds(at, piece.shape[0]), :] = piece.astype(f32)
            at += piece.shape[0]


def head_block(stage_ref, head):
    return jnp.concatenate([stage_ref[j, pl.ds(head * 8, 8), :] for j in range(PLANE)], axis=0)


def project_kernel(
    place_ref, left_ref, tokens_ref, right_ref, own_ref, *refs
):
    halves, refs = by_eighth(refs[:5]), refs[5:]
    bias_ref, q_ref, k_ref, v_ref, w_ref, x_ref, stage_ref = refs
    ways = halves[0][0].shape[0] + 1
    heads = own_ref.shape[1] // 24
    halo = left_ref.shape[0]
    own = tokens_ref.shape[0]
    width = tokens_ref.shape[1]
    inner = heads * HEAD
    x_ref[:halo] = left_ref[...]
    x_ref[pl.ds(halo, own)] = tokens_ref[...]
    x_ref[pl.ds(halo + own, halo)] = right_ref[...]
    for member in range(ways):
        stage_eighths(own_ref, halves, member, 0, stage_ref)
        for kind in range(3):
            blocks = [head_block(stage_ref, kind * heads + h) for h in range(heads)]
            at = kind * width + member * inner
            w_ref[pl.ds(at, inner)] = jnp.concatenate(blocks, axis=0).astype(bf16)

    def step(i, carry):
        rows = pl.ds(pl.multiple_of(i * 256, 256), 256)
        x = x_ref[rows, :]
        q = mm(x, w_ref[:width], NT) + bias_ref[0:1]
        q_ref[rows, :] = (q * (1.0 / math.sqrt(HEAD))).astype(bf16)
        k_ref[rows, :] = mm(x, w_ref[pl.ds(width, width)], NT).astype(bf16)
        v_ref[rows, :] = (mm(x, w_ref[pl.ds(2 * width, width)], NT) + bias_ref[1:2]).astype(bf16)
        return carry

    lax.fori_loop(0, x_ref.shape[0] // 256, step, 0)


def join_units(own_ref, halves, out_ref):
    rows = own_ref.shape[1]
    ways = halves[0][0].shape[0] + 1
    for j in range(PLANE):
        out_ref[pl.ds(j * ways * rows, rows), :] = own_ref[j]
        for member in range(1, ways):
            at = (j * ways + member) * rows
            for piece in eighth_rows(halves, j, member - 1, 0, rows):
                out_ref[pl.ds(at, piece.shape[0]), :] = piece
                at += piece.shape[0]


def join_units_kernel(place_ref, own_ref, *refs):
    join_units(own_ref, by_eighth(refs[:5]), refs[5])


def join_in_out_kernel(place_ref, own_ref, own_out_ref, *refs):
    halves = by_eighth(refs[:5])
    in_ref, out_ref, stage_ref = refs[5:]
    join_units(own_ref, halves, in_ref)
    heads = own_out_ref.shape[1] // 8
    for member in range(halves[0][0].shape[0] + 1):
        stage_eighths(own_out_ref, halves, member, own_ref.shape[1], stage_ref)
        for h in range(heads):
            block = head_block(stage_ref, h)
            out_ref[pl.ds((member * heads + h) * HEAD, HEAD), :] = block.astype(bf16)


def split_digits(values):
    digits = []
    for _ in range(3):
        digits.append(values.astype(bf16))
        values = values - digits[-1].astype(f32)
    return digits


def biases_kernel(place_ref, along_ref, in_ref, q_ref, v_ref, heads_ref, units_ref, line_ref):
    place = place_ref[0]
    ways = along_ref.shape[0] + 1
    inner = q_ref.shape[1]
    rows = in_ref.shape[1] // PLANE
    first = along_ref.shape[1] - 8
    others = along_ref[:, first:, :].astype(f32)
    digits = split_digits(jnp.concatenate([q_ref[...], v_ref[...]], axis=1))
    digits = [digit.astype(f32) for digit in digits]
    for member in range(ways - 1):
        digits.append(others[member, 3:6, : 2 * inner])
    digits = jnp.concatenate(digits, axis=0).astype(bf16)
    lane = lax.broadcasted_iota(jnp.int32, (2 * inner, 2 * inner), 0)
    to = lax.broadcasted_iota(jnp.int32, (2 * inner, 2 * inner), 1)
    chosen = jnp.where((lane ^ (place << 3)) == to, 1.0, 0.0).astype(bf16)
    moved = mm(digits, chosen)
    sums = [moved[3 * m : 3 * m + 1] + moved[3 * m + 1 : 3 * m + 2] + moved[3 * m + 2 : 3 * m + 3] for m in range(ways)]
    heads_ref[0:1] = jnp.concatenate([value[:, :inner] for value in sums], axis=1)
    heads_ref[1:2] = jnp.concatenate([value[:, inner:] for value in sums], axis=1)
    for member in range(ways):
        if member == 0:
            value = in_ref[...]
        else:
            three = others[member - 1]
            value = three[0:1] + three[1:2] + three[2:3]
        for p in range(PLANE):
            line_ref[member * PLANE + p, 0:1, :rows] = value[:, p * rows : (p + 1) * rows]
    held = [
        line_ref[member * PLANE + (place ^ j), 0:1, :rows] for j in range(PLANE) for member in range(ways)
    ]
    units_ref[...] = jnp.concatenate(held, axis=1)


def vectors_kernel(place_ref, *refs):
    stat_refs, (units_ref, out_ref, line_ref) = refs[:6], refs[6:]
    place, own = place_ref[0], place_ref[1]
    ways, _, width = out_ref.shape
    inner = width // ways
    rows = units_ref.shape[1] // PLANE // ways
    for j in range(PLANE):
        for member in range(ways):
            at = j * ways + member
            line_ref[at, 0:1, :rows] = units_ref[:, at * rows : (at + 1) * rows]
    stats = jnp.concatenate([ref[...] for ref in stat_refs], axis=0)
    parts = [stats[:, i * inner : (i + 1) * inner] for i in range(ways)]
    for member in range(ways):
        held = [line_ref[(place ^ p) * ways + member, 0:1, :rows] for p in range(PLANE)]
        mine = parts[0]
        for i in range(1, ways):
            mine = jnp.where((own ^ member) == i, parts[i], mine)
        norms = jnp.concatenate([mine[i : i + 1] for i in range(6)], axis=1)
        norms = jnp.concatenate([norms, jnp.zeros((1, 2 * inner), f32)], axis=1)
        lines = [jnp.concatenate(held, axis=1), norms[:, :width], norms[:, width:]]
        out_ref[member] = jnp.concatenate([*lines, jnp.zeros((5, width), f32)], axis=0)


def put_heads(ways, heads, sum_ref, kind, first_head, block):
    for i in range(block.shape[0] // HEAD):
        member, h = divmod(first_head + i, heads)
        for j in range(PLANE):
            part = block[i * HEAD + j * 8 : i * HEAD + j * 8 + 8]
            sum_ref[j * ways + member, pl.ds((kind * heads + h) * 8, 8), :] = part


def part_pieces(sum_ref, keep_ref, send_ref):
    half = keep_ref.shape[0]
    for i in range(half):
        keep_ref[i] = sum_ref[i].astype(bf16)
        send_ref[i] = sum_ref[half + i].astype(bf16)


def out_grads_kernel(ways, place_ref, left_ref, right_ref, first_ref, keep_ref, send_ref, sum_ref):
    width = first_ref.shape[1]
    heads = width // ways // HEAD
    sum_ref[:, heads * 8 :, :] = jnp.zeros((PLANE * ways, 8, width), f32)
    for g, ref in enumerate((left_ref, right_ref)):
        block = mm(ref[...], first_ref[...], TN)
        put_heads(ways, heads, sum_ref, 0, g * width // 2 // HEAD, block)
    part_pieces(sum_ref, keep_ref, send_ref)


def piece_grads_kernel(groups, place_ref, *refs):
    grad_refs = refs[: 3 * groups]
    tokens_ref, vectors_ref, keep_ref, send_ref, sum_ref = refs[3 * groups :]
    place = place_ref[0]
    ways = vectors_ref.shape[0]
    width = tokens_ref.shape[1]
    inner = width // ways
    heads = inner // HEAD
    lanes = width // groups
    for kind in range(3):
        for g in range(groups):
            block = mm(grad_refs[kind * groups + g][...], tokens_ref[...], TN)
            put_heads(ways, heads, sum_ref, kind, g * lanes // HEAD, block)
    lane = lax.broadcasted_iota(jnp.int32, (width, width), 0)
    to = lax.broadcasted_iota(jnp.int32, (width, width), 1)
    member = sum((lane >= i * inner).astype(jnp.int32) for i in range(1, ways))
    within = lane - member * inner
    spot = within ^ (place << 3)
    row = lax.broadcasted_iota(jnp.int32, (8, width), 0)
    column = lax.broadcasted_iota(jnp.int32, (8, width), 1)
    of = sum((column >= i * inner).astype(jnp.int32) for i in range(1, ways))
    ones = jnp.ones((8, tokens_ref.shape[0]), bf16)
    lines = jnp.zeros((8, width), f32)
    for kind, first in ((0, width - 2 * inner), (2, width - inner)):
        sums = [mm(ones, grad_refs[kind * groups + g][...]) for g in range(groups)]
        sums = jnp.where(of == row, jnp.concatenate(sums, axis=1), 0.0)
        chosen = jnp.where(spot + first == to, 1.0, 0.0).astype(bf16)
        lines = lines + mm(sums.astype(bf16), chosen)
    below = 3 * heads * 8
    for i in range(ways):
        block = vectors_ref[i] + jnp.where(row == 2, lines[i : i + 1], 0.0)
        for j in range(PLANE):
            sum_ref[j * ways + i, pl.ds(below, 8), :] = block
    part_pieces(sum_ref, keep_ref, send_ref)


def gather_heads(place, rows_ref, first, out_ref):
    held = []
    for h in range(out_ref.shape[0] // HEAD):
        for p in range(PLANE):
            held.append(rows_ref[place ^ p, pl.ds(first + h * 8, 8), :])
    out_ref[...] = jnp.concatenate(held, axis=0)


def finish_heads_kernel(place_ref, *refs):
    q_ref, k_ref, v_ref, rows_ref = refs[5:]
    stage_eighths(None, by_eighth(refs[:5]), 0, 0, rows_ref)
    for kind, ref in enumerate((q_ref, k_ref, v_ref)):
        gather_heads(place_ref[0], rows_ref, kind * ref.shape[0] // PLANE, ref)


def finish_units_kernel(place_ref, *refs):
    back_ref, in_ref, out_ref, rows_ref, turned_ref = refs[5:]
    place = place_ref[0]
    rows = back_ref.shape[0] // PLANE
    stage_eighths(None, by_eighth(refs[:5]), 0, 0, rows_ref)
    for p in range(PLANE):
        back_ref[pl.ds(p * rows, rows), :] = rows_ref[place ^ p, :rows, :]
        turned_ref[pl.ds(p * rows, rows), :] = rows_ref[place ^ p, pl.ds(rows, rows), :]
    in_ref[...] = turned_ref[...].T
    gather_heads(place, rows_ref, 2 * rows, out_ref)


def norm_parts(values):
    center = values - jnp.mean(values, axis=-1, keepdims=True)
    spread = jnp.mean(center * center, axis=-1, keepdims=True)
    return center, lax.rsqrt(spread + epsilon)


def norm_pull(grad, unit, inverse, gain):
    scaled = grad * gain
    mean = jnp.mean(scaled, axis=-1, keepdims=True)
    along = jnp.mean(scaled * unit, axis=-1, keepdims=True)
    return inverse * (scaled - mean - unit * along)


def gelu_both(before):
    half = 0.5 * (1.0 + lax.erf(before * math.sqrt(0.5)))
    bell = jnp.exp(-0.5 * before * before) * (1.0 / math.sqrt(2.0 * math.pi))
    return before * half, half + before * bell


def partner(values, step):
    ways = lax.axis_size("mp")
    return lax.ppermute(values, "mp", [(i, i ^ step) for i in range(ways)])


def halo_rows(values, halo):
    ways = lax.axis_size("mp")
    before = lax.ppermute(values[-halo:], "mp", [(i, i + 1) for i in range(ways - 1)])
    after = lax.ppermute(values[:halo], "mp", [(i + 1, i) for i in range(ways - 1)])
    return before, after


def group_tables(table):
    ways = lax.axis_size("mp")
    data_ways = lax.axis_size("dp")
    total = table
    for step in range(1, ways):
        total = total + partner(table, step)
    held = total[None]
    data_index = lax.axis_index("dp")
    level = 1
    while level < data_ways:
        other = lax.ppermute(held, "dp", [(i, i ^ level) for i in range(data_ways)])
        first = (data_index & level) == 0
        held = jnp.where(
            first, jnp.concatenate([held, other]), jnp.concatenate([other, held])
        )
        level *= 2
    return held


CORE, NEAR_X, NEAR_Y = 1, 2, 4


def swap(values, bit):
    ways = lax.axis_size("dp")
    return lax.ppermute(values, "dp", [(i, i ^ bit) for i in range(ways)])


def along(piece):
    return [partner(piece, step) for step in range(1, lax.axis_size("mp"))]


def bit_step(held, level, *gates):
    order = sorted(held)
    other = after(partner(jnp.stack([held[i] for i in order]), level), gates)
    return held | {i | level: other[at] for at, i in enumerate(order)}


def others_of(held):
    return jnp.stack([held[i] for i in sorted(held)[1:]])


def first_step(values, *gates):
    middle = values.shape[1] // 2
    first, second = values[:, :middle], values[:, middle:]
    arrived = after((swap(first, NEAR_X), swap(second, NEAR_Y)), gates)
    return [jnp.stack([first, arrived[0]]), jnp.stack([second, arrived[1]])]


def second_step(pairs, *gates):
    first, second = pairs
    arrived = after((swap(first, NEAR_Y), swap(second, NEAR_X)), gates)
    return [first, arrived[0], second, arrived[1]]


def core_step(held):
    return [*held, swap(jnp.stack(held), CORE)]


def after(value, *others):
    return lax.optimization_barrier((value, others))[0]


def add(first, second):
    return (first.astype(f32) + second.astype(f32)).astype(bf16)


def first_sum_step(sums):
    half = sums.shape[2] // 2
    first, second = sums[:, :, :half], sums[:, :, half:]
    return [(first[0], swap(first[1], NEAR_Y)), (second[:, 0], swap(second[:, 1], NEAR_X))]


def second_sum_step(halves):
    first, second = (add(*half) for half in halves)
    return [(first[0], swap(first[1], NEAR_X)), (second[0], swap(second[1], NEAR_Y))]


def over_groups(total):
    level = PLANE
    while level < lax.axis_size("dp"):
        total = total + swap(total, level)
        level *= 2
    return total


def sum_along(parts):
    total = parts[0].astype(f32)
    for step in range(1, len(parts)):
        total = total + partner(parts[step], step).astype(f32)
    return over_groups(total)


def shards(
    tokens, grad_out, pass_len, labels, w_query, w_key, w_value, b_query, b_value, w_out, b_out,
    ln1_gain, ln1_shift, w_in, b_in, w_back, b_back, ln2_gain, ln2_shift,
):
    ways = lax.axis_size("mp")
    data_ways = lax.axis_size("dp")
    mp_index = lax.axis_index("mp")
    data_index = lax.axis_index("dp")
    own_rows, width = tokens.shape
    rows_here = pass_len.shape[0]
    inner = w_query.shape[1]
    units = w_in.shape[1]
    halo = ROW_LEN // 4
    count = own_rows + 2 * halo
    scale = 1.0 / math.sqrt(HEAD)
    temper = 2.0 / math.sqrt(width)

    piece_rows = units // PLANE
    heads = inner // HEAD
    part = inner // PLANE
    place = jnp.stack([(data_index & CORE) << 2 | (data_index % PLANE) >> 1, mp_index])
    (qkv_own,) = local(
        own_heads_kernel, place, (w_query.T, w_key.T, w_value.T), [((PLANE, 3 * part, width), bf16)],
        [((3 * heads * PLANE, 8, width), f32)], 4, "own_heads",
    )
    biases = jnp.concatenate([b_in, b_query, b_value])
    digits, rest = [], biases
    for _ in range(3):
        digits.append(lax.reduce_precision(rest, 8, 7))
        rest = rest - digits[-1]
    digits = jnp.stack(digits)
    lines = jnp.concatenate(
        [digits[:, :units], jnp.pad(digits[:, units:], ((0, 0), (0, width - 2 * inner)))]
    )
    lines = jnp.pad(lines, ((0, 2), (0, 0))).astype(bf16)
    qkv_along = along(jnp.concatenate([qkv_own[0], lines]))
    tokens_before, tokens_after = halo_rows(tokens, halo)
    w_out, w_in, w_back, place = lax.optimization_barrier((w_out, w_in, w_back, place, qkv_own))[:4]
    out_own, in_own, back_own = local(
        own_units_kernel, place, (w_out, w_in, w_back),
        [((PLANE, part, width), bf16), ((PLANE, piece_rows, width), bf16), ((PLANE, piece_rows, width), bf16)],
        [((heads * PLANE, 8, width), f32), ((PLANE, piece_rows, width), f32)], 5, "own_units",
    )
    in_piece = jnp.concatenate([in_own[0], out_own[0], jnp.zeros((8, width), bf16), back_own[0]])
    in_piece = after(in_piece, qkv_along)
    qkv_along = jnp.stack(qkv_along)
    qkv_pairs = first_step(qkv_along)
    in_held = {0: in_piece}
    level = ways // 2
    while level > 1:
        in_held = bit_step(in_held, level)
        level //= 2
    in_held = after(in_held, qkv_pairs)
    qkv_held = second_step(after(qkv_pairs, tokens_before, tokens_after, in_held))
    in_along = others_of(bit_step(in_held, 1))
    bias_heads, bias_in = local(
        biases_kernel, place, (after(qkv_along, qkv_pairs), b_in[None], b_query[None], b_value[None]),
        [((2, width), f32), ((1, ways * units), f32)], [((ways * PLANE, 8, 128), f32)], 2, "biases",
    )
    start = after(mp_index * own_rows - halo, qkv_pairs)
    bounds = segment_bounds(pass_len, start, halo, own_rows)
    qkv_parts = core_step(after(qkv_held, in_along, bias_heads, bounds))
    in_start = after(in_along, qkv_parts)
    in_rows = piece_rows + part + 8

    tokens_before = after(tokens_before, in_along)
    qkv = (tokens_before, tokens, tokens_after, qkv_own, *qkv_parts, bias_heads)
    queries, keys, values, qkv_all = local(
        project_kernel, place, qkv, [((count, width), bf16)] * 3 + [((3 * width, width), bf16)],
        [((count, width), bf16), ((PLANE, 3 * part, width), f32)], 10, "project", 32,
    )
    own_queries = queries[halo : halo + own_rows]
    in_pairs = first_step(in_start[:, :in_rows], queries)
    own_queries = after(own_queries, in_pairs)
    context = [attend_forward(bounds, own_queries, keys, values, halo, 0, 2)]
    in_held = second_step(in_pairs, context[0])
    back_start = after(in_start[:, in_rows:], in_held)
    own_queries = after(own_queries, in_held, back_start, context[0])
    in_parts = core_step(in_held)
    context.append(attend_forward(bounds, own_queries, keys, values, halo, 1, 2))
    in_own = after(in_own, context[1])
    in_all, out_all = local(
        join_in_out_kernel, place, (in_own, out_own, *in_parts),
        [((ways * units, width), bf16), ((width, width), bf16)],
        [((PLANE, part, width), f32)], 5, "join_in_out",
    )
    back_held = second_step(first_step(back_start, context[1]), in_all)
    back_parts = core_step(back_held)
    (back_all,) = local(
        join_units_kernel, place, (back_own, *back_parts),
        [((ways * units, width), bf16)], [], 4, "join_back",
    )
    attended = mm(context[0], out_all[: width // 2]) + mm(context[1], out_all[width // 2 :])
    first_sum = tokens.astype(f32) + attended + b_out
    center_one, inverse_one = norm_parts(first_sum)
    unit_one = center_one * inverse_one
    hidden = unit_one * ln1_gain + ln1_shift
    hidden_low = after(hidden.astype(bf16), back_held)

    active, slope = gelu_both(mm(hidden_low, in_all, NT) + bias_in)
    active, slope = lax.optimization_barrier((active.astype(bf16), slope.astype(bf16)))
    second_sum = hidden + mm(active, back_all) + b_back
    center_two, inverse_two = norm_parts(second_sum)
    unit_two = center_two * inverse_two
    mixed = (unit_two * ln2_gain + ln2_shift).astype(bf16)

    query_count = PAIRS * rows_here
    places = cls_places(pass_len) + (jnp.arange(rows_here, dtype=jnp.int32) * ROW_LEN)[:, None]
    table_places = jnp.concatenate([places[:, :PAIRS].reshape(-1), places[:, PAIRS:].reshape(-1)])
    table_places = table_places - mp_index * own_rows
    picker = table_places[:, None] == jnp.arange(own_rows, dtype=jnp.int32)[None, :]
    table = mm(picker.astype(bf16), mixed).astype(bf16)
    digits = jnp.concatenate([labels // 32, labels % 32]).astype(bf16)
    digits = jnp.where(mp_index == 0, digits, 0)
    extra = jnp.zeros((8, width), bf16).at[0, : 2 * query_count].set(digits)
    tables = group_tables(jnp.concatenate([table, extra]))
    all_count = data_ways * query_count
    query_cls = tables[:, :query_count].reshape(all_count, width)
    passage_cls = tables[:, query_count : 2 * query_count].reshape(all_count, width)
    digits = tables[:, 2 * query_count, : 2 * query_count].astype(jnp.int32)
    all_labels = (digits[:, :query_count] * 32 + digits[:, query_count:]).reshape(-1)

    logits = mm(query_cls, passage_cls, NT) * temper
    targets = all_labels[:, None] == jnp.arange(all_count, dtype=jnp.int32)[None, :]
    top = jnp.max(logits, axis=1, keepdims=True)
    raised = jnp.exp(logits - top)
    total = jnp.sum(raised, axis=1, keepdims=True)
    losses = top[:, 0] + jnp.log(total[:, 0]) - jnp.sum(jnp.where(targets, logits, 0.0), axis=1)
    query_losses = lax.dynamic_slice_in_dim(losses, data_index * query_count, query_count)
    grad_logits = (raised / total - targets.astype(f32)) * temper
    rows_of = lax.dynamic_slice_in_dim(grad_logits, data_index * query_count, query_count, 0)
    columns_of = lax.dynamic_slice_in_dim(grad_logits, data_index * query_count, query_count, 1)
    grad_cls = jnp.concatenate(
        [
            jnp.dot(rows_of, passage_cls.astype(f32), precision=highest),
            jnp.dot(columns_of.T, query_cls.astype(f32), precision=highest),
        ]
    )
    grad_mixed = grad_out.astype(f32) + jnp.dot(
        picker.astype(f32).T, grad_cls, precision=highest
    )

    grad_second = norm_pull(grad_mixed, unit_two, inverse_two, ln2_gain)
    stats = [
        jnp.sum(grad_mixed * unit_two, axis=0, keepdims=True),
        jnp.sum(grad_mixed, axis=0, keepdims=True),
        jnp.sum(grad_second, axis=0, keepdims=True),
    ]
    second_low = grad_second.astype(bf16)

    def to_core(left, right):
        return mm(left[:, left.shape[1] // 2 :], right, TN).astype(bf16)

    def chip_sum(left, right, arrived):
        own = mm(left[:, : left.shape[1] // 2], right, TN)
        return add(own, arrived).reshape(2, 2, ways, piece_rows, width)

    back_sent = to_core(active, second_low)
    back_arrived = swap(back_sent, CORE)
    pulled, back_sent = lax.optimization_barrier((second_low, back_sent))
    grad_before = (mm(pulled, back_all, NT) * slope.astype(f32)).astype(bf16)
    back_sum = chip_sum(active, second_low, back_arrived)
    back_half = swap(back_sum[1], NEAR_Y)
    in_sent = to_core(grad_before, hidden_low)
    in_arrived = swap(in_sent, CORE)
    in_sum = chip_sum(grad_before, hidden_low, in_arrived)
    in_half = swap(in_sum[:, 1], NEAR_X)
    pulled = after(grad_before, back_sum, in_sum)
    grad_hidden = grad_second + mm(pulled, in_all)
    grad_first = norm_pull(grad_hidden, unit_one, inverse_one, ln1_gain)
    stats += [
        jnp.sum(grad_hidden * unit_one, axis=0, keepdims=True),
        jnp.sum(grad_hidden, axis=0, keepdims=True),
        jnp.sum(grad_first, axis=0, keepdims=True),
    ]
    first_low = grad_first.astype(bf16)
    first_before, first_after = halo_rows(first_low, halo)
    out_keep, out_sent = local(
        functools.partial(out_grads_kernel, ways), place, (*context, first_low),
        [((4 * ways, part + 8, width), bf16)] * 2, [((8 * ways, part + 8, width), f32)], 3, "out_grads",
    )
    out_sum = add(out_keep, swap(out_sent, CORE)).reshape(2, 2, ways, part + 8, width)
    out_half = swap(out_sum[1], NEAR_Y)

    d_b_in = jnp.sum(grad_before, axis=0, dtype=f32, keepdims=True)
    (vectors,) = local(
        vectors_kernel, place, (*stats, d_b_in), [((ways, 8, width), f32)],
        [((ways * PLANE, 8, 128), f32)], 2, "vectors",
    )

    first_window = jnp.concatenate([first_before, first_low, first_after])
    grad_context = mm(first_window, out_all, NT).astype(bf16)
    groups = 3
    parts = []

    def attend(grads, group):
        return attend_backward(bounds, queries, keys, values, grads, halo, group, groups)

    grad_context = after(grad_context, in_sum, back_sum, out_sum, vectors)
    parts.append(attend(grad_context, 0))
    back_half, in_half, out_half = after((back_half, in_half, out_half), parts[0])
    back_sum = add(back_sum[0], back_half)
    in_sum = add(in_sum[:, 0], in_half)
    out_sum = add(out_sum[0], out_half)
    back_half = swap(back_sum[1], NEAR_X)
    in_half = swap(in_sum[1], NEAR_Y)
    out_half = swap(out_sum[1], NEAR_X)
    grad_context = after(grad_context, back_sum, in_sum, out_sum, parts[0])
    parts.append(attend(grad_context, 1))
    halves = [(back_sum[0], back_half), (in_sum[0], in_half), (out_sum[0], out_half)]
    halves = after(halves, parts[1])
    early_sum = jnp.concatenate([add(*half) for half in halves], axis=1)
    early_parts = [early_sum[i] for i in range(ways)]
    early_odd = jnp.stack(early_parts[1::2])
    grad_context, early_odd = lax.optimization_barrier((grad_context, early_odd))
    early_odd = partner(early_odd, 1)
    parts.append(attend(grad_context, 2))
    early_odd = after(early_odd, parts[2])
    early_parts = [add(even, odd) for even, odd in zip(early_parts[::2], early_odd)]
    tokens_low = after(tokens, early_parts)

    grad_parts = [g[i] for i in range(3) for g in parts]
    late_rows = 3 * part + 8
    late_keep, late_sent = local(
        functools.partial(piece_grads_kernel, groups), place, (*grad_parts, tokens_low, vectors),
        [((4 * ways, late_rows, width), bf16)] * 2, [((8 * ways, late_rows, width), f32)], 8, "piece_grads", 36,
    )
    late_sum = add(late_keep, swap(late_sent, CORE)).reshape(2, 2, ways, late_rows, width)
    halves = first_sum_step(late_sum)
    level, early_own = 2, early_parts[0].astype(f32)
    while level < ways:
        early_own = early_own + after(partner(early_parts[level // 2], level), halves).astype(f32)
        level *= 2
    halves = second_sum_step(halves)
    early_held = first_step(over_groups(early_own).astype(bf16)[None])
    late_parts = [half[i] for half in (add(*h) for h in halves) for i in range(ways // 2)]
    early_held = second_step(after(early_held, late_parts))
    grad_queries, grad_keys, grad_values = (jnp.concatenate(p, axis=1) for p in zip(*parts))
    d_tokens = (
        grad_first
        + mm(grad_queries, qkv_all[:width])
        + mm(grad_keys, qkv_all[width : 2 * width])
        + mm(grad_values, qkv_all[2 * width :])
    )
    late_total = sum_along(late_parts)
    early_pieces = core_step(after(early_held, late_total))
    late_held = first_step(late_total.astype(bf16)[None])
    late_pieces = core_step(second_step(after(late_held, d_tokens)))
    line = late_total[3 * part :]

    d_query, d_key, d_value = local(
        finish_heads_kernel, place, late_pieces, [((inner, width), f32)] * 3,
        [((PLANE, 3 * part, width), f32)], 4, "finish_heads",
    )
    d_back, d_in, d_out = local(
        finish_units_kernel, place, early_pieces,
        [((units, width), f32), ((width, units), f32), ((inner, width), f32)],
        [((PLANE, 2 * piece_rows + part + 8, width), f32), ((units, width), f32)], 6, "finish_units",
    )
    norms = [line[1 + i // ways, i % ways * inner : (i % ways + 1) * inner] for i in range(8)]
    return (
        mixed,
        query_losses,
        d_tokens,
        d_query.T,
        d_key.T,
        d_value.T,
        norms[6],
        norms[7],
        d_out,
        norms[5],
        norms[3],
        norms[4],
        d_in,
        line[0],
        d_back,
        norms[2],
        norms[0],
        norms[1],
    )


def solution(mesh):
    return jax.shard_map(
        shards,
        mesh=mesh,
        in_specs=(
            P(("dp", "mp"), None), P(("dp", "mp"), None), P("dp", None), P("dp"),
            P(None, "mp"), P(None, "mp"), P(None, "mp"), P("mp"), P("mp"), P("mp", None), P(),
            P(), P(), P(None, "mp"), P("mp"), P("mp", None), P(), P(), P(),
        ),
        out_specs=(
            P(("dp", "mp"), None), P("dp"), P(("dp", "mp"), None),
            P(None, "mp"), P(None, "mp"), P(None, "mp"), P("mp"), P("mp"), P("mp", None),
            P("mp"), P("mp"), P("mp"), P(None, "mp"), P("mp"), P("mp", None), P("mp"), P("mp"), P("mp"),
        ),
        check_vma=False,
    )
```

```python
import functools
import math

import jax
import jax.numpy as jnp
from jax import lax
from jax.experimental import pallas as pl
from jax.experimental.pallas import tpu as pltpu
from jax.sharding import PartitionSpec as P

HEAD = 64
ROW_LEN = 1024
PAIRS = 4
QLEN = 32
TILE = 128
QUERIES = 64
QUAD = 4 * HEAD
ALIGN = 32
BLOCKS = (1, 2, 3, 4, 5, 7, 10)

epsilon = 1e-12
masked_score = -1e30
highest = lax.Precision.HIGHEST
f32 = jnp.float32
bf16 = jnp.bfloat16
NT = (((1,), (1,)), ((), ()))
TN = (((0,), (0,)), ((), ()))
NN = (((1,), (0,)), ((), ()))


def mm(a, b, dims=NN):
    return lax.dot_general(a, b, dims, preferred_element_type=f32)


def bounds_kernel(halo, own, start_ref, pass_ref, tiles_ref, low_ref, high_ref):
    start = start_ref[0]
    count = low_ref.shape[1]
    rows = pass_ref.shape[0]
    last = rows * ROW_LEN
    cuts = []
    for row in range(rows):
        cuts += [jnp.int32(row * ROW_LEN + j * QLEN) for j in range(PAIRS + 1)]
        for j in range(PAIRS):
            cuts.append(cuts[-1] + pass_ref[row, j])

    def low_of(place):
        low = jnp.full_like(place, start)
        for cut in cuts:
            low = jnp.where(cut <= place, cut, low)
        return jnp.clip(jnp.where(place >= last, last, low) - start, 0, count)

    def high_of(place):
        high = jnp.full_like(place, last)
        for cut in reversed(cuts):
            high = jnp.where(cut > place, cut, high)
        return jnp.clip(jnp.where(place >= last, start + count, high) - start, 0, count)

    place = start + lax.broadcasted_iota(jnp.int32, (1, count), 1)
    low_ref[...] = low_of(place)
    high_ref[...] = high_of(place)
    for tile in range(count // QUERIES):
        at = tile * QUERIES
        first = low_of(start + at)
        after_last = high_of(start + at + QUERIES - 1)
        low = first // ALIGN * ALIGN
        blocks = (after_last - low + TILE - 1) // TILE
        tiles_ref[0, tile] = low
        tiles_ref[1, tile] = blocks
        if at < halo:
            blocks = jnp.where(after_last > halo, blocks, 0)
        if at >= halo + own:
            blocks = jnp.where(first < halo + own, blocks, 0)
        tiles_ref[2, tile] = blocks


def segment_bounds(pass_len, start, halo, own):
    count = own + 2 * halo
    smem = pl.BlockSpec(memory_space=pltpu.SMEM)
    vmem = pl.BlockSpec(memory_space=pltpu.VMEM)
    line = jax.ShapeDtypeStruct((1, count), jnp.int32)
    return pl.pallas_call(
        functools.partial(bounds_kernel, halo, own),
        out_shape=(jax.ShapeDtypeStruct((3, count // QUERIES), jnp.int32), line, line),
        in_specs=[smem, smem],
        out_specs=(smem, vmem, vmem),
        compiler_params=pltpu.CompilerParams(vmem_limit_bytes=8 * 2**20),
        name="bounds",
    )(start.reshape(1), pass_len)


def cls_places(pass_len):
    lens = [pass_len[:, j] for j in range(PAIRS)]
    starts = [jnp.full_like(lens[0], j * QLEN) for j in range(PAIRS)]
    at = jnp.full_like(lens[0], PAIRS * QLEN)
    for j in range(PAIRS):
        starts.append(at)
        at = at + lens[j]
    return jnp.stack(starts, axis=1)


def by_span(blocks, count, act):
    least = 0
    for size in BLOCKS:
        if size * TILE > count:
            break

        @pl.when((blocks > least) & (blocks <= size))
        def _(size=size):
            act(size * TILE)

        least = size


def head_of(shape):
    return lax.broadcasted_iota(jnp.int32, shape, 1) // HEAD


def split_heads(block):
    head = head_of(block.shape)
    zero = jnp.zeros_like(block)
    return jnp.concatenate([jnp.where(head == h, block, zero) for h in range(4)], axis=0)


def join_heads(stacked):
    rows = stacked.shape[0] // 4
    head = head_of((rows, stacked.shape[1]))
    out = stacked[:rows]
    for h in range(1, 4):
        out = jnp.where(head == h, stacked[h * rows : (h + 1) * rows], out)
    return out


def four_times(ref, row):
    line = ref[:, pl.ds(pl.multiple_of(row // TILE * TILE, TILE), TILE)]
    turned = jnp.concatenate([line[:, QUERIES:], line[:, :QUERIES]], axis=1)
    lane = lax.broadcasted_iota(jnp.int32, line.shape, 1)
    odd = row % TILE >= QUERIES
    both = jnp.where((lane < QUERIES) != odd, line, turned)
    return jnp.concatenate([both, both], axis=1)


def write_bias(bias_ref, lo_ref, hi_ref, row, first, span):
    place = lax.broadcasted_iota(jnp.int32, (span, QUAD), 0) + first
    inside = (place >= four_times(lo_ref, row)) & (place < four_times(hi_ref, row))
    bias_ref[:span] = jnp.where(inside, 0.0, masked_score)


def head_weights(scores, bias):
    scores = [score + bias for score in scores]
    tops = [jnp.max(score, axis=0, keepdims=True) for score in scores]
    raised = [jnp.exp(score - top) for score, top in zip(scores, tops)]
    inverses = [1.0 / jnp.sum(value, axis=0, keepdims=True) for value in raised]
    return [value * inverse for value, inverse in zip(raised, inverses)]


def forward_kernel(halo, start, tiles_ref, lo_ref, hi_ref, q_ref, k_ref, v_ref, out_ref, bias_ref):
    count = k_ref.shape[0]
    quads = [pl.ds(i * QUAD, QUAD) for i in range(q_ref.shape[1] // QUAD)]

    def tile_step(tile, carry):
        here = tile + (start + halo) // QUERIES
        blocks = tiles_ref[1, here]

        def act(span):
            first = jnp.minimum(tiles_ref[0, here], count - span)
            keys = pl.ds(pl.multiple_of(first, ALIGN), span)
            to = pl.ds(pl.multiple_of(tile * QUERIES, QUERIES), QUERIES)
            row = pl.multiple_of(tile * QUERIES + start + halo, QUERIES)
            write_bias(bias_ref, lo_ref, hi_ref, row, first, span)
            rows = pl.ds(row, QUERIES)
            scores = [mm(k_ref[keys, lanes], split_heads(q_ref[rows, lanes]), NT) for lanes in quads]
            weights = [value.astype(bf16) for value in head_weights(scores, bias_ref[:span])]
            for lanes, value in zip(quads, weights):
                out_ref[to, lanes] = join_heads(mm(value, v_ref[keys, lanes], TN)).astype(bf16)

        by_span(blocks, count, act)
        return carry

    lax.fori_loop(0, out_ref.shape[0] // QUERIES, tile_step, 0)


def lasting(micros):
    return pl.CostEstimate(flops=int(micros * 2e7), bytes_accessed=int(micros * 7e4), transcendentals=0)


def attention(kernel, arrays, outs, scratch, micros, name, mib):
    smem = pl.BlockSpec(memory_space=pltpu.SMEM)
    vmem = pl.BlockSpec(memory_space=pltpu.VMEM)
    return pl.pallas_call(
        kernel,
        out_shape=tuple(jax.ShapeDtypeStruct(shape, dtype) for shape, dtype in outs),
        in_specs=[smem] + [vmem] * (len(arrays) - 1),
        out_specs=(vmem,) * len(outs),
        scratch_shapes=[pltpu.VMEM(shape, dtype) for shape, dtype in scratch],
        compiler_params=pltpu.CompilerParams(vmem_limit_bytes=mib * 2**20),
        cost_estimate=lasting(micros),
        name=name,
    )(*arrays)


def attend_forward(bounds, queries, keys, values, halo, part, parts):
    count, width = keys.shape
    rows = (count - 2 * halo) // parts
    (context,) = attention(
        functools.partial(forward_kernel, halo, part * rows), (*bounds, queries, keys, values),
        [((rows, width), bf16)], [((count, QUAD), f32)], 7, "attend_forward", 30,
    )
    return context


def backward_kernel(halo, start, carried, tiles_ref, lo_ref, hi_ref, q_ref, k_ref, v_ref, g_ref, *refs):
    count = k_ref.shape[0]
    own = count - 2 * halo
    if carried:
        dk_in, dv_in, dq_ref, dk_ref, dv_ref, bias_ref, dk_sum, dv_sum = refs
        dk_sum[...] = dk_in[...]
        dv_sum[...] = dv_in[...]
    else:
        dq_ref, dk_sum, dv_sum, bias_ref = refs
        dk_sum[...] = jnp.zeros_like(dk_sum)
        dv_sum[...] = jnp.zeros_like(dv_sum)
    quads = [pl.ds(i * QUAD, QUAD) for i in range(q_ref.shape[1] // QUAD)]
    low = max(start, halo)

    def tile_step(tile, carry):
        blocks = tiles_ref[2, tile]
        mine = (tile >= halo // QUERIES) & (tile < (halo + own) // QUERIES)

        def act(span):
            first = jnp.minimum(tiles_ref[0, tile], count - span)
            keys = pl.ds(pl.multiple_of(first, ALIGN), span)
            row = pl.multiple_of(tile * QUERIES, QUERIES)
            rows = pl.ds(row, QUERIES)
            write_bias(bias_ref, lo_ref, hi_ref, row, first, span)
            q4 = [split_heads(q_ref[rows, lanes]) for lanes in quads]
            scores = [mm(k_ref[keys, lanes], q, NT) for q, lanes in zip(q4, quads)]
            g4 = [split_heads(g_ref[rows, lanes]) for lanes in quads]
            slopes = [mm(v_ref[keys, lanes], g, NT) for g, lanes in zip(g4, quads)]
            weights = head_weights(scores, bias_ref[:span])
            inner = [jnp.sum(w * s, axis=0, keepdims=True) for w, s in zip(weights, slopes)]
            grads = [(w * (s - i)).astype(bf16) for w, s, i in zip(weights, slopes, inner)]
            for w, g, lanes in zip(weights, g4, quads):
                dv_sum[keys, lanes] += mm(w.astype(bf16), g)
            for d, q, lanes in zip(grads, q4, quads):
                dk_sum[keys, lanes] += mm(d, q)

            @pl.when(mine)
            def _():
                to = pl.ds(pl.multiple_of(row - low, QUERIES), QUERIES)
                for d, lanes in zip(grads, quads):
                    grad = join_heads(mm(d, k_ref[keys, lanes], TN)).astype(bf16)
                    dq_ref[to, lanes] = grad * jnp.asarray(1.0 / math.sqrt(HEAD), bf16)

        by_span(blocks, count, act)
        return carry

    tiles = count // QUERIES // 2
    lax.fori_loop(start // QUERIES, start // QUERIES + tiles, tile_step, 0)
    if carried:
        dk_ref[...] = dk_sum[pl.ds(halo, own), :].astype(bf16)
        dv_ref[...] = dv_sum[pl.ds(halo, own), :].astype(bf16)


def attend_backward(bounds, queries, keys, values, grads, halo, sums):
    count, width = keys.shape
    own = count - 2 * halo
    window = ((count, width), f32)
    outs = [((own // 2, width), bf16)]
    if sums:
        outs, scratch = outs + [((own, width), bf16)] * 2, [((count, QUAD), f32), window, window]
    else:
        outs, scratch = outs + [window, window], [((count, QUAD), f32)]
    return attention(
        functools.partial(backward_kernel, halo, count // 2 if sums else 0, bool(sums)),
        (*bounds, queries, keys, values, grads, *sums), outs, scratch, 16, "attend_backward", 48,
    )


SMEM = pl.BlockSpec(memory_space=pltpu.SMEM)
VMEM = pl.BlockSpec(memory_space=pltpu.VMEM)
PLANE = 8


def local(kernel, place, arrays, outs, scratch, micros, name, mib=20):
    return pl.pallas_call(
        kernel,
        out_shape=tuple(jax.ShapeDtypeStruct(shape, dtype) for shape, dtype in outs),
        in_specs=[SMEM] + [VMEM] * len(arrays),
        out_specs=(VMEM,) * len(outs),
        scratch_shapes=[pltpu.VMEM(shape, dtype) for shape, dtype in scratch],
        compiler_params=pltpu.CompilerParams(vmem_limit_bytes=mib * 2**20),
        cost_estimate=lasting(micros),
        name=name,
    )(place, *arrays)


def own_heads_kernel(place_ref, q_ref, k_ref, v_ref, out_ref, rows_ref):
    place = place_ref[0]
    eighths = q_ref.shape[0] // PLANE
    slabs = q_ref.shape[0] // 8
    for i, ref in enumerate((q_ref, k_ref, v_ref)):
        rows_ref[pl.ds(i * slabs, slabs)] = ref[...].astype(f32).reshape(slabs, 8, -1)
    heads = 3 * eighths // 8
    for j in range(PLANE):
        held = [rows_ref[h * PLANE + (place ^ j)] for h in range(heads)]
        out_ref[j] = jnp.concatenate(held, axis=0).astype(bf16)


def own_units_kernel(place_ref, o_ref, i_ref, b_ref, out_ref, in_ref, back_ref, rows_ref, units_ref):
    place = place_ref[0]
    rows = in_ref.shape[1]
    heads = out_ref.shape[1] // 8
    rows_ref[...] = o_ref[...].astype(f32).reshape(rows_ref.shape)
    units_ref[...] = i_ref[...].astype(f32).T.reshape(units_ref.shape)
    for j in range(PLANE):
        held = [rows_ref[h * PLANE + (place ^ j)] for h in range(heads)]
        out_ref[j] = jnp.concatenate(held, axis=0).astype(bf16)
        in_ref[j] = units_ref[place ^ j].astype(bf16)
        back_ref[j] = b_ref[pl.ds(pl.multiple_of((place ^ j) * rows, rows), rows), :]


def by_eighth(refs):
    first, second = [], []
    for j in range(PLANE):
        far, y, x = j // 4, j // 2 % 2, j % 2
        first.append(refs[4].at[y, x] if far else refs[y].at[x])
        second.append(refs[4].at[2 + x, y] if far else refs[2 + x].at[y])
    return first, second


def eighth_rows(halves, j, member, start, count):
    first, second = halves[0][j], halves[1][j]
    middle = first.shape[1]
    pieces = []
    if start < middle:
        pieces.append(first[member, pl.ds(start, min(count, middle - start)), :])
    if start + count > middle:
        at = max(start, middle)
        pieces.append(second[member, pl.ds(at - middle, start + count - at), :])
    return pieces


def stage_eighths(own_ref, halves, member, start, stage_ref):
    for j in range(PLANE):
        if own_ref is not None and member == 0:
            stage_ref[j] = own_ref[j].astype(f32)
            continue
        at = 0
        of = member if own_ref is None else member - 1
        for piece in eighth_rows(halves, j, of, start, stage_ref.shape[1]):
            stage_ref[j, pl.ds(at, piece.shape[0]), :] = piece.astype(f32)
            at += piece.shape[0]


def head_block(stage_ref, head):
    return jnp.concatenate([stage_ref[j, pl.ds(head * 8, 8), :] for j in range(PLANE)], axis=0)


def project_kernel(
    place_ref, left_ref, tokens_ref, right_ref, own_ref, *refs
):
    halves, refs = by_eighth(refs[:5]), refs[5:]
    bias_ref, q_ref, k_ref, v_ref, w_ref, x_ref, stage_ref = refs
    ways = halves[0][0].shape[0] + 1
    heads = own_ref.shape[1] // 24
    halo = left_ref.shape[0]
    own = tokens_ref.shape[0]
    width = tokens_ref.shape[1]
    inner = heads * HEAD
    x_ref[:halo] = left_ref[...]
    x_ref[pl.ds(halo, own)] = tokens_ref[...]
    x_ref[pl.ds(halo + own, halo)] = right_ref[...]
    for member in range(ways):
        stage_eighths(own_ref, halves, member, 0, stage_ref)
        for kind in range(3):
            blocks = [head_block(stage_ref, kind * heads + h) for h in range(heads)]
            at = kind * width + member * inner
            w_ref[pl.ds(at, inner)] = jnp.concatenate(blocks, axis=0).astype(bf16)

    def step(i, carry):
        rows = pl.ds(pl.multiple_of(i * 256, 256), 256)
        x = x_ref[rows, :]
        q = mm(x, w_ref[:width], NT) + bias_ref[0:1]
        q_ref[rows, :] = (q * (1.0 / math.sqrt(HEAD))).astype(bf16)
        k_ref[rows, :] = mm(x, w_ref[pl.ds(width, width)], NT).astype(bf16)
        v_ref[rows, :] = (mm(x, w_ref[pl.ds(2 * width, width)], NT) + bias_ref[1:2]).astype(bf16)
        return carry

    lax.fori_loop(0, x_ref.shape[0] // 256, step, 0)


def join_units(own_ref, halves, out_ref):
    rows = own_ref.shape[1]
    ways = halves[0][0].shape[0] + 1
    for j in range(PLANE):
        out_ref[pl.ds(j * ways * rows, rows), :] = own_ref[j]
        for member in range(1, ways):
            at = (j * ways + member) * rows
            for piece in eighth_rows(halves, j, member - 1, 0, rows):
                out_ref[pl.ds(at, piece.shape[0]), :] = piece
                at += piece.shape[0]


def join_units_kernel(place_ref, own_ref, *refs):
    join_units(own_ref, by_eighth(refs[:5]), refs[5])


def join_in_out_kernel(place_ref, own_ref, own_out_ref, *refs):
    halves = by_eighth(refs[:5])
    in_ref, out_ref, stage_ref = refs[5:]
    join_units(own_ref, halves, in_ref)
    heads = own_out_ref.shape[1] // 8
    for member in range(halves[0][0].shape[0] + 1):
        stage_eighths(own_out_ref, halves, member, own_ref.shape[1], stage_ref)
        for h in range(heads):
            block = head_block(stage_ref, h)
            out_ref[pl.ds((member * heads + h) * HEAD, HEAD), :] = block.astype(bf16)


def split_digits(values):
    digits = []
    for _ in range(3):
        digits.append(values.astype(bf16))
        values = values - digits[-1].astype(f32)
    return digits


def biases_kernel(place_ref, along_ref, in_ref, q_ref, v_ref, heads_ref, units_ref, line_ref):
    place = place_ref[0]
    ways = along_ref.shape[0] + 1
    inner = q_ref.shape[1]
    rows = in_ref.shape[1] // PLANE
    first = along_ref.shape[1] - 8
    others = along_ref[:, first:, :].astype(f32)
    digits = split_digits(jnp.concatenate([q_ref[...], v_ref[...]], axis=1))
    digits = [digit.astype(f32) for digit in digits]
    for member in range(ways - 1):
        digits.append(others[member, 3:6, : 2 * inner])
    digits = jnp.concatenate(digits, axis=0).astype(bf16)
    lane = lax.broadcasted_iota(jnp.int32, (2 * inner, 2 * inner), 0)
    to = lax.broadcasted_iota(jnp.int32, (2 * inner, 2 * inner), 1)
    chosen = jnp.where((lane ^ (place << 3)) == to, 1.0, 0.0).astype(bf16)
    moved = mm(digits, chosen)
    sums = [moved[3 * m : 3 * m + 1] + moved[3 * m + 1 : 3 * m + 2] + moved[3 * m + 2 : 3 * m + 3] for m in range(ways)]
    heads_ref[0:1] = jnp.concatenate([value[:, :inner] for value in sums], axis=1)
    heads_ref[1:2] = jnp.concatenate([value[:, inner:] for value in sums], axis=1)
    for member in range(ways):
        if member == 0:
            value = in_ref[...]
        else:
            three = others[member - 1]
            value = three[0:1] + three[1:2] + three[2:3]
        for p in range(PLANE):
            line_ref[member * PLANE + p, 0:1, :rows] = value[:, p * rows : (p + 1) * rows]
    held = [
        line_ref[member * PLANE + (place ^ j), 0:1, :rows] for j in range(PLANE) for member in range(ways)
    ]
    units_ref[...] = jnp.concatenate(held, axis=1)


def vectors_kernel(place_ref, *refs):
    stat_refs, (units_ref, out_ref, line_ref) = refs[:6], refs[6:]
    place, own = place_ref[0], place_ref[1]
    ways, _, width = out_ref.shape
    inner = width // ways
    rows = units_ref.shape[1] // PLANE // ways
    for j in range(PLANE):
        for member in range(ways):
            at = j * ways + member
            line_ref[at, 0:1, :rows] = units_ref[:, at * rows : (at + 1) * rows]
    stats = jnp.concatenate([ref[...] for ref in stat_refs], axis=0)
    parts = [stats[:, i * inner : (i + 1) * inner] for i in range(ways)]
    for member in range(ways):
        held = [line_ref[(place ^ p) * ways + member, 0:1, :rows] for p in range(PLANE)]
        mine = parts[0]
        for i in range(1, ways):
            mine = jnp.where((own ^ member) == i, parts[i], mine)
        norms = jnp.concatenate([mine[i : i + 1] for i in range(6)], axis=1)
        norms = jnp.concatenate([norms, jnp.zeros((1, 2 * inner), f32)], axis=1)
        lines = [jnp.concatenate(held, axis=1), norms[:, :width], norms[:, width:]]
        out_ref[member] = jnp.concatenate([*lines, jnp.zeros((5, width), f32)], axis=0)


def put_heads(ways, heads, sum_ref, kind, first_head, block):
    for i in range(block.shape[0] // HEAD):
        member, h = divmod(first_head + i, heads)
        for j in range(PLANE):
            part = block[i * HEAD + j * 8 : i * HEAD + j * 8 + 8]
            sum_ref[j * ways + member, pl.ds((kind * heads + h) * 8, 8), :] = part


def part_pieces(sum_ref, keep_ref, send_ref):
    half = keep_ref.shape[0]
    for i in range(half):
        keep_ref[i] = sum_ref[i].astype(bf16)
        send_ref[i] = sum_ref[half + i].astype(bf16)


def out_grads_kernel(ways, place_ref, context_ref, first_ref, keep_ref, send_ref, sum_ref):
    width = first_ref.shape[1]
    heads = width // ways // HEAD
    sum_ref[:, heads * 8 :, :] = jnp.zeros((PLANE * ways, 8, width), f32)
    put_heads(ways, heads, sum_ref, 0, 0, mm(context_ref[...], first_ref[...], TN))
    part_pieces(sum_ref, keep_ref, send_ref)


def piece_grads_kernel(
    place_ref, dq_first_ref, dq_second_ref, dk_ref, dv_ref, tokens_ref, vectors_ref, keep_ref, send_ref, sum_ref
):
    place = place_ref[0]
    ways = vectors_ref.shape[0]
    width = tokens_ref.shape[1]
    inner = width // ways
    heads = inner // HEAD
    half = dq_first_ref.shape[0]
    block = mm(dq_first_ref[...], tokens_ref[:half], TN) + mm(dq_second_ref[...], tokens_ref[half:], TN)
    put_heads(ways, heads, sum_ref, 0, 0, block)
    put_heads(ways, heads, sum_ref, 1, 0, mm(dk_ref[...], tokens_ref[...], TN))
    put_heads(ways, heads, sum_ref, 2, 0, mm(dv_ref[...], tokens_ref[...], TN))
    lane = lax.broadcasted_iota(jnp.int32, (width, width), 0)
    to = lax.broadcasted_iota(jnp.int32, (width, width), 1)
    member = sum((lane >= i * inner).astype(jnp.int32) for i in range(1, ways))
    within = lane - member * inner
    spot = within ^ (place << 3)
    row = lax.broadcasted_iota(jnp.int32, (8, width), 0)
    column = lax.broadcasted_iota(jnp.int32, (8, width), 1)
    of = sum((column >= i * inner).astype(jnp.int32) for i in range(1, ways))
    ones = jnp.ones((8, tokens_ref.shape[0]), bf16)
    lines = jnp.zeros((8, width), f32)
    sums_of = (
        mm(ones[:, :half], dq_first_ref[...]) + mm(ones[:, :half], dq_second_ref[...]),
        mm(ones, dv_ref[...]),
    )
    for sums, first in zip(sums_of, (width - 2 * inner, width - inner)):
        sums = jnp.where(of == row, sums, 0.0)
        chosen = jnp.where(spot + first == to, 1.0, 0.0).astype(bf16)
        lines = lines + mm(sums.astype(bf16), chosen)
    below = 3 * heads * 8
    for i in range(ways):
        block = vectors_ref[i] + jnp.where(row == 2, lines[i : i + 1], 0.0)
        for j in range(PLANE):
            sum_ref[j * ways + i, pl.ds(below, 8), :] = block
    part_pieces(sum_ref, keep_ref, send_ref)


def gather_heads(place, rows_ref, first, out_ref):
    held = []
    for h in range(out_ref.shape[0] // HEAD):
        for p in range(PLANE):
            held.append(rows_ref[place ^ p, pl.ds(first + h * 8, 8), :])
    out_ref[...] = jnp.concatenate(held, axis=0)


def finish_heads_kernel(place_ref, *refs):
    q_ref, k_ref, v_ref, rows_ref = refs[5:]
    stage_eighths(None, by_eighth(refs[:5]), 0, 0, rows_ref)
    for kind, ref in enumerate((q_ref, k_ref, v_ref)):
        gather_heads(place_ref[0], rows_ref, kind * ref.shape[0] // PLANE, ref)


def finish_units_kernel(place_ref, *refs):
    back_ref, in_ref, out_ref, rows_ref, turned_ref = refs[5:]
    place = place_ref[0]
    rows = back_ref.shape[0] // PLANE
    stage_eighths(None, by_eighth(refs[:5]), 0, 0, rows_ref)
    for p in range(PLANE):
        back_ref[pl.ds(p * rows, rows), :] = rows_ref[place ^ p, :rows, :]
        turned_ref[pl.ds(p * rows, rows), :] = rows_ref[place ^ p, pl.ds(rows, rows), :]
    in_ref[...] = turned_ref[...].T
    gather_heads(place, rows_ref, 2 * rows, out_ref)


def norm_parts(values):
    center = values - jnp.mean(values, axis=-1, keepdims=True)
    spread = jnp.mean(center * center, axis=-1, keepdims=True)
    return center, lax.rsqrt(spread + epsilon)


def norm_pull(grad, unit, inverse, gain):
    scaled = grad * gain
    mean = jnp.mean(scaled, axis=-1, keepdims=True)
    along = jnp.mean(scaled * unit, axis=-1, keepdims=True)
    return inverse * (scaled - mean - unit * along)


def gelu_both(before):
    half = 0.5 * (1.0 + lax.erf(before * math.sqrt(0.5)))
    bell = jnp.exp(-0.5 * before * before) * (1.0 / math.sqrt(2.0 * math.pi))
    return before * half, half + before * bell


def partner(values, step):
    ways = lax.axis_size("mp")
    return lax.ppermute(values, "mp", [(i, i ^ step) for i in range(ways)])


def halo_rows(values, halo):
    ways = lax.axis_size("mp")
    before = lax.ppermute(values[-halo:], "mp", [(i, i + 1) for i in range(ways - 1)])
    after = lax.ppermute(values[:halo], "mp", [(i + 1, i) for i in range(ways - 1)])
    return before, after


def group_tables(table):
    ways = lax.axis_size("mp")
    data_ways = lax.axis_size("dp")
    total = table
    for step in range(1, ways):
        total = total + partner(table, step)
    held = total[None]
    data_index = lax.axis_index("dp")
    level = 1
    while level < data_ways:
        other = lax.ppermute(held, "dp", [(i, i ^ level) for i in range(data_ways)])
        first = (data_index & level) == 0
        held = jnp.where(
            first, jnp.concatenate([held, other]), jnp.concatenate([other, held])
        )
        level *= 2
    return held


CORE, NEAR_X, NEAR_Y = 1, 2, 4


def swap(values, bit):
    ways = lax.axis_size("dp")
    return lax.ppermute(values, "dp", [(i, i ^ bit) for i in range(ways)])


def along(piece):
    return [partner(piece, step) for step in range(1, lax.axis_size("mp"))]


def bit_step(held, level, *gates):
    order = sorted(held)
    other = after(partner(jnp.stack([held[i] for i in order]), level), gates)
    return held | {i | level: other[at] for at, i in enumerate(order)}


def others_of(held):
    return jnp.stack([held[i] for i in sorted(held)[1:]])


def first_step(values, *gates):
    middle = values.shape[1] // 2
    first, second = values[:, :middle], values[:, middle:]
    arrived = after((swap(first, NEAR_X), swap(second, NEAR_Y)), gates)
    return [jnp.stack([first, arrived[0]]), jnp.stack([second, arrived[1]])]


def second_step(pairs, *gates):
    first, second = pairs
    arrived = after((swap(first, NEAR_Y), swap(second, NEAR_X)), gates)
    return [first, arrived[0], second, arrived[1]]


def core_step(held):
    return [*held, swap(jnp.stack(held), CORE)]


def after(value, *others):
    return lax.optimization_barrier((value, others))[0]


def add(first, second):
    return (first.astype(f32) + second.astype(f32)).astype(bf16)


def first_sum_step(sums):
    half = sums.shape[2] // 2
    first, second = sums[:, :, :half], sums[:, :, half:]
    return [(first[0], swap(first[1], NEAR_Y)), (second[:, 0], swap(second[:, 1], NEAR_X))]


def second_sum_step(halves):
    first, second = (add(*half) for half in halves)
    return [(first[0], swap(first[1], NEAR_X)), (second[0], swap(second[1], NEAR_Y))]


def over_groups(total):
    level = PLANE
    while level < lax.axis_size("dp"):
        total = total + swap(total, level)
        level *= 2
    return total


def sum_along(parts):
    total = parts[0].astype(f32)
    for step in range(1, len(parts)):
        total = total + partner(parts[step], step).astype(f32)
    return over_groups(total)


def shards(
    tokens, grad_out, pass_len, labels, w_query, w_key, w_value, b_query, b_value, w_out, b_out,
    ln1_gain, ln1_shift, w_in, b_in, w_back, b_back, ln2_gain, ln2_shift,
):
    ways = lax.axis_size("mp")
    data_ways = lax.axis_size("dp")
    mp_index = lax.axis_index("mp")
    data_index = lax.axis_index("dp")
    own_rows, width = tokens.shape
    rows_here = pass_len.shape[0]
    inner = w_query.shape[1]
    units = w_in.shape[1]
    halo = ROW_LEN // 4
    count = own_rows + 2 * halo
    scale = 1.0 / math.sqrt(HEAD)
    temper = 2.0 / math.sqrt(width)

    piece_rows = units // PLANE
    heads = inner // HEAD
    part = inner // PLANE
    place = jnp.stack([(data_index & CORE) << 2 | (data_index % PLANE) >> 1, mp_index])
    (qkv_own,) = local(
        own_heads_kernel, place, (w_query.T, w_key.T, w_value.T), [((PLANE, 3 * part, width), bf16)],
        [((3 * heads * PLANE, 8, width), f32)], 4, "own_heads",
    )
    biases = jnp.concatenate([b_in, b_query, b_value])
    digits, rest = [], biases
    for _ in range(3):
        digits.append(lax.reduce_precision(rest, 8, 7))
        rest = rest - digits[-1]
    digits = jnp.stack(digits)
    lines = jnp.concatenate(
        [digits[:, :units], jnp.pad(digits[:, units:], ((0, 0), (0, width - 2 * inner)))]
    )
    lines = jnp.pad(lines, ((0, 2), (0, 0))).astype(bf16)
    qkv_along = along(jnp.concatenate([qkv_own[0], lines]))
    tokens_before, tokens_after = halo_rows(tokens, halo)
    w_out, w_in, w_back, place = lax.optimization_barrier((w_out, w_in, w_back, place, qkv_own))[:4]
    out_own, in_own, back_own = local(
        own_units_kernel, place, (w_out, w_in, w_back),
        [((PLANE, part, width), bf16), ((PLANE, piece_rows, width), bf16), ((PLANE, piece_rows, width), bf16)],
        [((heads * PLANE, 8, width), f32), ((PLANE, piece_rows, width), f32)], 5, "own_units",
    )
    in_piece = jnp.concatenate([in_own[0], out_own[0], jnp.zeros((8, width), bf16), back_own[0]])
    in_piece = after(in_piece, qkv_along)
    qkv_along = jnp.stack(qkv_along)
    qkv_pairs = first_step(qkv_along)
    in_held = {0: in_piece}
    level = ways // 2
    while level > 1:
        in_held = bit_step(in_held, level)
        level //= 2
    in_held = after(in_held, qkv_pairs)
    qkv_held = second_step(after(qkv_pairs, tokens_before, tokens_after, in_held))
    in_along = others_of(bit_step(in_held, 1))
    bias_heads, bias_in = local(
        biases_kernel, place, (after(qkv_along, qkv_pairs), b_in[None], b_query[None], b_value[None]),
        [((2, width), f32), ((1, ways * units), f32)], [((ways * PLANE, 8, 128), f32)], 2, "biases",
    )
    start = after(mp_index * own_rows - halo, qkv_pairs)
    bounds = segment_bounds(pass_len, start, halo, own_rows)
    qkv_parts = core_step(after(qkv_held, in_along, bias_heads, bounds))
    in_start = after(in_along, qkv_parts)
    in_rows = piece_rows + part + 8

    tokens_before = after(tokens_before, in_along)
    qkv = (tokens_before, tokens, tokens_after, qkv_own, *qkv_parts, bias_heads)
    queries, keys, values, qkv_all = local(
        project_kernel, place, qkv, [((count, width), bf16)] * 3 + [((3 * width, width), bf16)],
        [((count, width), bf16), ((PLANE, 3 * part, width), f32)], 10, "project", 32,
    )
    in_pairs = first_step(in_start[:, :in_rows], queries)
    context = [attend_forward(bounds, after(queries, in_pairs), keys, values, halo, 0, 2)]
    in_held = second_step(in_pairs, context[0])
    back_start = after(in_start[:, in_rows:], in_held)
    in_parts = core_step(in_held)
    late_queries = after(queries, in_held, back_start, context[0])
    context.append(attend_forward(bounds, late_queries, keys, values, halo, 1, 2))
    context = jnp.concatenate(context)
    in_own = after(in_own, context)
    in_all, out_all = local(
        join_in_out_kernel, place, (in_own, out_own, *in_parts),
        [((ways * units, width), bf16), ((width, width), bf16)],
        [((PLANE, part, width), f32)], 5, "join_in_out",
    )
    attended = mm(context, out_all)
    back_held = second_step(first_step(back_start, context), attended)
    back_parts = core_step(back_held)
    (back_all,) = local(
        join_units_kernel, place, (back_own, *back_parts),
        [((ways * units, width), bf16)], [], 4, "join_back",
    )
    first_sum = tokens.astype(f32) + attended + b_out
    center_one, inverse_one = norm_parts(first_sum)
    unit_one = center_one * inverse_one
    hidden = unit_one * ln1_gain + ln1_shift
    hidden_low = after(hidden.astype(bf16), back_held)

    active, slope = gelu_both(mm(hidden_low, in_all, NT) + bias_in)
    active, slope = lax.optimization_barrier((active.astype(bf16), slope.astype(bf16)))
    second_sum = hidden + mm(active, back_all) + b_back
    center_two, inverse_two = norm_parts(second_sum)
    unit_two = center_two * inverse_two
    mixed = (unit_two * ln2_gain + ln2_shift).astype(bf16)

    query_count = PAIRS * rows_here
    places = cls_places(pass_len) + (jnp.arange(rows_here, dtype=jnp.int32) * ROW_LEN)[:, None]
    table_places = jnp.concatenate([places[:, :PAIRS].reshape(-1), places[:, PAIRS:].reshape(-1)])
    table_places = table_places - mp_index * own_rows
    picker = table_places[:, None] == jnp.arange(own_rows, dtype=jnp.int32)[None, :]
    table = mm(picker.astype(bf16), mixed).astype(bf16)
    digits = jnp.concatenate([labels // 32, labels % 32]).astype(bf16)
    digits = jnp.where(mp_index == 0, digits, 0)
    extra = jnp.zeros((8, width), bf16).at[0, : 2 * query_count].set(digits)
    tables = group_tables(jnp.concatenate([table, extra]))
    all_count = data_ways * query_count
    query_cls = tables[:, :query_count].reshape(all_count, width)
    passage_cls = tables[:, query_count : 2 * query_count].reshape(all_count, width)
    digits = tables[:, 2 * query_count, : 2 * query_count].astype(jnp.int32)
    all_labels = (digits[:, :query_count] * 32 + digits[:, query_count:]).reshape(-1)

    logits = mm(query_cls, passage_cls, NT) * temper
    targets = all_labels[:, None] == jnp.arange(all_count, dtype=jnp.int32)[None, :]
    top = jnp.max(logits, axis=1, keepdims=True)
    raised = jnp.exp(logits - top)
    total = jnp.sum(raised, axis=1, keepdims=True)
    losses = top[:, 0] + jnp.log(total[:, 0]) - jnp.sum(jnp.where(targets, logits, 0.0), axis=1)
    query_losses = lax.dynamic_slice_in_dim(losses, data_index * query_count, query_count)
    grad_logits = (raised / total - targets.astype(f32)) * temper
    rows_of = lax.dynamic_slice_in_dim(grad_logits, data_index * query_count, query_count, 0)
    columns_of = lax.dynamic_slice_in_dim(grad_logits, data_index * query_count, query_count, 1)
    grad_cls = jnp.concatenate(
        [
            jnp.dot(rows_of, passage_cls.astype(f32), precision=highest),
            jnp.dot(columns_of.T, query_cls.astype(f32), precision=highest),
        ]
    )
    grad_mixed = grad_out.astype(f32) + jnp.dot(
        picker.astype(f32).T, grad_cls, precision=highest
    )

    grad_second = norm_pull(grad_mixed, unit_two, inverse_two, ln2_gain)
    stats = [
        jnp.sum(grad_mixed * unit_two, axis=0, keepdims=True),
        jnp.sum(grad_mixed, axis=0, keepdims=True),
        jnp.sum(grad_second, axis=0, keepdims=True),
    ]
    second_low = grad_second.astype(bf16)

    def to_core(left, right):
        return mm(left[:, left.shape[1] // 2 :], right, TN).astype(bf16)

    def chip_sum(left, right, arrived):
        own = mm(left[:, : left.shape[1] // 2], right, TN)
        return add(own, arrived).reshape(2, 2, ways, piece_rows, width)

    back_sent = to_core(active, second_low)
    back_arrived = swap(back_sent, CORE)
    pulled, back_sent = lax.optimization_barrier((second_low, back_sent))
    grad_before = (mm(pulled, back_all, NT) * slope.astype(f32)).astype(bf16)
    back_sum = chip_sum(active, second_low, back_arrived)
    back_half = swap(back_sum[1], NEAR_Y)
    in_sent = to_core(grad_before, hidden_low)
    in_arrived = swap(in_sent, CORE)
    pulled = after(grad_before, back_sum, in_sent)
    grad_hidden = grad_second + mm(pulled, in_all)
    grad_first = norm_pull(grad_hidden, unit_one, inverse_one, ln1_gain)
    stats += [
        jnp.sum(grad_hidden * unit_one, axis=0, keepdims=True),
        jnp.sum(grad_hidden, axis=0, keepdims=True),
        jnp.sum(grad_first, axis=0, keepdims=True),
    ]
    first_low = grad_first.astype(bf16)
    first_before, first_after = halo_rows(first_low, halo)
    in_sum = chip_sum(after(grad_before, first_low), hidden_low, in_arrived)
    in_half = swap(in_sum[:, 1], NEAR_X)
    out_keep, out_sent = local(
        functools.partial(out_grads_kernel, ways), place, (context, first_low),
        [((4 * ways, part + 8, width), bf16)] * 2, [((8 * ways, part + 8, width), f32)], 3, "out_grads",
    )
    out_sum = add(out_keep, swap(out_sent, CORE)).reshape(2, 2, ways, part + 8, width)
    out_half = swap(out_sum[1], NEAR_Y)

    d_b_in = jnp.sum(grad_before, axis=0, dtype=f32, keepdims=True)
    (vectors,) = local(
        vectors_kernel, place, (*stats, d_b_in), [((ways, 8, width), f32)],
        [((ways * PLANE, 8, 128), f32)], 2, "vectors",
    )

    first_before, first_after = after((first_before, first_after), in_sum, out_sent, vectors)
    first_window = jnp.concatenate([first_before, first_low, first_after])
    grad_context = mm(first_window, out_all, NT).astype(bf16)
    grad_context = after(grad_context, in_sum, back_sum, out_sum, vectors)
    grad_query, *sums = attend_backward(bounds, queries, keys, values, grad_context, halo, ())
    back_half, in_half, out_half = after((back_half, in_half, out_half), grad_query)
    back_sum = add(back_sum[0], back_half)
    in_sum = add(in_sum[:, 0], in_half)
    out_sum = add(out_sum[0], out_half)
    back_half = swap(back_sum[1], NEAR_X)
    in_half = swap(in_sum[1], NEAR_Y)
    out_half = swap(out_sum[1], NEAR_X)
    grad_context = after(grad_context, back_sum, in_sum, out_sum, grad_query)
    late_query, grad_keys, grad_values = attend_backward(
        bounds, queries, keys, values, grad_context, halo, sums
    )
    halves = [(back_sum[0], back_half), (in_sum[0], in_half), (out_sum[0], out_half)]
    halves = after(halves, late_query)
    early_sum = jnp.concatenate([add(*half) for half in halves], axis=1)
    early_parts = [early_sum[i] for i in range(ways)]
    early_odd = jnp.stack(early_parts[1::2])
    tokens_low, early_odd = lax.optimization_barrier((tokens, early_odd))
    early_odd = partner(early_odd, 1)

    late_rows = 3 * part + 8
    late_keep, late_sent = local(
        piece_grads_kernel, place, (grad_query, late_query, grad_keys, grad_values, tokens_low, vectors),
        [((4 * ways, late_rows, width), bf16)] * 2, [((8 * ways, late_rows, width), f32)], 8, "piece_grads", 36,
    )
    late_sum = add(late_keep, swap(late_sent, CORE)).reshape(2, 2, ways, late_rows, width)
    halves = first_sum_step(late_sum)
    early_odd = after(early_odd, late_sum)
    early_parts = [add(even, odd) for even, odd in zip(early_parts[::2], early_odd)]
    halves = second_sum_step(halves)
    late_parts = [half[i] for half in (add(*h) for h in halves) for i in range(ways // 2)]
    level, early_own = 2, early_parts[0].astype(f32)
    while level < ways:
        early_own = early_own + after(partner(early_parts[level // 2], level), late_parts).astype(f32)
        level *= 2
    late_total = sum_along(late_parts)
    early_held = second_step(first_step(over_groups(early_own).astype(bf16)[None], late_total))
    grad_queries = jnp.concatenate([grad_query, late_query])
    d_tokens = (
        grad_first
        + mm(grad_queries, qkv_all[:width])
        + mm(grad_keys, qkv_all[width : 2 * width])
        + mm(grad_values, qkv_all[2 * width :])
    )
    late_held = first_step(late_total.astype(bf16)[None])
    early_pieces = core_step(after(early_held, late_held))
    late_pieces = core_step(second_step(late_held, d_tokens))
    line = late_total[3 * part :]

    d_query, d_key, d_value = local(
        finish_heads_kernel, place, late_pieces, [((inner, width), f32)] * 3,
        [((PLANE, 3 * part, width), f32)], 4, "finish_heads",
    )
    d_back, d_in, d_out = local(
        finish_units_kernel, place, early_pieces,
        [((units, width), f32), ((width, units), f32), ((inner, width), f32)],
        [((PLANE, 2 * piece_rows + part + 8, width), f32), ((units, width), f32)], 6, "finish_units",
    )
    norms = [line[1 + i // ways, i % ways * inner : (i % ways + 1) * inner] for i in range(8)]
    return (
        mixed,
        query_losses,
        d_tokens,
        d_query.T,
        d_key.T,
        d_value.T,
        norms[6],
        norms[7],
        d_out,
        norms[5],
        norms[3],
        norms[4],
        d_in,
        line[0],
        d_back,
        norms[2],
        norms[0],
        norms[1],
    )


def solution(mesh):
    return jax.shard_map(
        shards,
        mesh=mesh,
        in_specs=(
            P(("dp", "mp"), None), P(("dp", "mp"), None), P("dp", None), P("dp"),
            P(None, "mp"), P(None, "mp"), P(None, "mp"), P("mp"), P("mp"), P("mp", None), P(),
            P(), P(), P(None, "mp"), P("mp"), P("mp", None), P(), P(), P(),
        ),
        out_specs=(
            P(("dp", "mp"), None), P("dp"), P(("dp", "mp"), None),
            P(None, "mp"), P(None, "mp"), P(None, "mp"), P("mp"), P("mp"), P("mp", None),
            P("mp"), P("mp"), P("mp"), P(None, "mp"), P("mp"), P("mp", None), P("mp"), P("mp"), P("mp"),
        ),
        check_vma=False,
    )
```

```python
import functools
import math

import jax
import jax.numpy as jnp
from jax import lax
from jax.experimental import pallas as pl
from jax.experimental.pallas import tpu as pltpu
from jax.sharding import PartitionSpec as P

HEAD = 64
ROW_LEN = 1024
PAIRS = 4
QLEN = 32
TILE = 128
QUERIES = 64
QUAD = 4 * HEAD
FIRST = 14 * QUERIES
ALIGN = 32
BLOCKS = (1, 2, 3, 4, 5, 7, 10)

epsilon = 1e-12
masked_score = -1e30
highest = lax.Precision.HIGHEST
f32 = jnp.float32
bf16 = jnp.bfloat16
NT = (((1,), (1,)), ((), ()))
TN = (((0,), (0,)), ((), ()))
NN = (((1,), (0,)), ((), ()))


def mm(a, b, dims=NN):
    return lax.dot_general(a, b, dims, preferred_element_type=f32)


def bounds_kernel(halo, own, start_ref, pass_ref, tiles_ref, low_ref, high_ref):
    start = start_ref[0]
    count = low_ref.shape[1]
    rows = pass_ref.shape[0]
    last = rows * ROW_LEN
    cuts = []
    for row in range(rows):
        cuts += [jnp.int32(row * ROW_LEN + j * QLEN) for j in range(PAIRS + 1)]
        for j in range(PAIRS):
            cuts.append(cuts[-1] + pass_ref[row, j])

    def low_of(place):
        low = jnp.full_like(place, start)
        for cut in cuts:
            low = jnp.where(cut <= place, cut, low)
        return jnp.clip(jnp.where(place >= last, last, low) - start, 0, count)

    def high_of(place):
        high = jnp.full_like(place, last)
        for cut in reversed(cuts):
            high = jnp.where(cut > place, cut, high)
        return jnp.clip(jnp.where(place >= last, start + count, high) - start, 0, count)

    place = start + lax.broadcasted_iota(jnp.int32, (1, count), 1)
    low_ref[...] = low_of(place)
    high_ref[...] = high_of(place)
    for tile in range(count // QUERIES):
        at = tile * QUERIES
        first = low_of(start + at)
        after_last = high_of(start + at + QUERIES - 1)
        low = first // ALIGN * ALIGN
        blocks = (after_last - low + TILE - 1) // TILE
        tiles_ref[0, tile] = low
        tiles_ref[1, tile] = blocks
        if at < halo:
            blocks = jnp.where(after_last > halo, blocks, 0)
        if at >= halo + own:
            blocks = jnp.where(first < halo + own, blocks, 0)
        tiles_ref[2, tile] = blocks


def segment_bounds(pass_len, start, halo, own):
    count = own + 2 * halo
    smem = pl.BlockSpec(memory_space=pltpu.SMEM)
    vmem = pl.BlockSpec(memory_space=pltpu.VMEM)
    line = jax.ShapeDtypeStruct((1, count), jnp.int32)
    return pl.pallas_call(
        functools.partial(bounds_kernel, halo, own),
        out_shape=(jax.ShapeDtypeStruct((3, count // QUERIES), jnp.int32), line, line),
        in_specs=[smem, smem],
        out_specs=(smem, vmem, vmem),
        compiler_params=pltpu.CompilerParams(vmem_limit_bytes=8 * 2**20),
        name="bounds",
    )(start.reshape(1), pass_len)


def cls_places(pass_len):
    lens = [pass_len[:, j] for j in range(PAIRS)]
    starts = [jnp.full_like(lens[0], j * QLEN) for j in range(PAIRS)]
    at = jnp.full_like(lens[0], PAIRS * QLEN)
    for j in range(PAIRS):
        starts.append(at)
        at = at + lens[j]
    return jnp.stack(starts, axis=1)


def by_span(blocks, count, act):
    least = 0
    for size in BLOCKS:
        if size * TILE > count:
            break

        @pl.when((blocks > least) & (blocks <= size))
        def _(size=size):
            act(size * TILE)

        least = size


def head_of(shape):
    return lax.broadcasted_iota(jnp.int32, shape, 1) // HEAD


def split_heads(block):
    head = head_of(block.shape)
    zero = jnp.zeros_like(block)
    return jnp.concatenate([jnp.where(head == h, block, zero) for h in range(4)], axis=0)


def join_heads(stacked):
    rows = stacked.shape[0] // 4
    head = head_of((rows, stacked.shape[1]))
    out = stacked[:rows]
    for h in range(1, 4):
        out = jnp.where(head == h, stacked[h * rows : (h + 1) * rows], out)
    return out


def four_times(ref, row):
    line = ref[:, pl.ds(pl.multiple_of(row // TILE * TILE, TILE), TILE)]
    turned = jnp.concatenate([line[:, QUERIES:], line[:, :QUERIES]], axis=1)
    lane = lax.broadcasted_iota(jnp.int32, line.shape, 1)
    odd = row % TILE >= QUERIES
    both = jnp.where((lane < QUERIES) != odd, line, turned)
    return jnp.concatenate([both, both], axis=1)


def write_bias(bias_ref, lo_ref, hi_ref, row, first, span):
    place = lax.broadcasted_iota(jnp.int32, (span, QUAD), 0) + first
    inside = (place >= four_times(lo_ref, row)) & (place < four_times(hi_ref, row))
    bias_ref[:span] = jnp.where(inside, 0.0, masked_score)


def head_weights(scores, bias):
    scores = [score + bias for score in scores]
    tops = [jnp.max(score, axis=0, keepdims=True) for score in scores]
    raised = [jnp.exp(score - top) for score, top in zip(scores, tops)]
    inverses = [1.0 / jnp.sum(value, axis=0, keepdims=True) for value in raised]
    return [value * inverse for value, inverse in zip(raised, inverses)]


def forward_kernel(halo, start, tiles_ref, lo_ref, hi_ref, q_ref, k_ref, v_ref, out_ref, bias_ref):
    count = k_ref.shape[0]
    quads = [pl.ds(i * QUAD, QUAD) for i in range(q_ref.shape[1] // QUAD)]

    def tile_step(tile, carry):
        here = tile + (start + halo) // QUERIES
        blocks = tiles_ref[1, here]

        def act(span):
            first = jnp.minimum(tiles_ref[0, here], count - span)
            keys = pl.ds(pl.multiple_of(first, ALIGN), span)
            to = pl.ds(pl.multiple_of(tile * QUERIES, QUERIES), QUERIES)
            row = pl.multiple_of(tile * QUERIES + start + halo, QUERIES)
            write_bias(bias_ref, lo_ref, hi_ref, row, first, span)
            rows = pl.ds(row, QUERIES)
            scores = [mm(k_ref[keys, lanes], split_heads(q_ref[rows, lanes]), NT) for lanes in quads]
            weights = [value.astype(bf16) for value in head_weights(scores, bias_ref[:span])]
            for lanes, value in zip(quads, weights):
                out_ref[to, lanes] = join_heads(mm(value, v_ref[keys, lanes], TN)).astype(bf16)

        by_span(blocks, count, act)
        return carry

    lax.fori_loop(0, out_ref.shape[0] // QUERIES, tile_step, 0)


def lasting(micros):
    return pl.CostEstimate(flops=int(micros * 2e7), bytes_accessed=int(micros * 7e4), transcendentals=0)


def attention(kernel, arrays, outs, scratch, micros, name, mib):
    smem = pl.BlockSpec(memory_space=pltpu.SMEM)
    vmem = pl.BlockSpec(memory_space=pltpu.VMEM)
    return pl.pallas_call(
        kernel,
        out_shape=tuple(jax.ShapeDtypeStruct(shape, dtype) for shape, dtype in outs),
        in_specs=[smem] + [vmem] * (len(arrays) - 1),
        out_specs=(vmem,) * len(outs),
        scratch_shapes=[pltpu.VMEM(shape, dtype) for shape, dtype in scratch],
        compiler_params=pltpu.CompilerParams(vmem_limit_bytes=mib * 2**20),
        cost_estimate=lasting(micros),
        name=name,
    )(*arrays)


def attend_forward(bounds, queries, keys, values, halo, part, parts):
    count, width = keys.shape
    rows = (count - 2 * halo) // parts
    (context,) = attention(
        functools.partial(forward_kernel, halo, part * rows), (*bounds, queries, keys, values),
        [((rows, width), bf16)], [((count, QUAD), f32)], 7, "attend_forward", 14,
    )
    return context


def backward_kernel(halo, start, carried, tiles_ref, lo_ref, hi_ref, q_ref, k_ref, v_ref, g_ref, *refs):
    count = k_ref.shape[0]
    own = count - 2 * halo
    if carried:
        dk_in, dv_in, dq_ref, dk_ref, dv_ref, bias_ref, dk_sum, dv_sum = refs
        dk_sum[...] = dk_in[...]
        dv_sum[...] = dv_in[...]
    else:
        dq_ref, dk_sum, dv_sum, bias_ref = refs
        dk_sum[...] = jnp.zeros_like(dk_sum)
        dv_sum[...] = jnp.zeros_like(dv_sum)
    quads = [pl.ds(i * QUAD, QUAD) for i in range(q_ref.shape[1] // QUAD)]
    low = max(start, halo)

    def tile_step(tile, carry):
        blocks = tiles_ref[2, tile]
        mine = (tile >= halo // QUERIES) & (tile < (halo + own) // QUERIES)

        def act(span):
            first = jnp.minimum(tiles_ref[0, tile], count - span)
            keys = pl.ds(pl.multiple_of(first, ALIGN), span)
            row = pl.multiple_of(tile * QUERIES, QUERIES)
            rows = pl.ds(row, QUERIES)
            write_bias(bias_ref, lo_ref, hi_ref, row, first, span)
            q4 = [split_heads(q_ref[rows, lanes]) for lanes in quads]
            scores = [mm(k_ref[keys, lanes], q, NT) for q, lanes in zip(q4, quads)]
            g4 = [split_heads(g_ref[rows, lanes]) for lanes in quads]
            slopes = [mm(v_ref[keys, lanes], g, NT) for g, lanes in zip(g4, quads)]
            weights = head_weights(scores, bias_ref[:span])
            inner = [jnp.sum(w * s, axis=0, keepdims=True) for w, s in zip(weights, slopes)]
            grads = [(w * (s - i)).astype(bf16) for w, s, i in zip(weights, slopes, inner)]
            for w, g, lanes in zip(weights, g4, quads):
                dv_sum[keys, lanes] += mm(w.astype(bf16), g)
            for d, q, lanes in zip(grads, q4, quads):
                dk_sum[keys, lanes] += mm(d, q)

            @pl.when(mine)
            def _():
                to = pl.ds(pl.multiple_of(row - low, QUERIES), QUERIES)
                for d, lanes in zip(grads, quads):
                    grad = join_heads(mm(d, k_ref[keys, lanes], TN)).astype(bf16)
                    dq_ref[to, lanes] = grad * jnp.asarray(1.0 / math.sqrt(HEAD), bf16)

        by_span(blocks, count, act)
        return carry

    end = count if carried else FIRST
    lax.fori_loop(start // QUERIES, end // QUERIES, tile_step, 0)
    if carried:
        dk_ref[...] = dk_sum[pl.ds(halo, own), :].astype(bf16)
        dv_ref[...] = dv_sum[pl.ds(halo, own), :].astype(bf16)


def attend_backward(bounds, queries, keys, values, grads, halo, sums):
    count, width = keys.shape
    own = count - 2 * halo
    window = ((count, width), f32)
    rows = halo + own - FIRST if sums else FIRST - halo
    outs = [((rows, width), bf16)]
    if sums:
        outs, scratch = outs + [((own, width), bf16)] * 2, [((count, QUAD), f32), window, window]
    else:
        outs, scratch = outs + [window, window], [((count, QUAD), f32)]
    return attention(
        functools.partial(backward_kernel, halo, FIRST if sums else 0, bool(sums)),
        (*bounds, queries, keys, values, grads, *sums), outs, scratch, 16, "attend_backward", 28,
    )


SMEM = pl.BlockSpec(memory_space=pltpu.SMEM)
VMEM = pl.BlockSpec(memory_space=pltpu.VMEM)
PLANE = 8


def local(kernel, place, arrays, outs, scratch, micros, name, mib=20):
    return pl.pallas_call(
        kernel,
        out_shape=tuple(jax.ShapeDtypeStruct(shape, dtype) for shape, dtype in outs),
        in_specs=[SMEM] + [VMEM] * len(arrays),
        out_specs=(VMEM,) * len(outs),
        scratch_shapes=[pltpu.VMEM(shape, dtype) for shape, dtype in scratch],
        compiler_params=pltpu.CompilerParams(vmem_limit_bytes=mib * 2**20),
        cost_estimate=lasting(micros),
        name=name,
    )(place, *arrays)


def own_heads_kernel(place_ref, q_ref, k_ref, v_ref, out_ref, rows_ref):
    place = place_ref[0]
    eighths = q_ref.shape[0] // PLANE
    slabs = q_ref.shape[0] // 8
    for i, ref in enumerate((q_ref, k_ref, v_ref)):
        rows_ref[pl.ds(i * slabs, slabs)] = ref[...].astype(f32).reshape(slabs, 8, -1)
    heads = 3 * eighths // 8
    for j in range(PLANE):
        held = [rows_ref[h * PLANE + (place ^ j)] for h in range(heads)]
        out_ref[j] = jnp.concatenate(held, axis=0).astype(bf16)


def own_units_kernel(place_ref, o_ref, i_ref, b_ref, out_ref, in_ref, back_ref, rows_ref, units_ref):
    place = place_ref[0]
    rows = in_ref.shape[1]
    heads = out_ref.shape[1] // 8
    rows_ref[...] = o_ref[...].astype(f32).reshape(rows_ref.shape)
    units_ref[...] = i_ref[...].astype(f32).T.reshape(units_ref.shape)
    for j in range(PLANE):
        held = [rows_ref[h * PLANE + (place ^ j)] for h in range(heads)]
        out_ref[j] = jnp.concatenate(held, axis=0).astype(bf16)
        in_ref[j] = units_ref[place ^ j].astype(bf16)
        back_ref[j] = b_ref[pl.ds(pl.multiple_of((place ^ j) * rows, rows), rows), :]


def by_eighth(refs):
    first, second = [], []
    for j in range(PLANE):
        far, y, x = j // 4, j // 2 % 2, j % 2
        first.append(refs[4].at[y, x] if far else refs[y].at[x])
        second.append(refs[4].at[2 + x, y] if far else refs[2 + x].at[y])
    return first, second


def eighth_rows(halves, j, member, start, count):
    first, second = halves[0][j], halves[1][j]
    middle = first.shape[1]
    pieces = []
    if start < middle:
        pieces.append(first[member, pl.ds(start, min(count, middle - start)), :])
    if start + count > middle:
        at = max(start, middle)
        pieces.append(second[member, pl.ds(at - middle, start + count - at), :])
    return pieces


def stage_eighths(own_ref, halves, member, start, stage_ref):
    for j in range(PLANE):
        if own_ref is not None and member == 0:
            stage_ref[j] = own_ref[j].astype(f32)
            continue
        at = 0
        of = member if own_ref is None else member - 1
        for piece in eighth_rows(halves, j, of, start, stage_ref.shape[1]):
            stage_ref[j, pl.ds(at, piece.shape[0]), :] = piece.astype(f32)
            at += piece.shape[0]


def head_block(stage_ref, head):
    return jnp.concatenate([stage_ref[j, pl.ds(head * 8, 8), :] for j in range(PLANE)], axis=0)


def project_kernel(
    place_ref, left_ref, tokens_ref, right_ref, own_ref, *refs
):
    halves, refs = by_eighth(refs[:5]), refs[5:]
    bias_ref, q_ref, k_ref, v_ref, w_ref, x_ref, stage_ref = refs
    ways = halves[0][0].shape[0] + 1
    heads = own_ref.shape[1] // 24
    halo = left_ref.shape[0]
    own = tokens_ref.shape[0]
    width = tokens_ref.shape[1]
    inner = heads * HEAD
    x_ref[:halo] = left_ref[...]
    x_ref[pl.ds(halo, own)] = tokens_ref[...]
    x_ref[pl.ds(halo + own, halo)] = right_ref[...]
    for member in range(ways):
        stage_eighths(own_ref, halves, member, 0, stage_ref)
        for kind in range(3):
            blocks = [head_block(stage_ref, kind * heads + h) for h in range(heads)]
            at = kind * width + member * inner
            w_ref[pl.ds(at, inner)] = jnp.concatenate(blocks, axis=0).astype(bf16)

    def step(i, carry):
        rows = pl.ds(pl.multiple_of(i * 256, 256), 256)
        x = x_ref[rows, :]
        q = mm(x, w_ref[:width], NT) + bias_ref[0:1]
        q_ref[rows, :] = (q * (1.0 / math.sqrt(HEAD))).astype(bf16)
        k_ref[rows, :] = mm(x, w_ref[pl.ds(width, width)], NT).astype(bf16)
        v_ref[rows, :] = (mm(x, w_ref[pl.ds(2 * width, width)], NT) + bias_ref[1:2]).astype(bf16)
        return carry

    lax.fori_loop(0, x_ref.shape[0] // 256, step, 0)


def join_units(own_ref, halves, out_ref):
    rows = own_ref.shape[1]
    ways = halves[0][0].shape[0] + 1
    for j in range(PLANE):
        out_ref[pl.ds(j * ways * rows, rows), :] = own_ref[j]
        for member in range(1, ways):
            at = (j * ways + member) * rows
            for piece in eighth_rows(halves, j, member - 1, 0, rows):
                out_ref[pl.ds(at, piece.shape[0]), :] = piece
                at += piece.shape[0]


def join_units_kernel(place_ref, own_ref, *refs):
    join_units(own_ref, by_eighth(refs[:5]), refs[5])


def join_in_out_kernel(place_ref, own_ref, own_out_ref, *refs):
    halves = by_eighth(refs[:5])
    in_ref, out_ref, stage_ref = refs[5:]
    join_units(own_ref, halves, in_ref)
    heads = own_out_ref.shape[1] // 8
    for member in range(halves[0][0].shape[0] + 1):
        stage_eighths(own_out_ref, halves, member, own_ref.shape[1], stage_ref)
        for h in range(heads):
            block = head_block(stage_ref, h)
            out_ref[pl.ds((member * heads + h) * HEAD, HEAD), :] = block.astype(bf16)


def split_digits(values):
    digits = []
    for _ in range(3):
        digits.append(values.astype(bf16))
        values = values - digits[-1].astype(f32)
    return digits


def biases_kernel(place_ref, along_ref, in_ref, q_ref, v_ref, heads_ref, units_ref, line_ref):
    place = place_ref[0]
    ways = along_ref.shape[0] + 1
    inner = q_ref.shape[1]
    rows = in_ref.shape[1] // PLANE
    first = along_ref.shape[1] - 8
    others = along_ref[:, first:, :].astype(f32)
    digits = split_digits(jnp.concatenate([q_ref[...], v_ref[...]], axis=1))
    digits = [digit.astype(f32) for digit in digits]
    for member in range(ways - 1):
        digits.append(others[member, 3:6, : 2 * inner])
    digits = jnp.concatenate(digits, axis=0).astype(bf16)
    lane = lax.broadcasted_iota(jnp.int32, (2 * inner, 2 * inner), 0)
    to = lax.broadcasted_iota(jnp.int32, (2 * inner, 2 * inner), 1)
    chosen = jnp.where((lane ^ (place << 3)) == to, 1.0, 0.0).astype(bf16)
    moved = mm(digits, chosen)
    sums = [moved[3 * m : 3 * m + 1] + moved[3 * m + 1 : 3 * m + 2] + moved[3 * m + 2 : 3 * m + 3] for m in range(ways)]
    heads_ref[0:1] = jnp.concatenate([value[:, :inner] for value in sums], axis=1)
    heads_ref[1:2] = jnp.concatenate([value[:, inner:] for value in sums], axis=1)
    for member in range(ways):
        if member == 0:
            value = in_ref[...]
        else:
            three = others[member - 1]
            value = three[0:1] + three[1:2] + three[2:3]
        for p in range(PLANE):
            line_ref[member * PLANE + p, 0:1, :rows] = value[:, p * rows : (p + 1) * rows]
    held = [
        line_ref[member * PLANE + (place ^ j), 0:1, :rows] for j in range(PLANE) for member in range(ways)
    ]
    units_ref[...] = jnp.concatenate(held, axis=1)


def vectors_kernel(place_ref, *refs):
    stat_refs, (units_ref, out_ref, line_ref) = refs[:6], refs[6:]
    place, own = place_ref[0], place_ref[1]
    ways, _, width = out_ref.shape
    inner = width // ways
    rows = units_ref.shape[1] // PLANE // ways
    for j in range(PLANE):
        for member in range(ways):
            at = j * ways + member
            line_ref[at, 0:1, :rows] = units_ref[:, at * rows : (at + 1) * rows]
    stats = jnp.concatenate([ref[...] for ref in stat_refs], axis=0)
    parts = [stats[:, i * inner : (i + 1) * inner] for i in range(ways)]
    for member in range(ways):
        held = [line_ref[(place ^ p) * ways + member, 0:1, :rows] for p in range(PLANE)]
        mine = parts[0]
        for i in range(1, ways):
            mine = jnp.where((own ^ member) == i, parts[i], mine)
        norms = jnp.concatenate([mine[i : i + 1] for i in range(6)], axis=1)
        norms = jnp.concatenate([norms, jnp.zeros((1, 2 * inner), f32)], axis=1)
        lines = [jnp.concatenate(held, axis=1), norms[:, :width], norms[:, width:]]
        out_ref[member] = jnp.concatenate([*lines, jnp.zeros((5, width), f32)], axis=0)


def put_heads(ways, heads, sum_ref, kind, first_head, block):
    for i in range(block.shape[0] // HEAD):
        member, h = divmod(first_head + i, heads)
        for j in range(PLANE):
            part = block[i * HEAD + j * 8 : i * HEAD + j * 8 + 8]
            sum_ref[j * ways + member, pl.ds((kind * heads + h) * 8, 8), :] = part


def part_pieces(sum_ref, keep_ref, send_ref):
    half = keep_ref.shape[0]
    for i in range(half):
        keep_ref[i] = sum_ref[i].astype(bf16)
        send_ref[i] = sum_ref[half + i].astype(bf16)


def out_grads_kernel(ways, place_ref, context_ref, first_ref, keep_ref, send_ref, sum_ref):
    width = first_ref.shape[1]
    heads = width // ways // HEAD
    sum_ref[:, heads * 8 :, :] = jnp.zeros((PLANE * ways, 8, width), f32)
    put_heads(ways, heads, sum_ref, 0, 0, mm(context_ref[...], first_ref[...], TN))
    part_pieces(sum_ref, keep_ref, send_ref)


def piece_grads_kernel(
    place_ref, dq_first_ref, dq_second_ref, dk_ref, dv_ref, tokens_ref, vectors_ref, keep_ref, send_ref, sum_ref
):
    place = place_ref[0]
    ways = vectors_ref.shape[0]
    width = tokens_ref.shape[1]
    inner = width // ways
    heads = inner // HEAD
    half = dq_first_ref.shape[0]
    block = mm(dq_first_ref[...], tokens_ref[:half], TN) + mm(dq_second_ref[...], tokens_ref[half:], TN)
    put_heads(ways, heads, sum_ref, 0, 0, block)
    put_heads(ways, heads, sum_ref, 1, 0, mm(dk_ref[...], tokens_ref[...], TN))
    put_heads(ways, heads, sum_ref, 2, 0, mm(dv_ref[...], tokens_ref[...], TN))
    lane = lax.broadcasted_iota(jnp.int32, (width, width), 0)
    to = lax.broadcasted_iota(jnp.int32, (width, width), 1)
    member = sum((lane >= i * inner).astype(jnp.int32) for i in range(1, ways))
    within = lane - member * inner
    spot = within ^ (place << 3)
    row = lax.broadcasted_iota(jnp.int32, (8, width), 0)
    column = lax.broadcasted_iota(jnp.int32, (8, width), 1)
    of = sum((column >= i * inner).astype(jnp.int32) for i in range(1, ways))
    ones = jnp.ones((8, tokens_ref.shape[0]), bf16)
    lines = jnp.zeros((8, width), f32)
    sums_of = (
        mm(ones[:, :half], dq_first_ref[...]) + mm(ones[:, half:], dq_second_ref[...]),
        mm(ones, dv_ref[...]),
    )
    for sums, first in zip(sums_of, (width - 2 * inner, width - inner)):
        sums = jnp.where(of == row, sums, 0.0)
        chosen = jnp.where(spot + first == to, 1.0, 0.0).astype(bf16)
        lines = lines + mm(sums.astype(bf16), chosen)
    below = 3 * heads * 8
    for i in range(ways):
        block = vectors_ref[i] + jnp.where(row == 2, lines[i : i + 1], 0.0)
        for j in range(PLANE):
            sum_ref[j * ways + i, pl.ds(below, 8), :] = block
    part_pieces(sum_ref, keep_ref, send_ref)


def gather_heads(place, rows_ref, first, out_ref):
    held = []
    for h in range(out_ref.shape[0] // HEAD):
        for p in range(PLANE):
            held.append(rows_ref[place ^ p, pl.ds(first + h * 8, 8), :])
    out_ref[...] = jnp.concatenate(held, axis=0)


def finish_heads_kernel(place_ref, *refs):
    q_ref, k_ref, v_ref, rows_ref = refs[5:]
    stage_eighths(None, by_eighth(refs[:5]), 0, 0, rows_ref)
    for kind, ref in enumerate((q_ref, k_ref, v_ref)):
        gather_heads(place_ref[0], rows_ref, kind * ref.shape[0] // PLANE, ref)


def finish_units_kernel(place_ref, *refs):
    back_ref, in_ref, out_ref, rows_ref, turned_ref = refs[5:]
    place = place_ref[0]
    rows = back_ref.shape[0] // PLANE
    stage_eighths(None, by_eighth(refs[:5]), 0, 0, rows_ref)
    for p in range(PLANE):
        back_ref[pl.ds(p * rows, rows), :] = rows_ref[place ^ p, :rows, :]
        turned_ref[pl.ds(p * rows, rows), :] = rows_ref[place ^ p, pl.ds(rows, rows), :]
    in_ref[...] = turned_ref[...].T
    gather_heads(place, rows_ref, 2 * rows, out_ref)


def norm_parts(values):
    center = values - jnp.mean(values, axis=-1, keepdims=True)
    spread = jnp.mean(center * center, axis=-1, keepdims=True)
    return center, lax.rsqrt(spread + epsilon)


def norm_pull(grad, unit, inverse, gain):
    scaled = grad * gain
    mean = jnp.mean(scaled, axis=-1, keepdims=True)
    along = jnp.mean(scaled * unit, axis=-1, keepdims=True)
    return inverse * (scaled - mean - unit * along)


def gelu_both(before):
    half = 0.5 * (1.0 + lax.erf(before * math.sqrt(0.5)))
    bell = jnp.exp(-0.5 * before * before) * (1.0 / math.sqrt(2.0 * math.pi))
    return before * half, half + before * bell


def partner(values, step):
    ways = lax.axis_size("mp")
    return lax.ppermute(values, "mp", [(i, i ^ step) for i in range(ways)])


def halo_rows(values, halo):
    ways = lax.axis_size("mp")
    before = lax.ppermute(values[-halo:], "mp", [(i, i + 1) for i in range(ways - 1)])
    after = lax.ppermute(values[:halo], "mp", [(i + 1, i) for i in range(ways - 1)])
    return before, after


def group_tables(table):
    ways = lax.axis_size("mp")
    data_ways = lax.axis_size("dp")
    total = table
    for step in range(1, ways):
        total = total + partner(table, step)
    held = total[None]
    data_index = lax.axis_index("dp")
    level = 1
    while level < data_ways:
        other = lax.ppermute(held, "dp", [(i, i ^ level) for i in range(data_ways)])
        first = (data_index & level) == 0
        held = jnp.where(
            first, jnp.concatenate([held, other]), jnp.concatenate([other, held])
        )
        level *= 2
    return held


CORE, NEAR_X, NEAR_Y = 1, 2, 4


def swap(values, bit):
    ways = lax.axis_size("dp")
    return lax.ppermute(values, "dp", [(i, i ^ bit) for i in range(ways)])


def along(piece):
    return [partner(piece, step) for step in range(1, lax.axis_size("mp"))]


def bit_step(held, level, *gates):
    order = sorted(held)
    other = after(partner(jnp.stack([held[i] for i in order]), level), gates)
    return held | {i | level: other[at] for at, i in enumerate(order)}


def others_of(held):
    return jnp.stack([held[i] for i in sorted(held)[1:]])


def first_step(values, *gates):
    middle = values.shape[1] // 2
    first, second = values[:, :middle], values[:, middle:]
    arrived = after((swap(first, NEAR_X), swap(second, NEAR_Y)), gates)
    return [jnp.stack([first, arrived[0]]), jnp.stack([second, arrived[1]])]


def second_step(pairs, *gates):
    first, second = pairs
    arrived = after((swap(first, NEAR_Y), swap(second, NEAR_X)), gates)
    return [first, arrived[0], second, arrived[1]]


def core_step(held):
    return [*held, swap(jnp.stack(held), CORE)]


def after(value, *others):
    return lax.optimization_barrier((value, others))[0]


def add(first, second):
    return (first.astype(f32) + second.astype(f32)).astype(bf16)


def first_sum_step(sums):
    half = sums.shape[2] // 2
    first, second = sums[:, :, :half], sums[:, :, half:]
    return [(first[0], swap(first[1], NEAR_Y)), (second[:, 0], swap(second[:, 1], NEAR_X))]


def second_sum_step(halves):
    first, second = (add(*half) for half in halves)
    return [(first[0], swap(first[1], NEAR_X)), (second[0], swap(second[1], NEAR_Y))]


def over_groups(total):
    level = PLANE
    while level < lax.axis_size("dp"):
        total = total + swap(total, level)
        level *= 2
    return total


def sum_along(parts):
    total = parts[0].astype(f32)
    for step in range(1, len(parts)):
        total = total + partner(parts[step], step).astype(f32)
    return over_groups(total)


def shards(
    tokens, grad_out, pass_len, labels, w_query, w_key, w_value, b_query, b_value, w_out, b_out,
    ln1_gain, ln1_shift, w_in, b_in, w_back, b_back, ln2_gain, ln2_shift,
):
    ways = lax.axis_size("mp")
    data_ways = lax.axis_size("dp")
    mp_index = lax.axis_index("mp")
    data_index = lax.axis_index("dp")
    own_rows, width = tokens.shape
    rows_here = pass_len.shape[0]
    inner = w_query.shape[1]
    units = w_in.shape[1]
    halo = ROW_LEN // 4
    count = own_rows + 2 * halo
    scale = 1.0 / math.sqrt(HEAD)
    temper = 2.0 / math.sqrt(width)

    piece_rows = units // PLANE
    heads = inner // HEAD
    part = inner // PLANE
    place = jnp.stack([(data_index & CORE) << 2 | (data_index % PLANE) >> 1, mp_index])
    (qkv_own,) = local(
        own_heads_kernel, place, (w_query.T, w_key.T, w_value.T), [((PLANE, 3 * part, width), bf16)],
        [((3 * heads * PLANE, 8, width), f32)], 4, "own_heads",
    )
    biases = jnp.concatenate([b_in, b_query, b_value])
    digits, rest = [], biases
    for _ in range(3):
        digits.append(lax.reduce_precision(rest, 8, 7))
        rest = rest - digits[-1]
    digits = jnp.stack(digits)
    lines = jnp.concatenate(
        [digits[:, :units], jnp.pad(digits[:, units:], ((0, 0), (0, width - 2 * inner)))]
    )
    lines = jnp.pad(lines, ((0, 2), (0, 0))).astype(bf16)
    qkv_along = along(jnp.concatenate([qkv_own[0], lines]))
    tokens_before, tokens_after = halo_rows(tokens, halo)
    w_out, w_in, w_back, place = lax.optimization_barrier((w_out, w_in, w_back, place, qkv_own))[:4]
    out_own, in_own, back_own = local(
        own_units_kernel, place, (w_out, w_in, w_back),
        [((PLANE, part, width), bf16), ((PLANE, piece_rows, width), bf16), ((PLANE, piece_rows, width), bf16)],
        [((heads * PLANE, 8, width), f32), ((PLANE, piece_rows, width), f32)], 5, "own_units",
    )
    in_piece = jnp.concatenate([in_own[0], out_own[0], jnp.zeros((8, width), bf16), back_own[0]])
    in_piece = after(in_piece, qkv_along)
    qkv_along = jnp.stack(qkv_along)
    qkv_pairs = first_step(qkv_along)
    in_held = {0: in_piece}
    level = ways // 2
    while level > 1:
        in_held = bit_step(in_held, level)
        level //= 2
    in_held = after(in_held, qkv_pairs)
    qkv_held = second_step(after(qkv_pairs, tokens_before, tokens_after, in_held))
    in_along = others_of(bit_step(in_held, 1))
    bias_heads, bias_in = local(
        biases_kernel, place, (after(qkv_along, qkv_pairs), b_in[None], b_query[None], b_value[None]),
        [((2, width), f32), ((1, ways * units), f32)], [((ways * PLANE, 8, 128), f32)], 2, "biases",
    )
    start = after(mp_index * own_rows - halo, qkv_pairs)
    bounds = segment_bounds(pass_len, start, halo, own_rows)
    qkv_parts = core_step(after(qkv_held, in_along, bias_heads, bounds))
    in_start = after(in_along, qkv_parts)
    in_rows = piece_rows + part + 8

    tokens_before = after(tokens_before, in_along)
    qkv = (tokens_before, tokens, tokens_after, qkv_own, *qkv_parts, bias_heads)
    queries, keys, values, qkv_all = local(
        project_kernel, place, qkv, [((count, width), bf16)] * 3 + [((3 * width, width), bf16)],
        [((count, width), bf16), ((PLANE, 3 * part, width), f32)], 10, "project", 32,
    )
    in_pairs = first_step(in_start[:, :in_rows], queries)
    context = [attend_forward(bounds, after(queries, in_pairs), keys, values, halo, 0, 2)]
    in_held = second_step(in_pairs, context[0])
    back_start = after(in_start[:, in_rows:], in_held)
    in_parts = core_step(in_held)
    late_queries = after(queries, in_held, back_start, context[0])
    context.append(attend_forward(bounds, late_queries, keys, values, halo, 1, 2))
    context = jnp.concatenate(context)
    in_own = after(in_own, context)
    in_all, out_all = local(
        join_in_out_kernel, place, (in_own, out_own, *in_parts),
        [((ways * units, width), bf16), ((width, width), bf16)],
        [((PLANE, part, width), f32)], 5, "join_in_out",
    )
    attended = mm(context, out_all)
    first_sum = tokens.astype(f32) + attended + b_out
    center_one, inverse_one = norm_parts(first_sum)
    unit_one = center_one * inverse_one
    hidden = unit_one * ln1_gain + ln1_shift
    hidden_low = hidden.astype(bf16)
    back_held = second_step(first_step(back_start, context), hidden_low)
    back_parts = core_step(back_held)
    (back_all,) = local(
        join_units_kernel, place, (back_own, *back_parts),
        [((ways * units, width), bf16)], [], 4, "join_back",
    )
    hidden_low = after(hidden_low, back_held)

    active, slope = gelu_both(mm(hidden_low, in_all, NT) + bias_in)
    active, slope = lax.optimization_barrier((active.astype(bf16), slope.astype(bf16)))
    second_sum = hidden + mm(active, back_all) + b_back
    center_two, inverse_two = norm_parts(second_sum)
    unit_two = center_two * inverse_two
    mixed = (unit_two * ln2_gain + ln2_shift).astype(bf16)

    query_count = PAIRS * rows_here
    places = cls_places(pass_len) + (jnp.arange(rows_here, dtype=jnp.int32) * ROW_LEN)[:, None]
    table_places = jnp.concatenate([places[:, :PAIRS].reshape(-1), places[:, PAIRS:].reshape(-1)])
    table_places = table_places - mp_index * own_rows
    picker = table_places[:, None] == jnp.arange(own_rows, dtype=jnp.int32)[None, :]
    table = mm(picker.astype(bf16), mixed).astype(bf16)
    digits = jnp.concatenate([labels // 32, labels % 32]).astype(bf16)
    digits = jnp.where(mp_index == 0, digits, 0)
    extra = jnp.zeros((8, width), bf16).at[0, : 2 * query_count].set(digits)
    tables = group_tables(jnp.concatenate([table, extra]))
    all_count = data_ways * query_count
    query_cls = tables[:, :query_count].reshape(all_count, width)
    passage_cls = tables[:, query_count : 2 * query_count].reshape(all_count, width)
    digits = tables[:, 2 * query_count, : 2 * query_count].astype(jnp.int32)
    all_labels = (digits[:, :query_count] * 32 + digits[:, query_count:]).reshape(-1)

    logits = mm(query_cls, passage_cls, NT) * temper
    targets = all_labels[:, None] == jnp.arange(all_count, dtype=jnp.int32)[None, :]
    top = jnp.max(logits, axis=1, keepdims=True)
    raised = jnp.exp(logits - top)
    total = jnp.sum(raised, axis=1, keepdims=True)
    losses = top[:, 0] + jnp.log(total[:, 0]) - jnp.sum(jnp.where(targets, logits, 0.0), axis=1)
    query_losses = lax.dynamic_slice_in_dim(losses, data_index * query_count, query_count)
    grad_logits = (raised / total - targets.astype(f32)) * temper
    rows_of = lax.dynamic_slice_in_dim(grad_logits, data_index * query_count, query_count, 0)
    columns_of = lax.dynamic_slice_in_dim(grad_logits, data_index * query_count, query_count, 1)
    grad_cls = jnp.concatenate(
        [
            jnp.dot(rows_of, passage_cls.astype(f32), precision=highest),
            jnp.dot(columns_of.T, query_cls.astype(f32), precision=highest),
        ]
    )
    grad_mixed = grad_out.astype(f32) + jnp.dot(
        picker.astype(f32).T, grad_cls, precision=highest
    )

    grad_second = norm_pull(grad_mixed, unit_two, inverse_two, ln2_gain)
    stats = [
        jnp.sum(grad_mixed * unit_two, axis=0, keepdims=True),
        jnp.sum(grad_mixed, axis=0, keepdims=True),
        jnp.sum(grad_second, axis=0, keepdims=True),
    ]
    second_low = grad_second.astype(bf16)

    def to_core(left, right):
        return mm(left[:, left.shape[1] // 2 :], right, TN).astype(bf16)

    def chip_sum(left, right, arrived):
        own = mm(left[:, : left.shape[1] // 2], right, TN)
        return add(own, arrived).reshape(2, 2, ways, piece_rows, width)

    back_sent = to_core(active, second_low)
    back_arrived = swap(back_sent, CORE)
    pulled, back_sent = lax.optimization_barrier((second_low, back_sent))
    grad_before = (mm(pulled, back_all, NT) * slope.astype(f32)).astype(bf16)
    back_sum = chip_sum(active, second_low, back_arrived)
    back_half = swap(back_sum[1], NEAR_Y)
    in_sent = to_core(grad_before, hidden_low)
    in_arrived = swap(in_sent, CORE)
    pulled = after(grad_before, back_sum, in_sent)
    grad_hidden = grad_second + mm(pulled, in_all)
    grad_first = norm_pull(grad_hidden, unit_one, inverse_one, ln1_gain)
    stats += [
        jnp.sum(grad_hidden * unit_one, axis=0, keepdims=True),
        jnp.sum(grad_hidden, axis=0, keepdims=True),
        jnp.sum(grad_first, axis=0, keepdims=True),
    ]
    first_low = grad_first.astype(bf16)
    first_before, first_after = halo_rows(first_low, halo)
    in_sum = chip_sum(after(grad_before, first_low), hidden_low, in_arrived)
    in_half = swap(in_sum[:, 1], NEAR_X)
    out_keep, out_sent = local(
        functools.partial(out_grads_kernel, ways), place, (context, first_low),
        [((4 * ways, part + 8, width), bf16)] * 2, [((8 * ways, part + 8, width), f32)], 3, "out_grads",
    )
    out_sum = add(out_keep, swap(out_sent, CORE)).reshape(2, 2, ways, part + 8, width)
    out_half = swap(out_sum[1], NEAR_Y)

    d_b_in = jnp.sum(grad_before, axis=0, dtype=f32, keepdims=True)
    (vectors,) = local(
        vectors_kernel, place, (*stats, d_b_in), [((ways, 8, width), f32)],
        [((ways * PLANE, 8, 128), f32)], 2, "vectors",
    )

    first_before, first_after = after((first_before, first_after), in_sum, out_sent, vectors)
    first_window = jnp.concatenate([first_before, first_low, first_after])
    grad_context = mm(first_window, out_all, NT).astype(bf16)
    grad_context = after(grad_context, in_sum, back_sum, out_sum, vectors)
    grad_query, *sums = attend_backward(bounds, queries, keys, values, grad_context, halo, ())
    back_half, in_half, out_half = after((back_half, in_half, out_half), grad_query)
    back_sum = add(back_sum[0], back_half)
    in_sum = add(in_sum[:, 0], in_half)
    out_sum = add(out_sum[0], out_half)
    back_half = swap(back_sum[1], NEAR_X)
    in_half = swap(in_sum[1], NEAR_Y)
    out_half = swap(out_sum[1], NEAR_X)
    grad_context = after(grad_context, back_sum, in_sum, out_sum, grad_query)
    late_query, grad_keys, grad_values = attend_backward(
        bounds, queries, keys, values, grad_context, halo, sums
    )
    early_halves = [(back_sum[0], back_half), (in_sum[0], in_half), (out_sum[0], out_half)]
    early_halves = after(early_halves, late_query)
    early_sum = jnp.concatenate([add(*half) for half in early_halves], axis=1)
    early_parts = [early_sum[i] for i in range(ways)]
    tokens_low = after(tokens, early_parts)

    late_rows = 3 * part + 8
    late_keep, late_sent = local(
        piece_grads_kernel, place, (grad_query, late_query, grad_keys, grad_values, tokens_low, vectors),
        [((4 * ways, late_rows, width), bf16)] * 2, [((8 * ways, late_rows, width), f32)], 8, "piece_grads", 36,
    )
    late_arrived = swap(late_sent, CORE)
    early_odd = partner(jnp.stack(early_parts[1::2]), 1)
    late_sum = add(late_keep, late_arrived).reshape(2, 2, ways, late_rows, width)
    halves = first_sum_step(late_sum)
    early_odd = after(early_odd, halves)
    early_parts = [add(even, odd) for even, odd in zip(early_parts[::2], early_odd)]
    halves = second_sum_step(halves)
    late_parts = [half[i] for half in (add(*h) for h in halves) for i in range(ways // 2)]
    level, early_own = 2, early_parts[0].astype(f32)
    while level < ways:
        early_own = early_own + after(partner(early_parts[level // 2], level), late_parts).astype(f32)
        level *= 2
    late_total = sum_along(late_parts)
    early_held = second_step(first_step(over_groups(early_own).astype(bf16)[None], late_total))
    grad_queries = jnp.concatenate([grad_query, late_query])
    d_tokens = (
        grad_first
        + mm(grad_queries, qkv_all[:width])
        + mm(grad_keys, qkv_all[width : 2 * width])
        + mm(grad_values, qkv_all[2 * width :])
    )
    late_held = first_step(late_total.astype(bf16)[None])
    early_pieces = core_step(after(early_held, late_held))
    late_pieces = core_step(second_step(late_held, d_tokens))
    line = late_total[3 * part :]

    d_query, d_key, d_value = local(
        finish_heads_kernel, place, late_pieces, [((inner, width), f32)] * 3,
        [((PLANE, 3 * part, width), f32)], 4, "finish_heads",
    )
    d_back, d_in, d_out = local(
        finish_units_kernel, place, early_pieces,
        [((units, width), f32), ((width, units), f32), ((inner, width), f32)],
        [((PLANE, 2 * piece_rows + part + 8, width), f32), ((units, width), f32)], 6, "finish_units",
    )
    norms = [line[1 + i // ways, i % ways * inner : (i % ways + 1) * inner] for i in range(8)]
    return (
        mixed,
        query_losses,
        d_tokens,
        d_query.T,
        d_key.T,
        d_value.T,
        norms[6],
        norms[7],
        d_out,
        norms[5],
        norms[3],
        norms[4],
        d_in,
        line[0],
        d_back,
        norms[2],
        norms[0],
        norms[1],
    )


def solution(mesh):
    return jax.shard_map(
        shards,
        mesh=mesh,
        in_specs=(
            P(("dp", "mp"), None), P(("dp", "mp"), None), P("dp", None), P("dp"),
            P(None, "mp"), P(None, "mp"), P(None, "mp"), P("mp"), P("mp"), P("mp", None), P(),
            P(), P(), P(None, "mp"), P("mp"), P("mp", None), P(), P(), P(),
        ),
        out_specs=(
            P(("dp", "mp"), None), P("dp"), P(("dp", "mp"), None),
            P(None, "mp"), P(None, "mp"), P(None, "mp"), P("mp"), P("mp"), P("mp", None),
            P("mp"), P("mp"), P("mp"), P(None, "mp"), P("mp"), P("mp", None), P("mp"), P("mp"), P("mp"),
        ),
        check_vma=False,
    )
```

```python
import functools
import math

import jax
import jax.numpy as jnp
from jax import lax
from jax.experimental import pallas as pl
from jax.experimental.pallas import tpu as pltpu
from jax.sharding import PartitionSpec as P

HEAD = 64
ROW_LEN = 1024
PAIRS = 4
QLEN = 32
TILE = 128
QUERIES = 64
QUAD = 4 * HEAD
FIRST = 14 * QUERIES
ALIGN = 32
BLOCKS = (1, 2, 3, 4, 5, 7, 10)

epsilon = 1e-12
masked_score = -1e30
highest = lax.Precision.HIGHEST
f32 = jnp.float32
bf16 = jnp.bfloat16
NT = (((1,), (1,)), ((), ()))
TN = (((0,), (0,)), ((), ()))
NN = (((1,), (0,)), ((), ()))


def mm(a, b, dims=NN):
    return lax.dot_general(a, b, dims, preferred_element_type=f32)


def bounds_kernel(halo, own, start_ref, pass_ref, tiles_ref, low_ref, high_ref):
    start = start_ref[0]
    count = low_ref.shape[1]
    rows = pass_ref.shape[0]
    last = rows * ROW_LEN
    cuts = []
    for row in range(rows):
        cuts += [jnp.int32(row * ROW_LEN + j * QLEN) for j in range(PAIRS + 1)]
        for j in range(PAIRS):
            cuts.append(cuts[-1] + pass_ref[row, j])

    def low_of(place):
        low = jnp.full_like(place, start)
        for cut in cuts:
            low = jnp.where(cut <= place, cut, low)
        return jnp.clip(jnp.where(place >= last, last, low) - start, 0, count)

    def high_of(place):
        high = jnp.full_like(place, last)
        for cut in reversed(cuts):
            high = jnp.where(cut > place, cut, high)
        return jnp.clip(jnp.where(place >= last, start + count, high) - start, 0, count)

    place = start + lax.broadcasted_iota(jnp.int32, (1, count), 1)
    low_ref[...] = low_of(place)
    high_ref[...] = high_of(place)
    for tile in range(count // QUERIES):
        at = tile * QUERIES
        first = low_of(start + at)
        after_last = high_of(start + at + QUERIES - 1)
        low = first // ALIGN * ALIGN
        blocks = (after_last - low + TILE - 1) // TILE
        tiles_ref[0, tile] = low
        tiles_ref[1, tile] = blocks
        if at < halo:
            blocks = jnp.where(after_last > halo, blocks, 0)
        if at >= halo + own:
            blocks = jnp.where(first < halo + own, blocks, 0)
        tiles_ref[2, tile] = blocks


def segment_bounds(pass_len, start, halo, own):
    count = own + 2 * halo
    smem = pl.BlockSpec(memory_space=pltpu.SMEM)
    vmem = pl.BlockSpec(memory_space=pltpu.VMEM)
    line = jax.ShapeDtypeStruct((1, count), jnp.int32)
    return pl.pallas_call(
        functools.partial(bounds_kernel, halo, own),
        out_shape=(jax.ShapeDtypeStruct((3, count // QUERIES), jnp.int32), line, line),
        in_specs=[smem, smem],
        out_specs=(smem, vmem, vmem),
        compiler_params=pltpu.CompilerParams(vmem_limit_bytes=8 * 2**20),
        name="bounds",
    )(start.reshape(1), pass_len)


def cls_places(pass_len):
    lens = [pass_len[:, j] for j in range(PAIRS)]
    starts = [jnp.full_like(lens[0], j * QLEN) for j in range(PAIRS)]
    at = jnp.full_like(lens[0], PAIRS * QLEN)
    for j in range(PAIRS):
        starts.append(at)
        at = at + lens[j]
    return jnp.stack(starts, axis=1)


def by_span(blocks, count, act):
    least = 0
    for size in BLOCKS:
        if size * TILE > count:
            break

        @pl.when((blocks > least) & (blocks <= size))
        def _(size=size):
            act(size * TILE)

        least = size


def head_of(shape):
    return lax.broadcasted_iota(jnp.int32, shape, 1) // HEAD


def split_heads(block):
    head = head_of(block.shape)
    zero = jnp.zeros_like(block)
    return jnp.concatenate([jnp.where(head == h, block, zero) for h in range(4)], axis=0)


def join_heads(stacked):
    rows = stacked.shape[0] // 4
    head = head_of((rows, stacked.shape[1]))
    out = stacked[:rows]
    for h in range(1, 4):
        out = jnp.where(head == h, stacked[h * rows : (h + 1) * rows], out)
    return out


def four_times(ref, row):
    line = ref[:, pl.ds(pl.multiple_of(row // TILE * TILE, TILE), TILE)]
    turned = jnp.concatenate([line[:, QUERIES:], line[:, :QUERIES]], axis=1)
    lane = lax.broadcasted_iota(jnp.int32, line.shape, 1)
    odd = row % TILE >= QUERIES
    both = jnp.where((lane < QUERIES) != odd, line, turned)
    return jnp.concatenate([both, both], axis=1)


def write_bias(bias_ref, lo_ref, hi_ref, row, first, span):
    place = lax.broadcasted_iota(jnp.int32, (span, QUAD), 0) + first
    inside = (place >= four_times(lo_ref, row)) & (place < four_times(hi_ref, row))
    bias_ref[:span] = jnp.where(inside, 0.0, masked_score)


def head_weights(scores, bias):
    scores = [score + bias for score in scores]
    tops = [jnp.max(score, axis=0, keepdims=True) for score in scores]
    raised = [jnp.exp(score - top) for score, top in zip(scores, tops)]
    inverses = [1.0 / jnp.sum(value, axis=0, keepdims=True) for value in raised]
    return [value * inverse for value, inverse in zip(raised, inverses)]


def forward_kernel(halo, start, tiles_ref, lo_ref, hi_ref, q_ref, k_ref, v_ref, out_ref, bias_ref):
    count = k_ref.shape[0]
    quads = [pl.ds(i * QUAD, QUAD) for i in range(q_ref.shape[1] // QUAD)]

    def tile_step(tile, carry):
        here = tile + (start + halo) // QUERIES
        blocks = tiles_ref[1, here]

        def act(span):
            first = jnp.minimum(tiles_ref[0, here], count - span)
            keys = pl.ds(pl.multiple_of(first, ALIGN), span)
            to = pl.ds(pl.multiple_of(tile * QUERIES, QUERIES), QUERIES)
            row = pl.multiple_of(tile * QUERIES + start + halo, QUERIES)
            write_bias(bias_ref, lo_ref, hi_ref, row, first, span)
            rows = pl.ds(row, QUERIES)
            scores = [mm(k_ref[keys, lanes], split_heads(q_ref[rows, lanes]), NT) for lanes in quads]
            weights = [value.astype(bf16) for value in head_weights(scores, bias_ref[:span])]
            for lanes, value in zip(quads, weights):
                out_ref[to, lanes] = join_heads(mm(value, v_ref[keys, lanes], TN)).astype(bf16)

        by_span(blocks, count, act)
        return carry

    lax.fori_loop(0, out_ref.shape[0] // QUERIES, tile_step, 0)


def lasting(micros):
    return pl.CostEstimate(flops=int(micros * 2e7), bytes_accessed=int(micros * 7e4), transcendentals=0)


def attention(kernel, arrays, outs, scratch, micros, name, mib):
    smem = pl.BlockSpec(memory_space=pltpu.SMEM)
    vmem = pl.BlockSpec(memory_space=pltpu.VMEM)
    return pl.pallas_call(
        kernel,
        out_shape=tuple(jax.ShapeDtypeStruct(shape, dtype) for shape, dtype in outs),
        in_specs=[smem] + [vmem] * (len(arrays) - 1),
        out_specs=(vmem,) * len(outs),
        scratch_shapes=[pltpu.VMEM(shape, dtype) for shape, dtype in scratch],
        compiler_params=pltpu.CompilerParams(vmem_limit_bytes=mib * 2**20),
        cost_estimate=lasting(micros),
        name=name,
    )(*arrays)


def attend_forward(bounds, queries, keys, values, halo, part, parts):
    count, width = keys.shape
    rows = (count - 2 * halo) // parts
    (context,) = attention(
        functools.partial(forward_kernel, halo, part * rows), (*bounds, queries, keys, values),
        [((rows, width), bf16)], [((count, QUAD), f32)], 7, "attend_forward", 14,
    )
    return context


def backward_kernel(halo, start, carried, tiles_ref, lo_ref, hi_ref, q_ref, k_ref, v_ref, g_ref, *refs):
    count = k_ref.shape[0]
    own = count - 2 * halo
    if carried:
        dk_in, dv_in, dq_ref, dk_ref, dv_ref, bias_ref, dk_sum, dv_sum = refs
        dk_sum[...] = dk_in[...]
        dv_sum[...] = dv_in[...]
    else:
        dq_ref, dk_sum, dv_sum, bias_ref = refs
        dk_sum[...] = jnp.zeros_like(dk_sum)
        dv_sum[...] = jnp.zeros_like(dv_sum)
    quads = [pl.ds(i * QUAD, QUAD) for i in range(q_ref.shape[1] // QUAD)]
    low = max(start, halo)

    def tile_step(tile, carry):
        blocks = tiles_ref[2, tile]
        mine = (tile >= halo // QUERIES) & (tile < (halo + own) // QUERIES)

        def act(span):
            first = jnp.minimum(tiles_ref[0, tile], count - span)
            keys = pl.ds(pl.multiple_of(first, ALIGN), span)
            row = pl.multiple_of(tile * QUERIES, QUERIES)
            rows = pl.ds(row, QUERIES)
            write_bias(bias_ref, lo_ref, hi_ref, row, first, span)
            q4 = [split_heads(q_ref[rows, lanes]) for lanes in quads]
            scores = [mm(k_ref[keys, lanes], q, NT) for q, lanes in zip(q4, quads)]
            g4 = [split_heads(g_ref[rows, lanes]) for lanes in quads]
            slopes = [mm(v_ref[keys, lanes], g, NT) for g, lanes in zip(g4, quads)]
            weights = head_weights(scores, bias_ref[:span])
            inner = [jnp.sum(w * s, axis=0, keepdims=True) for w, s in zip(weights, slopes)]
            grads = [(w * (s - i)).astype(bf16) for w, s, i in zip(weights, slopes, inner)]
            for w, g, lanes in zip(weights, g4, quads):
                dv_sum[keys, lanes] += mm(w.astype(bf16), g)
            for d, q, lanes in zip(grads, q4, quads):
                dk_sum[keys, lanes] += mm(d, q)

            @pl.when(mine)
            def _():
                to = pl.ds(pl.multiple_of(row - low, QUERIES), QUERIES)
                for d, lanes in zip(grads, quads):
                    grad = join_heads(mm(d, k_ref[keys, lanes], TN)).astype(bf16)
                    dq_ref[to, lanes] = grad * jnp.asarray(1.0 / math.sqrt(HEAD), bf16)

        by_span(blocks, count, act)
        return carry

    end = count if carried else FIRST
    lax.fori_loop(start // QUERIES, end // QUERIES, tile_step, 0)
    if carried:
        dk_ref[...] = dk_sum[pl.ds(halo, own), :].astype(bf16)
        dv_ref[...] = dv_sum[pl.ds(halo, own), :].astype(bf16)


def attend_backward(bounds, queries, keys, values, grads, halo, sums):
    count, width = keys.shape
    own = count - 2 * halo
    window = ((count, width), f32)
    rows = halo + own - FIRST if sums else FIRST - halo
    outs = [((rows, width), bf16)]
    if sums:
        outs, scratch = outs + [((own, width), bf16)] * 2, [((count, QUAD), f32), window, window]
    else:
        outs, scratch = outs + [window, window], [((count, QUAD), f32)]
    return attention(
        functools.partial(backward_kernel, halo, FIRST if sums else 0, bool(sums)),
        (*bounds, queries, keys, values, grads, *sums), outs, scratch, 16, "attend_backward", 28,
    )


SMEM = pl.BlockSpec(memory_space=pltpu.SMEM)
VMEM = pl.BlockSpec(memory_space=pltpu.VMEM)
PLANE = 8


def local(kernel, place, arrays, outs, scratch, micros, name, mib=20):
    return pl.pallas_call(
        kernel,
        out_shape=tuple(jax.ShapeDtypeStruct(shape, dtype) for shape, dtype in outs),
        in_specs=[SMEM] + [VMEM] * len(arrays),
        out_specs=(VMEM,) * len(outs),
        scratch_shapes=[pltpu.VMEM(shape, dtype) for shape, dtype in scratch],
        compiler_params=pltpu.CompilerParams(vmem_limit_bytes=mib * 2**20),
        cost_estimate=lasting(micros),
        name=name,
    )(place, *arrays)


def own_heads_kernel(place_ref, q_ref, k_ref, v_ref, out_ref, rows_ref):
    place = place_ref[0]
    eighths = q_ref.shape[0] // PLANE
    slabs = q_ref.shape[0] // 8
    for i, ref in enumerate((q_ref, k_ref, v_ref)):
        rows_ref[pl.ds(i * slabs, slabs)] = ref[...].astype(f32).reshape(slabs, 8, -1)
    heads = 3 * eighths // 8
    for j in range(PLANE):
        held = [rows_ref[h * PLANE + (place ^ j)] for h in range(heads)]
        out_ref[j] = jnp.concatenate(held, axis=0).astype(bf16)


def own_units_kernel(place_ref, o_ref, i_ref, b_ref, out_ref, in_ref, back_ref, rows_ref, units_ref):
    place = place_ref[0]
    rows = in_ref.shape[1]
    heads = out_ref.shape[1] // 8
    rows_ref[...] = o_ref[...].astype(f32).reshape(rows_ref.shape)
    units_ref[...] = i_ref[...].astype(f32).T.reshape(units_ref.shape)
    for j in range(PLANE):
        held = [rows_ref[h * PLANE + (place ^ j)] for h in range(heads)]
        out_ref[j] = jnp.concatenate(held, axis=0).astype(bf16)
        in_ref[j] = units_ref[place ^ j].astype(bf16)
        back_ref[j] = b_ref[pl.ds(pl.multiple_of((place ^ j) * rows, rows), rows), :]


def by_eighth(refs):
    first, second = [], []
    for j in range(PLANE):
        far, y, x = j // 4, j // 2 % 2, j % 2
        first.append(refs[4].at[y, x] if far else refs[y].at[x])
        second.append(refs[4].at[2 + x, y] if far else refs[2 + x].at[y])
    return first, second


def eighth_rows(halves, j, member, start, count):
    first, second = halves[0][j], halves[1][j]
    middle = first.shape[1]
    pieces = []
    if start < middle:
        pieces.append(first[member, pl.ds(start, min(count, middle - start)), :])
    if start + count > middle:
        at = max(start, middle)
        pieces.append(second[member, pl.ds(at - middle, start + count - at), :])
    return pieces


def stage_eighths(own_ref, halves, member, start, stage_ref):
    for j in range(PLANE):
        if own_ref is not None and member == 0:
            stage_ref[j] = own_ref[j].astype(f32)
            continue
        at = 0
        of = member if own_ref is None else member - 1
        for piece in eighth_rows(halves, j, of, start, stage_ref.shape[1]):
            stage_ref[j, pl.ds(at, piece.shape[0]), :] = piece.astype(f32)
            at += piece.shape[0]


def head_block(stage_ref, head):
    return jnp.concatenate([stage_ref[j, pl.ds(head * 8, 8), :] for j in range(PLANE)], axis=0)


def project_kernel(
    place_ref, left_ref, tokens_ref, right_ref, own_ref, *refs
):
    halves, refs = by_eighth(refs[:5]), refs[5:]
    bias_ref, q_ref, k_ref, v_ref, w_ref, x_ref, stage_ref = refs
    ways = halves[0][0].shape[0] + 1
    heads = own_ref.shape[1] // 24
    halo = left_ref.shape[0]
    own = tokens_ref.shape[0]
    width = tokens_ref.shape[1]
    inner = heads * HEAD
    x_ref[:halo] = left_ref[...]
    x_ref[pl.ds(halo, own)] = tokens_ref[...]
    x_ref[pl.ds(halo + own, halo)] = right_ref[...]
    for member in range(ways):
        stage_eighths(own_ref, halves, member, 0, stage_ref)
        for kind in range(3):
            blocks = [head_block(stage_ref, kind * heads + h) for h in range(heads)]
            at = kind * width + member * inner
            w_ref[pl.ds(at, inner)] = jnp.concatenate(blocks, axis=0).astype(bf16)

    def step(i, carry):
        rows = pl.ds(pl.multiple_of(i * 256, 256), 256)
        x = x_ref[rows, :]
        q = mm(x, w_ref[:width], NT) + bias_ref[0:1]
        q_ref[rows, :] = (q * (1.0 / math.sqrt(HEAD))).astype(bf16)
        k_ref[rows, :] = mm(x, w_ref[pl.ds(width, width)], NT).astype(bf16)
        v_ref[rows, :] = (mm(x, w_ref[pl.ds(2 * width, width)], NT) + bias_ref[1:2]).astype(bf16)
        return carry

    lax.fori_loop(0, x_ref.shape[0] // 256, step, 0)


def join_units(own_ref, halves, out_ref):
    rows = own_ref.shape[1]
    ways = halves[0][0].shape[0] + 1
    for j in range(PLANE):
        out_ref[pl.ds(j * ways * rows, rows), :] = own_ref[j]
        for member in range(1, ways):
            at = (j * ways + member) * rows
            for piece in eighth_rows(halves, j, member - 1, 0, rows):
                out_ref[pl.ds(at, piece.shape[0]), :] = piece
                at += piece.shape[0]


def join_units_kernel(place_ref, own_ref, *refs):
    join_units(own_ref, by_eighth(refs[:5]), refs[5])


def join_in_out_kernel(place_ref, own_ref, own_out_ref, *refs):
    halves = by_eighth(refs[:5])
    in_ref, out_ref, stage_ref = refs[5:]
    join_units(own_ref, halves, in_ref)
    heads = own_out_ref.shape[1] // 8
    for member in range(halves[0][0].shape[0] + 1):
        stage_eighths(own_out_ref, halves, member, own_ref.shape[1], stage_ref)
        for h in range(heads):
            block = head_block(stage_ref, h)
            out_ref[pl.ds((member * heads + h) * HEAD, HEAD), :] = block.astype(bf16)


def split_digits(values):
    digits = []
    for _ in range(3):
        digits.append(values.astype(bf16))
        values = values - digits[-1].astype(f32)
    return digits


def biases_kernel(place_ref, along_ref, in_ref, q_ref, v_ref, heads_ref, units_ref, line_ref):
    place = place_ref[0]
    ways = along_ref.shape[0] + 1
    inner = q_ref.shape[1]
    rows = in_ref.shape[1] // PLANE
    first = along_ref.shape[1] - 8
    others = along_ref[:, first:, :].astype(f32)
    digits = split_digits(jnp.concatenate([q_ref[...], v_ref[...]], axis=1))
    digits = [digit.astype(f32) for digit in digits]
    for member in range(ways - 1):
        digits.append(others[member, 3:6, : 2 * inner])
    digits = jnp.concatenate(digits, axis=0).astype(bf16)
    lane = lax.broadcasted_iota(jnp.int32, (2 * inner, 2 * inner), 0)
    to = lax.broadcasted_iota(jnp.int32, (2 * inner, 2 * inner), 1)
    chosen = jnp.where((lane ^ (place << 3)) == to, 1.0, 0.0).astype(bf16)
    moved = mm(digits, chosen)
    sums = [moved[3 * m : 3 * m + 1] + moved[3 * m + 1 : 3 * m + 2] + moved[3 * m + 2 : 3 * m + 3] for m in range(ways)]
    heads_ref[0:1] = jnp.concatenate([value[:, :inner] for value in sums], axis=1)
    heads_ref[1:2] = jnp.concatenate([value[:, inner:] for value in sums], axis=1)
    for member in range(ways):
        if member == 0:
            value = in_ref[...]
        else:
            three = others[member - 1]
            value = three[0:1] + three[1:2] + three[2:3]
        for p in range(PLANE):
            line_ref[member * PLANE + p, 0:1, :rows] = value[:, p * rows : (p + 1) * rows]
    held = [
        line_ref[member * PLANE + (place ^ j), 0:1, :rows] for j in range(PLANE) for member in range(ways)
    ]
    units_ref[...] = jnp.concatenate(held, axis=1)


def vectors_kernel(place_ref, *refs):
    stat_refs, (units_ref, out_ref, line_ref) = refs[:6], refs[6:]
    place, own = place_ref[0], place_ref[1]
    ways, _, width = out_ref.shape
    inner = width // ways
    rows = units_ref.shape[1] // PLANE // ways
    for j in range(PLANE):
        for member in range(ways):
            at = j * ways + member
            line_ref[at, 0:1, :rows] = units_ref[:, at * rows : (at + 1) * rows]
    stats = jnp.concatenate([ref[...] for ref in stat_refs], axis=0)
    parts = [stats[:, i * inner : (i + 1) * inner] for i in range(ways)]
    for member in range(ways):
        held = [line_ref[(place ^ p) * ways + member, 0:1, :rows] for p in range(PLANE)]
        mine = parts[0]
        for i in range(1, ways):
            mine = jnp.where((own ^ member) == i, parts[i], mine)
        norms = jnp.concatenate([mine[i : i + 1] for i in range(6)], axis=1)
        norms = jnp.concatenate([norms, jnp.zeros((1, 2 * inner), f32)], axis=1)
        lines = [jnp.concatenate(held, axis=1), norms[:, :width], norms[:, width:]]
        out_ref[member] = jnp.concatenate([*lines, jnp.zeros((5, width), f32)], axis=0)


def put_heads(ways, heads, sum_ref, kind, first_head, block):
    for i in range(block.shape[0] // HEAD):
        member, h = divmod(first_head + i, heads)
        for j in range(PLANE):
            part = block[i * HEAD + j * 8 : i * HEAD + j * 8 + 8]
            sum_ref[j * ways + member, pl.ds((kind * heads + h) * 8, 8), :] = part


def part_pieces(sum_ref, keep_ref, send_ref):
    half = keep_ref.shape[0]
    for i in range(half):
        keep_ref[i] = sum_ref[i].astype(bf16)
        send_ref[i] = sum_ref[half + i].astype(bf16)


def out_grads_kernel(ways, place_ref, context_ref, first_ref, keep_ref, send_ref, sum_ref):
    width = first_ref.shape[1]
    heads = width // ways // HEAD
    sum_ref[:, heads * 8 :, :] = jnp.zeros((PLANE * ways, 8, width), f32)
    put_heads(ways, heads, sum_ref, 0, 0, mm(context_ref[...], first_ref[...], TN))
    part_pieces(sum_ref, keep_ref, send_ref)


def piece_grads_kernel(
    place_ref, dq_first_ref, dq_second_ref, dk_ref, dv_ref, tokens_ref, vectors_ref, keep_ref, send_ref, sum_ref
):
    place = place_ref[0]
    ways = vectors_ref.shape[0]
    width = tokens_ref.shape[1]
    inner = width // ways
    heads = inner // HEAD
    half = dq_first_ref.shape[0]
    block = mm(dq_first_ref[...], tokens_ref[:half], TN) + mm(dq_second_ref[...], tokens_ref[half:], TN)
    put_heads(ways, heads, sum_ref, 0, 0, block)
    put_heads(ways, heads, sum_ref, 1, 0, mm(dk_ref[...], tokens_ref[...], TN))
    put_heads(ways, heads, sum_ref, 2, 0, mm(dv_ref[...], tokens_ref[...], TN))
    lane = lax.broadcasted_iota(jnp.int32, (width, width), 0)
    to = lax.broadcasted_iota(jnp.int32, (width, width), 1)
    member = sum((lane >= i * inner).astype(jnp.int32) for i in range(1, ways))
    within = lane - member * inner
    spot = within ^ (place << 3)
    row = lax.broadcasted_iota(jnp.int32, (8, width), 0)
    column = lax.broadcasted_iota(jnp.int32, (8, width), 1)
    of = sum((column >= i * inner).astype(jnp.int32) for i in range(1, ways))
    ones = jnp.ones((8, tokens_ref.shape[0]), bf16)
    lines = jnp.zeros((8, width), f32)
    sums_of = (
        mm(ones[:, :half], dq_first_ref[...]) + mm(ones[:, half:], dq_second_ref[...]),
        mm(ones, dv_ref[...]),
    )
    for sums, first in zip(sums_of, (width - 2 * inner, width - inner)):
        sums = jnp.where(of == row, sums, 0.0)
        chosen = jnp.where(spot + first == to, 1.0, 0.0).astype(bf16)
        lines = lines + mm(sums.astype(bf16), chosen)
    below = 3 * heads * 8
    for i in range(ways):
        block = vectors_ref[i] + jnp.where(row == 2, lines[i : i + 1], 0.0)
        for j in range(PLANE):
            sum_ref[j * ways + i, pl.ds(below, 8), :] = block
    part_pieces(sum_ref, keep_ref, send_ref)


def gather_heads(place, rows_ref, first, out_ref):
    held = []
    for h in range(out_ref.shape[0] // HEAD):
        for p in range(PLANE):
            held.append(rows_ref[place ^ p, pl.ds(first + h * 8, 8), :])
    out_ref[...] = jnp.concatenate(held, axis=0)


def finish_heads_kernel(place_ref, *refs):
    q_ref, k_ref, v_ref, rows_ref = refs[5:]
    stage_eighths(None, by_eighth(refs[:5]), 0, 0, rows_ref)
    for kind, ref in enumerate((q_ref, k_ref, v_ref)):
        gather_heads(place_ref[0], rows_ref, kind * ref.shape[0] // PLANE, ref)


def finish_units_kernel(place_ref, *refs):
    back_ref, in_ref, out_ref, rows_ref, turned_ref = refs[5:]
    place = place_ref[0]
    rows = back_ref.shape[0] // PLANE
    stage_eighths(None, by_eighth(refs[:5]), 0, 0, rows_ref)
    for p in range(PLANE):
        back_ref[pl.ds(p * rows, rows), :] = rows_ref[place ^ p, :rows, :]
        turned_ref[pl.ds(p * rows, rows), :] = rows_ref[place ^ p, pl.ds(rows, rows), :]
    in_ref[...] = turned_ref[...].T
    gather_heads(place, rows_ref, 2 * rows, out_ref)


def norm_parts(values):
    center = values - jnp.mean(values, axis=-1, keepdims=True)
    spread = jnp.mean(center * center, axis=-1, keepdims=True)
    return center, lax.rsqrt(spread + epsilon)


def norm_pull(grad, unit, inverse, gain):
    scaled = grad * gain
    mean = jnp.mean(scaled, axis=-1, keepdims=True)
    along = jnp.mean(scaled * unit, axis=-1, keepdims=True)
    return inverse * (scaled - mean - unit * along)


def gelu_both(before):
    half = 0.5 * (1.0 + lax.erf(before * math.sqrt(0.5)))
    bell = jnp.exp(-0.5 * before * before) * (1.0 / math.sqrt(2.0 * math.pi))
    return before * half, half + before * bell


def partner(values, step):
    ways = lax.axis_size("mp")
    return lax.ppermute(values, "mp", [(i, i ^ step) for i in range(ways)])


def halo_rows(values, halo):
    ways = lax.axis_size("mp")
    before = lax.ppermute(values[-halo:], "mp", [(i, i + 1) for i in range(ways - 1)])
    after = lax.ppermute(values[:halo], "mp", [(i + 1, i) for i in range(ways - 1)])
    return before, after


def group_tables(table):
    ways = lax.axis_size("mp")
    data_ways = lax.axis_size("dp")
    total = table
    for step in range(1, ways):
        total = total + partner(table, step)
    held = total[None]
    data_index = lax.axis_index("dp")
    level = 1
    while level < data_ways:
        other = lax.ppermute(held, "dp", [(i, i ^ level) for i in range(data_ways)])
        first = (data_index & level) == 0
        held = jnp.where(
            first, jnp.concatenate([held, other]), jnp.concatenate([other, held])
        )
        level *= 2
    return held


CORE, NEAR_X, NEAR_Y = 1, 2, 4


def swap(values, bit):
    ways = lax.axis_size("dp")
    return lax.ppermute(values, "dp", [(i, i ^ bit) for i in range(ways)])


def along(piece):
    return [partner(piece, step) for step in range(1, lax.axis_size("mp"))]


def bit_step(held, level, *gates):
    order = sorted(held)
    other = after(partner(jnp.stack([held[i] for i in order]), level), gates)
    return held | {i | level: other[at] for at, i in enumerate(order)}


def others_of(held):
    return jnp.stack([held[i] for i in sorted(held)[1:]])


def first_step(values, *gates):
    middle = values.shape[1] // 2
    first, second = values[:, :middle], values[:, middle:]
    arrived = after((swap(first, NEAR_X), swap(second, NEAR_Y)), gates)
    return [jnp.stack([first, arrived[0]]), jnp.stack([second, arrived[1]])]


def second_step(pairs, *gates):
    first, second = pairs
    arrived = after((swap(first, NEAR_Y), swap(second, NEAR_X)), gates)
    return [first, arrived[0], second, arrived[1]]


def core_step(held):
    return [*held, swap(jnp.stack(held), CORE)]


def after(value, *others):
    return lax.optimization_barrier((value, others))[0]


def add(first, second):
    return (first.astype(f32) + second.astype(f32)).astype(bf16)


def first_sum_step(sums):
    half = sums.shape[2] // 2
    first, second = sums[:, :, :half], sums[:, :, half:]
    return [(first[0], swap(first[1], NEAR_Y)), (second[:, 0], swap(second[:, 1], NEAR_X))]


def second_sum_step(halves):
    first, second = (add(*half) for half in halves)
    return [(first[0], swap(first[1], NEAR_X)), (second[0], swap(second[1], NEAR_Y))]


def over_groups(total):
    level = PLANE
    while level < lax.axis_size("dp"):
        total = total + swap(total, level)
        level *= 2
    return total


def sum_along(parts):
    total = parts[0].astype(f32)
    for step in range(1, len(parts)):
        total = total + partner(parts[step], step).astype(f32)
    return over_groups(total)


def shards(
    tokens, grad_out, pass_len, labels, w_query, w_key, w_value, b_query, b_value, w_out, b_out,
    ln1_gain, ln1_shift, w_in, b_in, w_back, b_back, ln2_gain, ln2_shift,
):
    ways = lax.axis_size("mp")
    data_ways = lax.axis_size("dp")
    mp_index = lax.axis_index("mp")
    data_index = lax.axis_index("dp")
    own_rows, width = tokens.shape
    rows_here = pass_len.shape[0]
    inner = w_query.shape[1]
    units = w_in.shape[1]
    halo = ROW_LEN // 4
    count = own_rows + 2 * halo
    scale = 1.0 / math.sqrt(HEAD)
    temper = 2.0 / math.sqrt(width)

    piece_rows = units // PLANE
    heads = inner // HEAD
    part = inner // PLANE
    place = jnp.stack([(data_index & CORE) << 2 | (data_index % PLANE) >> 1, mp_index])
    (qkv_own,) = local(
        own_heads_kernel, place, (w_query.T, w_key.T, w_value.T), [((PLANE, 3 * part, width), bf16)],
        [((3 * heads * PLANE, 8, width), f32)], 4, "own_heads",
    )
    biases = jnp.concatenate([b_in, b_query, b_value])
    digits, rest = [], biases
    for _ in range(3):
        digits.append(lax.reduce_precision(rest, 8, 7))
        rest = rest - digits[-1]
    digits = jnp.stack(digits)
    lines = jnp.concatenate(
        [digits[:, :units], jnp.pad(digits[:, units:], ((0, 0), (0, width - 2 * inner)))]
    )
    lines = jnp.pad(lines, ((0, 2), (0, 0))).astype(bf16)
    qkv_along = along(jnp.concatenate([qkv_own[0], lines]))
    tokens_before, tokens_after = halo_rows(tokens, halo)
    w_out, w_in, w_back, place = lax.optimization_barrier((w_out, w_in, w_back, place, qkv_own))[:4]
    out_own, in_own, back_own = local(
        own_units_kernel, place, (w_out, w_in, w_back),
        [((PLANE, part, width), bf16), ((PLANE, piece_rows, width), bf16), ((PLANE, piece_rows, width), bf16)],
        [((heads * PLANE, 8, width), f32), ((PLANE, piece_rows, width), f32)], 5, "own_units",
    )
    in_piece = jnp.concatenate([in_own[0], out_own[0], jnp.zeros((8, width), bf16), back_own[0]])
    in_piece = after(in_piece, qkv_along)
    qkv_along = jnp.stack(qkv_along)
    qkv_pairs = first_step(qkv_along)
    in_held = {0: in_piece}
    level = ways // 2
    while level > 1:
        in_held = bit_step(in_held, level)
        level //= 2
    in_held = after(in_held, qkv_pairs)
    qkv_held = second_step(after(qkv_pairs, tokens_before, tokens_after, in_held))
    in_along = others_of(bit_step(in_held, 1))
    bias_heads, bias_in = local(
        biases_kernel, place, (after(qkv_along, qkv_pairs), b_in[None], b_query[None], b_value[None]),
        [((2, width), f32), ((1, ways * units), f32)], [((ways * PLANE, 8, 128), f32)], 2, "biases",
    )
    start = after(mp_index * own_rows - halo, qkv_pairs)
    bounds = segment_bounds(pass_len, start, halo, own_rows)
    qkv_parts = core_step(after(qkv_held, in_along, bias_heads, bounds))
    in_start = after(in_along, qkv_parts)
    in_rows = piece_rows + part + 8

    tokens_before = after(tokens_before, in_along)
    qkv = (tokens_before, tokens, tokens_after, qkv_own, *qkv_parts, bias_heads)
    queries, keys, values, qkv_all = local(
        project_kernel, place, qkv, [((count, width), bf16)] * 3 + [((3 * width, width), bf16)],
        [((count, width), bf16), ((PLANE, 3 * part, width), f32)], 10, "project", 32,
    )
    in_pairs = first_step(in_start[:, :in_rows], queries)
    context = [attend_forward(bounds, after(queries, in_pairs), keys, values, halo, 0, 2)]
    in_held = second_step(in_pairs, context[0])
    back_start = after(in_start[:, in_rows:], in_held)
    in_parts = core_step(in_held)
    late_queries = after(queries, in_held, back_start, context[0])
    context.append(attend_forward(bounds, late_queries, keys, values, halo, 1, 2))
    context = jnp.concatenate(context)
    in_own = after(in_own, context)
    in_all, out_all = local(
        join_in_out_kernel, place, (in_own, out_own, *in_parts),
        [((ways * units, width), bf16), ((width, width), bf16)],
        [((PLANE, part, width), f32)], 5, "join_in_out",
    )
    attended = mm(context, out_all)
    first_sum = tokens.astype(f32) + attended + b_out
    center_one, inverse_one = norm_parts(first_sum)
    unit_one = center_one * inverse_one
    hidden = unit_one * ln1_gain + ln1_shift
    hidden_low = hidden.astype(bf16)
    back_held = second_step(first_step(back_start, context), hidden_low)
    back_parts = core_step(back_held)
    (back_all,) = local(
        join_units_kernel, place, (back_own, *back_parts),
        [((ways * units, width), bf16)], [], 4, "join_back",
    )
    hidden_low = after(hidden_low, back_held)

    active, slope = gelu_both(mm(hidden_low, in_all, NT) + bias_in)
    active, slope = lax.optimization_barrier((active.astype(bf16), slope.astype(bf16)))
    second_sum = hidden + mm(active, back_all) + b_back
    center_two, inverse_two = norm_parts(second_sum)
    unit_two = center_two * inverse_two
    mixed = (unit_two * ln2_gain + ln2_shift).astype(bf16)

    query_count = PAIRS * rows_here
    places = cls_places(pass_len) + (jnp.arange(rows_here, dtype=jnp.int32) * ROW_LEN)[:, None]
    table_places = jnp.concatenate([places[:, :PAIRS].reshape(-1), places[:, PAIRS:].reshape(-1)])
    table_places = table_places - mp_index * own_rows
    picker = table_places[:, None] == jnp.arange(own_rows, dtype=jnp.int32)[None, :]
    table = mm(picker.astype(bf16), mixed).astype(bf16)
    digits = jnp.concatenate([labels // 32, labels % 32]).astype(bf16)
    digits = jnp.where(mp_index == 0, digits, 0)
    extra = jnp.zeros((8, width), bf16).at[0, : 2 * query_count].set(digits)
    tables = group_tables(jnp.concatenate([table, extra]))
    all_count = data_ways * query_count
    query_cls = tables[:, :query_count].reshape(all_count, width)
    passage_cls = tables[:, query_count : 2 * query_count].reshape(all_count, width)
    digits = tables[:, 2 * query_count, : 2 * query_count].astype(jnp.int32)
    all_labels = (digits[:, :query_count] * 32 + digits[:, query_count:]).reshape(-1)

    logits = mm(query_cls, passage_cls, NT) * temper
    targets = all_labels[:, None] == jnp.arange(all_count, dtype=jnp.int32)[None, :]
    top = jnp.max(logits, axis=1, keepdims=True)
    raised = jnp.exp(logits - top)
    total = jnp.sum(raised, axis=1, keepdims=True)
    losses = top[:, 0] + jnp.log(total[:, 0]) - jnp.sum(jnp.where(targets, logits, 0.0), axis=1)
    query_losses = lax.dynamic_slice_in_dim(losses, data_index * query_count, query_count)
    grad_logits = (raised / total - targets.astype(f32)) * temper
    rows_of = lax.dynamic_slice_in_dim(grad_logits, data_index * query_count, query_count, 0)
    columns_of = lax.dynamic_slice_in_dim(grad_logits, data_index * query_count, query_count, 1)
    grad_cls = jnp.concatenate(
        [
            jnp.dot(rows_of, passage_cls.astype(f32), precision=highest),
            jnp.dot(columns_of.T, query_cls.astype(f32), precision=highest),
        ]
    )
    grad_mixed = grad_out.astype(f32) + jnp.dot(
        picker.astype(f32).T, grad_cls, precision=highest
    )

    grad_second = norm_pull(grad_mixed, unit_two, inverse_two, ln2_gain)
    stats = [
        jnp.sum(grad_mixed * unit_two, axis=0, keepdims=True),
        jnp.sum(grad_mixed, axis=0, keepdims=True),
        jnp.sum(grad_second, axis=0, keepdims=True),
    ]
    second_low = grad_second.astype(bf16)

    def to_core(left, right):
        return mm(left[:, left.shape[1] // 2 :], right, TN).astype(bf16)

    def chip_sum(left, right, arrived):
        own = mm(left[:, : left.shape[1] // 2], right, TN)
        return add(own, arrived).reshape(2, 2, ways, piece_rows, width)

    back_sent = to_core(active, second_low)
    back_arrived = swap(back_sent, CORE)
    pulled, back_sent = lax.optimization_barrier((second_low, back_sent))
    grad_before = (mm(pulled, back_all, NT) * slope.astype(f32)).astype(bf16)
    back_sum = chip_sum(active, second_low, back_arrived)
    back_half = swap(back_sum[1], NEAR_Y)
    in_sent = to_core(grad_before, hidden_low)
    in_arrived = swap(in_sent, CORE)
    pulled = after(grad_before, back_sum, in_sent)
    grad_hidden = grad_second + mm(pulled, in_all)
    grad_first = norm_pull(grad_hidden, unit_one, inverse_one, ln1_gain)
    stats += [
        jnp.sum(grad_hidden * unit_one, axis=0, keepdims=True),
        jnp.sum(grad_hidden, axis=0, keepdims=True),
        jnp.sum(grad_first, axis=0, keepdims=True),
    ]
    first_low = grad_first.astype(bf16)
    first_before, first_after = halo_rows(first_low, halo)
    in_sum = chip_sum(after(grad_before, first_low), hidden_low, in_arrived)
    in_half = swap(in_sum[:, 1], NEAR_X)
    out_keep, out_sent = local(
        functools.partial(out_grads_kernel, ways), place, (context, first_low),
        [((4 * ways, part + 8, width), bf16)] * 2, [((8 * ways, part + 8, width), f32)], 3, "out_grads",
    )
    out_sum = add(out_keep, swap(out_sent, CORE)).reshape(2, 2, ways, part + 8, width)
    out_half = swap(out_sum[1], NEAR_Y)

    d_b_in = jnp.sum(grad_before, axis=0, dtype=f32, keepdims=True)
    (vectors,) = local(
        vectors_kernel, place, (*stats, d_b_in), [((ways, 8, width), f32)],
        [((ways * PLANE, 8, 128), f32)], 2, "vectors",
    )

    first_before, first_after = after((first_before, first_after), in_sum, out_sent, vectors)
    first_window = jnp.concatenate([first_before, first_low, first_after])
    grad_context = mm(first_window, out_all, NT).astype(bf16)
    grad_context = after(grad_context, in_sum, back_sum, out_sum, vectors)
    grad_query, *sums = attend_backward(bounds, queries, keys, values, grad_context, halo, ())
    back_half, in_half, out_half = after((back_half, in_half, out_half), grad_query)
    back_sum = add(back_sum[0], back_half)
    in_sum = add(in_sum[:, 0], in_half)
    out_sum = add(out_sum[0], out_half)
    back_half = swap(back_sum[1], NEAR_X)
    in_half = swap(in_sum[1], NEAR_Y)
    out_half = swap(out_sum[1], NEAR_X)
    grad_context = after(grad_context, back_sum, in_sum, out_sum, grad_query)
    late_query, grad_keys, grad_values = attend_backward(
        bounds, queries, keys, values, grad_context, halo, sums
    )
    early_halves = [(back_sum[0], back_half), (in_sum[0], in_half), (out_sum[0], out_half)]
    early_halves = after(early_halves, late_query)
    early_sum = jnp.concatenate([add(*half) for half in early_halves], axis=1)
    tokens_low, early_sum = lax.optimization_barrier((tokens, early_sum))
    early_parts = [early_sum[i] for i in range(ways)]

    late_rows = 3 * part + 8
    late_keep, late_sent = local(
        piece_grads_kernel, place, (grad_query, late_query, grad_keys, grad_values, tokens_low, vectors),
        [((4 * ways, late_rows, width), bf16)] * 2, [((8 * ways, late_rows, width), f32)], 8, "piece_grads", 36,
    )
    late_arrived = swap(late_sent, CORE)
    early_odd = partner(jnp.stack(early_parts[1::2]), 1)
    late_sum = add(late_keep, late_arrived).reshape(2, 2, ways, late_rows, width)
    halves = first_sum_step(late_sum)
    early_odd = after(early_odd, halves)
    early_parts = [add(even, odd) for even, odd in zip(early_parts[::2], early_odd)]
    halves = second_sum_step(halves)
    late_parts = [half[i] for half in (add(*h) for h in halves) for i in range(ways // 2)]
    level, early_own = 2, early_parts[0].astype(f32)
    while level < ways:
        early_own = early_own + after(partner(early_parts[level // 2], level), late_parts).astype(f32)
        level *= 2
    late_total = sum_along(late_parts)
    early_held = second_step(first_step(over_groups(early_own).astype(bf16)[None], late_total))
    grad_queries = jnp.concatenate([grad_query, late_query])
    d_tokens = (
        grad_first
        + mm(grad_queries, qkv_all[:width])
        + mm(grad_keys, qkv_all[width : 2 * width])
        + mm(grad_values, qkv_all[2 * width :])
    )
    late_held = first_step(late_total.astype(bf16)[None])
    early_pieces = core_step(after(early_held, late_held))
    late_pieces = core_step(second_step(late_held, d_tokens))
    line = late_total[3 * part :]

    d_query, d_key, d_value = local(
        finish_heads_kernel, place, late_pieces, [((inner, width), f32)] * 3,
        [((PLANE, 3 * part, width), f32)], 4, "finish_heads",
    )
    d_back, d_in, d_out = local(
        finish_units_kernel, place, early_pieces,
        [((units, width), f32), ((width, units), f32), ((inner, width), f32)],
        [((PLANE, 2 * piece_rows + part + 8, width), f32), ((units, width), f32)], 6, "finish_units",
    )
    norms = [line[1 + i // ways, i % ways * inner : (i % ways + 1) * inner] for i in range(8)]
    return (
        mixed,
        query_losses,
        d_tokens,
        d_query.T,
        d_key.T,
        d_value.T,
        norms[6],
        norms[7],
        d_out,
        norms[5],
        norms[3],
        norms[4],
        d_in,
        line[0],
        d_back,
        norms[2],
        norms[0],
        norms[1],
    )


def solution(mesh):
    return jax.shard_map(
        shards,
        mesh=mesh,
        in_specs=(
            P(("dp", "mp"), None), P(("dp", "mp"), None), P("dp", None), P("dp"),
            P(None, "mp"), P(None, "mp"), P(None, "mp"), P("mp"), P("mp"), P("mp", None), P(),
            P(), P(), P(None, "mp"), P("mp"), P("mp", None), P(), P(), P(),
        ),
        out_specs=(
            P(("dp", "mp"), None), P("dp"), P(("dp", "mp"), None),
            P(None, "mp"), P(None, "mp"), P(None, "mp"), P("mp"), P("mp"), P("mp", None),
            P("mp"), P("mp"), P("mp"), P(None, "mp"), P("mp"), P("mp", None), P("mp"), P("mp"), P("mp"),
        ),
        check_vma=False,
    )
```
